32 devices in a mesh: wide: 8 (over z, x), narrow: 4 (over y, core).
Axes of the slice: x: 2, y: 2, z: 4, core: 2. Of those that a mesh axis runs over, the one named last changes fastest.
Arguments:
- inputs: bfloat16 [16384, 1024], P('wide', 'narrow'), may hold values from -6 to 6
- cotangent: bfloat16 [16384, 1024], P('wide', 'narrow'), may hold values from -6 to 6
- lengths: int32 [8], P('wide'), may hold values from 213 to 1024, as said below
- ln_gain: float32 [1024], replicated, may hold values from 0.5 to 1.5
- ln_bias: float32 [1024], replicated, may hold values from -3 to 3
- w_qkv: bfloat16 [1024, 3072], replicated, may hold values from -0.1875 to 0.1875
- w_out: bfloat16 [1024, 1024], replicated, may hold values from -3 to 3
- w_in: bfloat16 [1024, 4096], P(None, 'narrow'), may hold values from -0.1875 to 0.1875
- b_in: float32 [4096], P('narrow'), may hold values from -3 to 3
- w_down: bfloat16 [4096, 1024], P('narrow'), may hold values from -0.09375 to 0.09375
- b_down: float32 [1024], P('narrow'), may hold values from -3 to 3
Outputs:
- mixed: bfloat16 [16384, 1024], P('wide', 'narrow')
- g_inputs: float32 [16384, 1024], P('wide', 'narrow')
- g_ln_gain: float32 [1024], P('narrow')
- g_ln_bias: float32 [1024], P('narrow')
- g_w_qkv: float32 [1024, 3, 1024], P('wide', None, 'narrow')
- g_w_out: float32 [1024, 1024], P('narrow', 'wide')
- g_w_in: float32 [1024, 4096], P('wide', 'narrow')
- g_b_in: float32 [4096], P('narrow')
- g_w_down: float32 [4096, 1024], P('narrow', 'wide')
- g_b_down: float32 [1024], P('narrow')
The draws below stay inside these ranges and needn't reach their ends.
Inputs may be any that keep to these rules, and one draw needn't show every extreme that they name: `lengths`: both rows of a pair have this length; positions at or past it are padding. The longest length in all is exactly 1024.
All inputs are finite; a program needn't handle non-finite values.
Results may differ from the reference program's by a relative error of at most 0.0096.
Values may be sent and summed in bfloat16 or wider, within the bound.
No kernel may reach another device: no remote copies, remote signals or barrier semaphores. Data moves between devices by JAX's collectives and lax.ppermute only.
A program may use at most 384 MiB of HBM per device.

```python
import jax
import jax.numpy as jnp
from jax import lax

D = 1024
HEADS = 16
HEAD_DIM = 64
ROT = 32
FF = 4096
PAD = 1024
PAIRS = 1
NGROUPS = 8
PAIRS_ALL = 8
ROWS = 16384


def draw_lengths(key, part):
    key = jax.random.fold_in(key, 11)
    group_index = jnp.arange(PAIRS_ALL) // PAIRS
    base_length = PAD // 3 + (PAD - PAD // 3) * group_index // max(NGROUPS - 1, 1)
    jitter = jax.random.randint(key, (PAIRS_ALL,), 0, PAD // 8 + 1)
    values = jnp.clip(base_length - jitter, 1, PAD).astype(jnp.int32)
    return values.at[PAIRS_ALL - 1].set(PAD)


def raised(entries, own_key, source, target, blocks, factor):
    owner, partner = [(jnp.arange(entries.shape[dim]) // (entries.shape[dim] // blocks)).reshape([-1 if axis == dim else 1 for axis in range(entries.ndim)]) for dim in (source, target)]
    chosen = jax.random.permutation(own_key, blocks)[partner]
    strong = (owner == chosen) | (owner == (partner + blocks // 2) % blocks)
    return jnp.where(strong, factor * entries, entries)


def levels(stream_key, dims, cuts, low, largest):
    loudness = 1.0
    for dim, parts in cuts:
        draws = jax.random.uniform(jax.random.fold_in(jax.random.fold_in(stream_key, 6), dim), (parts,), jnp.float32, low / len(cuts), largest / len(cuts))
        loudness = loudness * jnp.repeat(jnp.exp(draws), dims[dim] // parts).reshape((-1,) + (1,) * (len(dims) - 1 - dim))
    return loudness


def gaussian(key, extent, deviation, bound, shards=(), kind=jnp.bfloat16):
    level = levels(key, extent, shards, -0.22, 0.18) if shards else 1.0
    values = jax.random.normal(key, extent, jnp.float32) * deviation * level
    return jnp.minimum(jnp.maximum(values, -bound), bound).astype(kind)


def bell_draw_with(rng, extent, width, most, cuts, heavy, dtype=jnp.bfloat16):
    drawn = width * jax.random.normal(rng, extent, jnp.float32)
    if cuts:
        drawn = drawn * levels(rng, extent, cuts, -0.22, 0.18)
    return jnp.clip(raised(drawn, jax.random.fold_in(rng, 3), *heavy), -most, most).astype(dtype)


def setup_inputs(seed: int = 0) -> dict:
    arg_keys = jax.random.split(jax.random.key(seed), 12)
    return {
        "inputs": gaussian(arg_keys[0], (ROWS, D), 1.0, 6.0, ((0, 8), (1, 4))),
        "cotangent": bell_draw_with(arg_keys[1], (ROWS, D), 1.0, 6.0, ((0, 8), (1, 4)), (0, 1, 8, 2.0)),
        "lengths": draw_lengths(jax.random.fold_in(arg_keys[11], 71), 0),
        "ln_gain": jnp.clip(1.0 + 0.1 * jax.random.normal(arg_keys[3], (D,), jnp.float32), 0.5, 1.5),
        "ln_bias": gaussian(arg_keys[4], (D,), 0.3, 3.0, (), jnp.float32),
        "w_qkv": gaussian(arg_keys[5], (D, 3 * D), D ** -0.5, 0.1875),
        "w_out": gaussian(arg_keys[6], (D, D), (D * 4 // PAD) ** -0.5, 3.0),
        "w_in": gaussian(arg_keys[7], (D, FF), D ** -0.5, 0.1875, ((1, 4),)),
        "b_in": gaussian(arg_keys[8], (FF,), 0.5, 3.0, ((0, 4),), jnp.float32),
        "w_down": gaussian(arg_keys[9], (FF, D), FF ** -0.5, 0.09375, ((0, 4),)),
        "b_down": gaussian(arg_keys[10], (D,), 0.5, 3.0, ((0, 4),), jnp.float32),
    }


@jax.custom_vjp
def low(v):
    return lax.optimization_barrier(v.astype(jnp.bfloat16)).astype(jnp.float32)

@jax.custom_vjp
def low_back(v):
    return v

def low_keep(v):
    return (low(v), None)

def low_pass(kept, grad):
    return (grad,)

def back_keep(v):
    return (v, None)

def back_low(kept, grad):
    return (low(grad),)
low.defvjp(low_keep, low_pass)
low_back.defvjp(back_keep, back_low)
norm_eps = 1e-05
top_precision = lax.Precision.HIGHEST

def gelu_tanh(value_in):
    return 0.5 * value_in * (1.0 + jnp.tanh(0.7978845608028654 * (value_in + 0.044715 * value_in * value_in * value_in)))

def rotary_tables(seq_len, rot_dims):
    position = jnp.arange(seq_len).astype(jnp.float32)[:, None]
    freq_index = jnp.arange(rot_dims // 2).astype(jnp.float32)[None, :]
    angles = position * 10000.0 ** (-2.0 * freq_index / rot_dims)
    return (jnp.cos(angles), jnp.sin(angles))

def rotate(field_in, cosine, sine_table, rot_dims):
    rotated = field_in[..., :rot_dims]
    others = field_in[..., rot_dims:]
    pair_view = rotated.reshape(rotated.shape[:-1] + (rot_dims // 2, 2))
    first_half = pair_view[..., 0]
    second_half = pair_view[..., 1]
    cos_table = cosine[:, None, :]
    sin_table = sine_table[:, None, :]
    new_first = first_half * cos_table - second_half * sin_table
    new_second = second_half * cos_table + first_half * sin_table
    joined = jnp.stack([new_first, new_second], axis=-1).reshape(rotated.shape)
    return jnp.concatenate([joined, others], axis=-1)

def attend_sequence(packed):
    queries, key_rows, values, length = packed
    scores = jnp.einsum('qhd,khd->hqk', queries, key_rows, precision=top_precision) * HEAD_DIM ** (-0.5)
    scores = low_back(scores)
    position = jnp.arange(PAD)
    allowed = (position[None, :] <= position[:, None]) & (position[None, :] < length)
    scores = jnp.where(allowed[None], scores, -1e+30)
    row_max = lax.optimization_barrier(jnp.max(scores, axis=-1, keepdims=True))
    exp_scores = jnp.exp(scores - row_max)
    probs = low(exp_scores / lax.optimization_barrier(jnp.sum(exp_scores, axis=-1, keepdims=True)))
    return jnp.einsum('hqk,khd->qhd', probs, values, precision=top_precision)

def group_forward(values_in, seq_lengths, ln_gain, ln_bias, w_qkv, w_out, w_in, b_in, w_down, b_down):
    row_mean = lax.optimization_barrier(jnp.mean(values_in, axis=-1, keepdims=True))
    centered = values_in - row_mean
    variance = lax.optimization_barrier(jnp.mean(centered * centered, axis=-1, keepdims=True))
    normed = centered * lax.rsqrt(variance + norm_eps) * ln_gain + ln_bias
    hidden = low(normed)
    qkv_proj = low_back(jnp.dot(hidden, w_qkv, precision=top_precision))
    qkv_proj = qkv_proj.reshape(-1, PAD, 3, HEADS, HEAD_DIM)
    cosine, sine_table = rotary_tables(PAD, ROT)
    queries = low(rotate(qkv_proj[:, :, 0], cosine, sine_table, ROT))
    key_rows = low(rotate(qkv_proj[:, :, 1], cosine, sine_table, ROT))
    values = low(qkv_proj[:, :, 2])
    attended = lax.map(jax.checkpoint(attend_sequence), (queries, key_rows, values, seq_lengths))
    attended = low_back(low(attended.reshape(-1, HEADS * HEAD_DIM)))
    attn_out = jnp.dot(attended, w_out, precision=top_precision)
    up_proj = low_back(jnp.dot(hidden, w_in, precision=top_precision) + b_in)
    activation = low(gelu_tanh(up_proj))
    mlp_out = jnp.dot(activation, w_down, precision=top_precision) + b_down
    return values_in + low_back(attn_out + mlp_out)

def reference(inputs, cotangent, lengths, ln_gain, ln_bias, w_qkv, w_out, w_in, b_in, w_down, b_down):
    seq_lengths = jnp.repeat(lengths, 2)
    position = jnp.arange(PAD)
    valid_rows = (position[None, :] < seq_lengths[:, None]).astype(jnp.float32).reshape(ROWS, 1)
    counts = 2.0 * lax.optimization_barrier(jnp.sum(lengths.reshape(NGROUPS, PAIRS), axis=1)).astype(jnp.float32)
    group_weight = NGROUPS * counts / jnp.sum(counts)
    row_weight = jnp.repeat(group_weight, 2 * PAIRS * PAD)[:, None]
    grad_out = row_weight * valid_rows * cotangent.astype(jnp.float32)
    params = (ln_gain.astype(jnp.float32), ln_bias.astype(jnp.float32), w_qkv.astype(jnp.float32), w_out.astype(jnp.float32), w_in.astype(jnp.float32), b_in.astype(jnp.float32), w_down.astype(jnp.float32), b_down.astype(jnp.float32))
    group_lengths = seq_lengths.reshape(NGROUPS, 2 * PAIRS)

    def whole_layer(values_in, gain_in, bias_in, qkv_in, out_in, proj_in, bias_up, down_in, bias_down):
        grouped = values_in.reshape(NGROUPS, 2 * PAIRS * PAD, D)

        def one_group(packed):
            return group_forward(packed[0], packed[1], gain_in, bias_in, qkv_in, out_in, proj_in, bias_up, down_in, bias_down)
        result = lax.map(jax.checkpoint(one_group), (grouped, group_lengths))
        return result.reshape(ROWS, D)
    outputs, pull_back = jax.vjp(whole_layer, inputs.astype(jnp.float32), *params)
    grads = pull_back(grad_out)
    return (outputs.astype(jnp.bfloat16), grads[0], grads[1], grads[2], grads[3].reshape(D, 3, D), grads[4], grads[5], grads[6], grads[7], grads[8])
```

```python
import functools

import jax
import jax.numpy as jnp
import numpy as np
from jax import lax
from jax.experimental import pallas as pl
from jax.experimental.pallas import tpu as pltpu
from jax.sharding import PartitionSpec as P

HEAD_DIM = 64
ROT = 32
GELU_A = 0.7978845608028654
GELU_B = 0.044715
VMEM_BYTES = 56 * 1024 * 1024
F32 = jnp.float32
BF = jnp.bfloat16
NN = (((1,), (0,)), ((), ()))
NT = (((1,), (1,)), ((), ()))
TN = (((0,), (0,)), ((), ()))


norm_eps = 1e-05


def gelu_tanh(value_in):
    return (
        0.5
        * value_in
        * (
            1.0
            + jnp.tanh(0.7978845608028654 * (value_in + 0.044715 * value_in * value_in * value_in))
        )
    )


def rotary_tables(seq_len, rot_dims):
    position = jnp.arange(seq_len).astype(jnp.float32)[:, None]
    freq_index = jnp.arange(rot_dims // 2).astype(jnp.float32)[None, :]
    angles = position * 10000.0 ** (-2.0 * freq_index / rot_dims)
    return (jnp.cos(angles), jnp.sin(angles))


def rotate(field_in, cosine, sine_table, rot_dims):
    rotated = field_in[..., :rot_dims]
    others = field_in[..., rot_dims:]
    pair_view = rotated.reshape(rotated.shape[:-1] + (rot_dims // 2, 2))
    first_half = pair_view[..., 0]
    second_half = pair_view[..., 1]
    cos_table = cosine[:, None, :]
    sin_table = sine_table[:, None, :]
    new_first = first_half * cos_table - second_half * sin_table
    new_second = second_half * cos_table + first_half * sin_table
    joined = jnp.stack([new_first, new_second], axis=-1).reshape(rotated.shape)
    return jnp.concatenate([joined, others], axis=-1)


def causal_mask(first_row, block_rows, last_row, length):
    query_pos = first_row + jnp.arange(block_rows)[:, None]
    key_pos = jnp.arange(last_row)[None, :]
    return (key_pos <= query_pos) & (key_pos < length)


def block_scores(queries, key_rows, first_row, last_row, length):
    score_scale = HEAD_DIM ** (-0.5)
    scores = (
        jnp.einsum(
            "qhd,khd->hqk",
            queries[first_row:last_row],
            key_rows[:last_row],
            preferred_element_type=jnp.float32,
        )
        * score_scale
    )
    allowed = causal_mask(first_row, last_row - first_row, last_row, length)
    return jnp.where(allowed[None], scores, -1e30)


def attend_forward(queries, key_rows, values, length, block_rows):
    seq_len = queries.shape[0]
    queries = queries.reshape(seq_len, -1, HEAD_DIM)
    key_rows = key_rows.reshape(seq_len, -1, HEAD_DIM)
    values = values.reshape(seq_len, -1, HEAD_DIM)
    outputs = []
    lse_parts = []
    for first_row in range(0, seq_len, block_rows):
        last_row = first_row + block_rows
        scores = block_scores(queries, key_rows, first_row, last_row, length)
        row_max = jnp.max(scores, axis=-1, keepdims=True)
        exp_scores = jnp.exp(scores - row_max)
        row_total = jnp.sum(exp_scores, axis=-1, keepdims=True)
        probs_low = (exp_scores / row_total).astype(jnp.bfloat16)
        outputs.append(
            jnp.einsum(
                "hqk,khd->qhd", probs_low, values[:last_row], preferred_element_type=jnp.float32
            )
        )
        lse_parts.append((row_max + jnp.log(row_total))[..., 0])
    return (
        jnp.concatenate(outputs, axis=0).reshape(seq_len, -1),
        jnp.concatenate(lse_parts, axis=1),
    )


def attend_backward(queries, key_rows, values, grad_att, lse_rows, length, block_rows):
    seq_len = queries.shape[0]
    score_scale = HEAD_DIM ** (-0.5)
    queries = queries.reshape(seq_len, -1, HEAD_DIM)
    key_rows = key_rows.reshape(seq_len, -1, HEAD_DIM)
    values = values.reshape(seq_len, -1, HEAD_DIM)
    grad_att = grad_att.reshape(seq_len, -1, HEAD_DIM)
    key_grads = jnp.zeros(key_rows.shape, jnp.float32)
    value_grads = jnp.zeros(values.shape, jnp.float32)
    query_grads = []
    for first_row in range(0, seq_len, block_rows):
        last_row = first_row + block_rows
        scores = block_scores(queries, key_rows, first_row, last_row, length)
        probs = jnp.exp(scores - lse_rows[:, first_row:last_row, None])
        probs_low = probs.astype(jnp.bfloat16)
        grad_block = grad_att[first_row:last_row]
        grad_probs = jnp.einsum(
            "qhd,khd->hqk", grad_block, values[:last_row], preferred_element_type=jnp.float32
        )
        row_inner = jnp.sum(probs * grad_probs, axis=-1, keepdims=True)
        grad_scores = (probs * (grad_probs - row_inner)).astype(jnp.bfloat16)
        query_grads.append(
            jnp.einsum(
                "hqk,khd->qhd", grad_scores, key_rows[:last_row], preferred_element_type=jnp.float32
            )
            * score_scale
        )
        key_grads = key_grads.at[:last_row].add(
            jnp.einsum(
                "hqk,qhd->khd",
                grad_scores,
                queries[first_row:last_row],
                preferred_element_type=jnp.float32,
            )
            * score_scale
        )
        value_grads = value_grads.at[:last_row].add(
            jnp.einsum("hqk,qhd->khd", probs_low, grad_block, preferred_element_type=jnp.float32)
        )
    return (jnp.concatenate(query_grads, axis=0), key_grads, value_grads)


def on_device(
    inputs, cotangent, lengths, ln_gain, ln_bias, w_qkv, w_out, w_in, b_in, w_down, b_down
):
    groups = lax.axis_size("wide")
    narrow_size = lax.axis_size("narrow")
    column = lax.axis_index("narrow")
    seq_count = 2 * lengths.shape[0]
    rows_all = inputs.shape[0]
    pad_len = rows_all // seq_count
    model_width = w_qkv.shape[0]
    share_cols = model_width // narrow_size
    block_rows = min(512, pad_len)
    col_start = column * share_cols
    token_count = 2.0 * jnp.sum(lengths.astype(jnp.float32))
    token_sum = lax.psum(token_count, "wide")
    group_scale = groups * token_count / token_sum
    full_x, full_cot = (
        lax.all_gather(inputs, "narrow", axis=1, tiled=True),
        lax.all_gather(cotangent, "narrow", axis=1, tiled=True),
    )
    seq_lengths = jnp.repeat(lengths, 2)
    valid_rows = (
        (jnp.arange(pad_len)[None, :] < seq_lengths[:, None])
        .astype(jnp.float32)
        .reshape(rows_all, 1)
    )
    x_full = full_x.astype(jnp.float32)
    row_mean = jnp.mean(x_full, axis=-1, keepdims=True)
    centered = x_full - row_mean
    inv_std = lax.rsqrt(jnp.mean(centered * centered, axis=-1, keepdims=True) + norm_eps)
    x_hat = centered * inv_std
    hidden = (x_hat * ln_gain + ln_bias).astype(jnp.bfloat16)
    qkv_proj = jnp.dot(hidden, w_qkv, preferred_element_type=jnp.float32)
    qkv_proj = qkv_proj.reshape(seq_count, pad_len, 3, -1, HEAD_DIM)
    cosine, sine_table = rotary_tables(pad_len, ROT)
    q_seq = (
        rotate(qkv_proj[:, :, 0], cosine, sine_table, ROT)
        .astype(jnp.bfloat16)
        .reshape(seq_count, pad_len, -1)
    )
    k_seq = (
        rotate(qkv_proj[:, :, 1], cosine, sine_table, ROT)
        .astype(jnp.bfloat16)
        .reshape(seq_count, pad_len, -1)
    )
    v_seq = qkv_proj[:, :, 2].astype(jnp.bfloat16).reshape(seq_count, pad_len, -1)
    att_width = q_seq.shape[2]
    up_proj = jnp.dot(hidden, w_in, preferred_element_type=jnp.float32) + b_in
    activation = gelu_tanh(up_proj).astype(jnp.bfloat16)
    mlp_part = jnp.dot(activation, w_down, preferred_element_type=jnp.float32)

    def forward_one(packed):
        return attend_forward(packed[0], packed[1], packed[2], packed[3], block_rows)

    att_rows, lse_all = lax.map(forward_one, (q_seq, k_seq, v_seq, seq_lengths))
    attended = att_rows.astype(jnp.bfloat16).reshape(rows_all, att_width)
    branch_share = lax.psum_scatter(
        mlp_part.astype(jnp.bfloat16), "narrow", scatter_dimension=1, tiled=True
    ).astype(jnp.float32)
    w_out_cols = lax.dynamic_slice_in_dim(w_out, col_start, share_cols, 1)
    attn_share = jnp.dot(attended, w_out_cols, preferred_element_type=jnp.float32)
    mixed = (inputs.astype(jnp.float32) + (attn_share + (branch_share + b_down))).astype(
        jnp.bfloat16
    )
    grad_share = group_scale * valid_rows * cotangent.astype(jnp.float32)
    grad_share_low = grad_share.astype(jnp.bfloat16)
    grad_low = (group_scale * valid_rows * full_cot.astype(jnp.float32)).astype(jnp.bfloat16)
    g_b_down = jnp.sum(grad_share_low.astype(jnp.float32), axis=0)
    g_w_down = jnp.einsum("rf,rd->fd", activation, grad_low, preferred_element_type=jnp.float32)
    g_act = jnp.dot(grad_low, w_down.T, preferred_element_type=jnp.float32)
    gelu_value, gelu_pull = jax.vjp(gelu_tanh, up_proj)
    g_up = gelu_pull(g_act)[0].astype(jnp.bfloat16)
    g_b_in = jnp.sum(g_up.astype(jnp.float32), axis=0)
    g_w_in = jnp.einsum("rd,rf->df", hidden, g_up, preferred_element_type=jnp.float32)
    g_hidden_mlp = jnp.dot(g_up, w_in.T, preferred_element_type=jnp.float32)
    g_w_out_rows = jnp.einsum("rd,re->de", attended, grad_low, preferred_element_type=jnp.float32)
    g_att = jnp.dot(grad_low, w_out.T, preferred_element_type=jnp.float32).astype(jnp.bfloat16)

    def backward_one(packed):
        return attend_backward(
            packed[0], packed[1], packed[2], packed[3], packed[4], packed[5], block_rows
        )

    g_qrot, g_krot, g_val = lax.map(
        backward_one,
        (q_seq, k_seq, v_seq, g_att.reshape(seq_count, pad_len, att_width), lse_all, seq_lengths),
    )
    g_query = rotate(g_qrot, cosine, -sine_table, ROT)
    g_key = rotate(g_krot, cosine, -sine_table, ROT)
    g_qkv = (
        jnp.stack([g_query, g_key, g_val], axis=2)
        .reshape(rows_all, 3 * att_width)
        .astype(jnp.bfloat16)
    )
    g_w_qkv = jnp.einsum("rd,rc->dc", hidden, g_qkv, preferred_element_type=jnp.float32)
    g_hidden_attn = jnp.dot(g_qkv, w_qkv.T, preferred_element_type=jnp.float32)
    g_hidden = g_hidden_attn + lax.psum(g_hidden_mlp.astype(jnp.bfloat16), "narrow").astype(
        jnp.float32
    )
    d_hat = g_hidden * ln_gain
    g_x_full = inv_std * (
        d_hat
        - jnp.mean(d_hat, axis=-1, keepdims=True)
        - x_hat * jnp.mean(d_hat * x_hat, axis=-1, keepdims=True)
    )
    g_x_share = lax.dynamic_slice_in_dim(g_x_full, col_start, share_cols, 1)
    g_gain = lax.dynamic_slice_in_dim(jnp.sum(g_hidden * x_hat, axis=0), col_start, share_cols, 0)
    g_bias = lax.dynamic_slice_in_dim(jnp.sum(g_hidden, axis=0), col_start, share_cols, 0)
    g_inputs = grad_share + g_x_share
    qkv_three = g_w_qkv.reshape(model_width, 3, att_width)
    summed = (
        lax.psum_scatter(qkv_three, "wide", scatter_dimension=0, tiled=True),
        lax.psum_scatter(g_w_out_rows, "wide", scatter_dimension=1, tiled=True),
        lax.psum_scatter(g_w_in, "wide", scatter_dimension=0, tiled=True),
        lax.psum_scatter(g_w_down, "wide", scatter_dimension=1, tiled=True),
    )
    g_qkv_part = lax.dynamic_slice_in_dim(summed[0], col_start, share_cols, 2)
    g_out_part = lax.dynamic_slice_in_dim(summed[1], col_start, share_cols, 0)
    small = lax.psum((g_gain, g_bias, g_b_in, g_b_down), "wide")
    return (
        mixed,
        g_inputs,
        small[0],
        small[1],
        g_qkv_part,
        g_out_part,
        summed[2],
        small[2],
        summed[3],
        small[3],
    )


LOG2E = 1.4426950408889634


def mm(left, right, dims=NN):
    return lax.dot_general(left, right, dims, preferred_element_type=F32)


def norm_mlp_kernel(
    place, scale, x0, x1, x2, x3, c0, c1, c2, c3, gain, bias, w_in, b_in, w_down,
    hidden, grad_low, act, g_up, branch, g_hid, stats, sum_up, sum_grad,
):
    step = pl.program_id(0)
    rows, cols = x0.shape
    width, units = w_in.shape
    own = place[0]
    xs = [ref[...].astype(F32) for ref in (x0, x1, x2, x3)]
    mean = jnp.sum(xs[0] + xs[1] + xs[2] + xs[3], axis=1, keepdims=True) * (1.0 / width)
    cs = [x - mean for x in xs]
    squares = cs[0] * cs[0] + cs[1] * cs[1] + cs[2] * cs[2] + cs[3] * cs[3]
    inv_std = lax.rsqrt(jnp.sum(squares, axis=1, keepdims=True) * (1.0 / width) + norm_eps)
    row = step * rows + lax.broadcasted_iota(jnp.int32, (rows, 1), 0)
    weight = jnp.where(row < place[1], scale[0], 0.0)
    for j, (centered, cot) in enumerate(zip(cs, (c0, c1, c2, c3))):
        here = pl.ds(pl.multiple_of((own ^ j) * cols, cols), cols)
        hidden[:, here] = (centered * inv_std * gain[:, here] + bias[:, here]).astype(BF)
        low = (weight * cot[...].astype(F32)).astype(BF)
        grad_low[:, here] = low
        if j == 0:
            sum_grad[...] = jnp.sum(low.astype(F32).reshape(rows // 8, 8, cols), axis=0)
    lane = lax.broadcasted_iota(jnp.int32, (rows, 128), 1)
    stats[...] = jnp.where(lane == 0, mean, inv_std)
    h = hidden[...]
    g = grad_low[...]
    part = min(512, units)
    for first in range(0, units, part):
        here = pl.ds(first, part)
        up = mm(h, w_in[:, here]) + b_in[:, here]
        g_act = mm(g, w_down[here, :], NT)
        square = up * up
        tanh = jnp.tanh(up * (GELU_A + GELU_A * GELU_B * square))
        half = 0.5 * up
        plus = 1.0 + tanh
        slope = 0.5 * plus + (half * (1.0 - tanh * tanh)) * (GELU_A + 3.0 * GELU_A * GELU_B * square)
        g_here = (slope * g_act).astype(BF)
        act[:, here] = (half * plus).astype(BF)
        g_up[:, here] = g_here
        sum_up[:, here] = jnp.sum(g_here.astype(F32).reshape(rows // 8, 8, part), axis=0)
    branch[...] = mm(act[...], w_down[...]).astype(BF)
    g_hid[...] = mm(g_up[...], w_in[...], NT).astype(BF)


def norm_mlp(place, scale, xs, cots, gain, bias, w_in, b_in, w_down):
    rows, cols = xs[0].shape
    width, units = w_in.shape
    tile = min(256, rows)
    tiles = rows // tile

    def rowed(size):
        return pl.BlockSpec((tile, size), lambda i: (i, 0))

    def whole(shape):
        return pl.BlockSpec(shape, lambda i: (0, 0), pipeline_mode=pl.Buffered(1))

    scalar = pl.BlockSpec(memory_space=pltpu.SMEM)
    shape = jax.ShapeDtypeStruct
    return pl.pallas_call(
        norm_mlp_kernel,
        grid=(tiles,),
        in_specs=[scalar, scalar]
        + [rowed(cols)] * 8
        + [whole((1, width)), whole((1, width)), whole((width, units)), whole((1, units)), whole((units, width))],
        out_specs=[rowed(width), rowed(width), rowed(units), rowed(units), rowed(width), rowed(width), rowed(128),
                   pl.BlockSpec((8, units), lambda i: (i, 0)), pl.BlockSpec((8, cols), lambda i: (i, 0))],
        out_shape=[shape((rows, width), BF), shape((rows, width), BF), shape((rows, units), BF), shape((rows, units), BF),
                   shape((rows, width), BF), shape((rows, width), BF), shape((rows, 128), F32),
                   shape((8 * tiles, units), F32), shape((8 * tiles, cols), F32)],
        compiler_params=pltpu.CompilerParams(vmem_limit_bytes=VMEM_BYTES),
        cost_estimate=pl.CostEstimate(flops=8 * rows * width * units, bytes_accessed=24 * rows * width, transcendentals=rows * units),
        name="norm_mlp",
    )(place, scale, *xs, *cots, gain, bias, w_in, b_in, w_down)


def turn(field, cosine, sine):
    lane = lax.broadcasted_iota(jnp.int32, field.shape, 1)
    size = field.shape[1]
    other = jnp.where(lane % 2 == 0, pltpu.roll(field, size - 1, 1), pltpu.roll(field, 1, 1))
    return field * cosine + other * sine


def attend_kernel(
    place, hidden, grad_low, w_q, w_k, w_v, w_o, cosine, sine, cos_all, sin_all, branch_in, g_hid_in, gain, bias,
    branch, g_hid, attended, g_qkv, sums,
    k_aug, k_t, v_nat, v_t, q_nat, q_aug, d_out, att_s, gq_s, gk_acc, gv_acc, *, tiles, tile, pairs,
):
    step = pl.program_id(0)
    own = place[0]
    length = place[1]
    rows = tiles * tile

    @pl.when(step < tiles)
    def project():
        h = hidden[...]
        cos = cosine[...]
        sin = sine[...]
        q_all = mm(h, w_q[...])
        k_all = mm(h, w_k[...])
        v_all = mm(h, w_v[...])
        g_all = mm(grad_low[...], w_o[...], NT)
        start = pl.multiple_of(step * tile, tile)
        here = pl.ds(start, tile)
        lane = lax.broadcasted_iota(jnp.int32, (tile, 128), 1)
        key_row = start + lax.broadcasted_iota(jnp.int32, (tile, 128), 0)
        closed = jnp.where(key_row < length, 0.0, -1e30)
        first = lane < HEAD_DIM
        sub = lax.broadcasted_iota(jnp.int32, (128, tile), 0)
        for p in range(pairs):
            cut = slice(128 * p, 128 * (p + 1))
            q = turn(q_all[:, cut], cos, sin) * HEAD_DIM ** (-0.5)
            k = turn(k_all[:, cut], cos, sin)
            v = v_all[:, cut]
            q_nat[p, here, :] = q.astype(BF)
            v_nat[p, here, :] = v.astype(BF)
            k_aug[2 * p, here, :] = jnp.where(first, k, jnp.where(lane == HEAD_DIM, closed, 0.0)).astype(BF)
            k_aug[2 * p + 1, here, :] = jnp.where(first, jnp.where(lane == 0, closed, 0.0), k).astype(BF)
            q_t = q.T
            q_aug[2 * p, :, here] = jnp.where(sub < HEAD_DIM, q_t, jnp.where(sub == HEAD_DIM, 1.0, 0.0)).astype(BF)
            q_aug[2 * p + 1, :, here] = jnp.where(sub < HEAD_DIM, jnp.where(sub == 0, 1.0, 0.0), q_t).astype(BF)
            k_t[p, :, here] = k.T.astype(BF)
            v_t[p, :, here] = v.T.astype(BF)
            d_out[p, :, here] = g_all[:, cut].T

    @pl.when((step >= tiles) & (step < tiles + pairs))
    def attend():
        p = step - tiles
        lane = lax.broadcasted_iota(jnp.int32, (tile, 128), 1)
        first = lane < HEAD_DIM
        sub = lax.broadcasted_iota(jnp.int32, (128, tile), 0)
        later = lax.broadcasted_iota(jnp.int32, (tile, tile), 0) > lax.broadcasted_iota(jnp.int32, (tile, tile), 1)
        out_cut = pl.ds(pl.multiple_of(p * 128, 128), 128)
        for i in range(tiles):
            n = (i + 1) * tile
            here = slice(i * tile, n)
            outs = []
            scaled = []
            weights = []
            row_inner = []
            d_here = d_out[p, :, here]
            for half in range(2):
                s = mm(k_aug[2 * p + half, :n, :], q_aug[2 * p + half, :, here])
                tail = jnp.where(later, -1e30, s[n - tile :])
                s = tail if i == 0 else jnp.concatenate([s[: n - tile], tail], axis=0)
                top = jnp.max(s, axis=0, keepdims=True)
                e = jnp.exp(s - top)
                share = 1.0 / jnp.sum(e, axis=0, keepdims=True)
                e_low = e.astype(BF)
                half_cut = slice(half * HEAD_DIM, (half + 1) * HEAD_DIM)
                out = mm(v_t[p, half_cut, :n], e_low) * share
                d = d_here[half_cut]
                row_inner.append(jnp.sum(d * out, axis=0, keepdims=True) * share)
                outs.append(out)
                scaled.append(d * share)
                weights.append((e, e_low))
            att_s[here, out_cut] = jnp.concatenate(outs, axis=0).T.astype(BF)
            d_scaled = jnp.concatenate(scaled, axis=0)
            d_nat = d_scaled.T
            q_here = q_nat[p, here, :]
            g_q = []
            for half in range(2):
                e, e_low = weights[half]
                mine_t = (sub < HEAD_DIM) if half == 0 else (sub >= HEAD_DIM)
                mine = first if half == 0 else ~first
                d_t = jnp.where(mine_t, d_scaled, 0.0).astype(BF)
                g_s = (e * (mm(v_nat[p, :n, :], d_t) - row_inner[half])).astype(BF)
                half_cut = slice(half * HEAD_DIM, (half + 1) * HEAD_DIM)
                g_q.append(mm(k_t[p, half_cut, :n], g_s))
                add_v = mm(e_low, jnp.where(mine, d_nat, 0.0).astype(BF))
                add_k = mm(g_s, jnp.where(mine, q_here, 0.0).astype(BF))
                if half == 0:
                    first_v, first_k = add_v, add_k
            add_v = first_v + add_v
            add_k = first_k + add_k
            if i < tiles - 1:
                if i > 0:
                    gv_acc[: n - tile] += add_v[: n - tile]
                    gk_acc[: n - tile] += add_k[: n - tile]
                gv_acc[here] = add_v[n - tile :]
                gk_acc[here] = add_k[n - tile :]
            else:
                if i > 0:
                    add_v = add_v + jnp.concatenate([gv_acc[: n - tile], jnp.zeros((tile, 128), F32)], axis=0)
                    add_k = add_k + jnp.concatenate([gk_acc[: n - tile], jnp.zeros((tile, 128), F32)], axis=0)
                gq_s[2, :, out_cut] = add_v.astype(BF)
                gq_s[1, :, out_cut] = turn(add_k, cos_all[...], -sin_all[...]).astype(BF)
            g_q = jnp.concatenate(g_q, axis=0).T * HEAD_DIM ** (-0.5)
            gq_s[0, here, out_cut] = turn(g_q, cos_all[here, :], -sin_all[here, :]).astype(BF)

    @pl.when(step >= tiles + pairs)
    def finish():
        start = pl.multiple_of((step - tiles - pairs) * tile, tile)
        here = pl.ds(start, tile)
        att = att_s[here, :]
        attended[...] = att
        total = mm(att, w_o[...]) + branch_in[...].astype(F32)
        size = att.shape[1]
        g_total = g_hid_in[...].astype(F32)
        for j, w in enumerate((w_q, w_k, w_v)):
            g = gq_s[j, here, :]
            g_qkv[:, j * size : (j + 1) * size] = g
            g_total += mm(g, w[...], NT)
        width = total.shape[1]
        share = width // 4
        for j in range(4):
            core_slot = (j & 1) ^ (own & 1)
            y_slot = (j >> 1) ^ (own >> 1)
            cut = slice(j * share, (j + 1) * share)
            branch[core_slot, y_slot] = total[:, cut].astype(BF)
            g_hid[core_slot, y_slot] = g_total[:, cut].astype(BF)
        mean_part = jnp.sum(g_total * gain[...], axis=1, keepdims=True)
        inner_part = jnp.sum(g_total * (hidden[...].astype(F32) - bias[...]), axis=1, keepdims=True)
        lane = lax.broadcasted_iota(jnp.int32, (tile, 128), 1)
        both = jnp.where(lane == 0, mean_part, inner_part)
        sums[...] = both.T[:8, :]


def attend(place, hidden, grad_low, w_qkv, w_out, cosine, sine, branch_in, g_hid_in, gain, bias):
    rows, width = hidden.shape
    share = width // 4
    pairs = share // 128
    tile = min(256, rows)
    tiles = rows // tile
    steps = 2 * tiles + pairs

    def early(i, _):
        return (jnp.minimum(i, tiles - 1), 0)

    def late_row(i):
        return jnp.maximum(i - tiles - pairs, 0)

    def late(i, _):
        return (late_row(i), 0)

    def both(i, _):
        return (jnp.where(i < tiles + pairs, jnp.minimum(i, tiles - 1), i - tiles - pairs), 0)

    def whole(shape):
        return pl.BlockSpec(shape, lambda i, _: (0, 0), pipeline_mode=pl.Buffered(1))

    def column(j):
        return pl.BlockSpec((width, share), lambda i, where: (0, 4 * j + where[0]), pipeline_mode=pl.Buffered(1))

    shape = jax.ShapeDtypeStruct
    slots = pl.BlockSpec((2, 2, tile, share), lambda i, _: (0, 0, late_row(i), 0))
    return pl.pallas_call(
        functools.partial(attend_kernel, tiles=tiles, tile=tile, pairs=pairs),
        grid_spec=pltpu.PrefetchScalarGridSpec(
            num_scalar_prefetch=1,
            grid=(steps,),
            in_specs=[
                pl.BlockSpec((tile, width), both),
                pl.BlockSpec((tile, width), early),
                column(0), column(1), column(2),
                pl.BlockSpec((share, width), lambda i, where: (where[0], 0), pipeline_mode=pl.Buffered(1)),
                pl.BlockSpec((tile, 128), early),
                pl.BlockSpec((tile, 128), early),
                whole((rows, 128)), whole((rows, 128)),
                pl.BlockSpec((tile, width), late),
                pl.BlockSpec((tile, width), late),
                whole((1, width)), whole((1, width)),
            ],
            out_specs=[
                slots, slots,
                pl.BlockSpec((tile, share), late),
                pl.BlockSpec((tile, 3 * share), late),
                pl.BlockSpec((8, tile), lambda i, _: (0, late_row(i))),
            ],
            scratch_shapes=[
                pltpu.VMEM((2 * pairs, rows, 128), BF),
                pltpu.VMEM((pairs, 128, rows), BF),
                pltpu.VMEM((pairs, rows, 128), BF),
                pltpu.VMEM((pairs, 128, rows), BF),
                pltpu.VMEM((pairs, rows, 128), BF),
                pltpu.VMEM((2 * pairs, 128, rows), BF),
                pltpu.VMEM((pairs, 128, rows), F32),
                pltpu.VMEM((rows, share), BF),
                pltpu.VMEM((3, rows, share), BF),
                pltpu.VMEM((rows, 128), F32),
                pltpu.VMEM((rows, 128), F32),
            ],
        ),
        out_shape=[
            shape((2, 2, rows, share), BF), shape((2, 2, rows, share), BF),
            shape((rows, share), BF), shape((rows, 3 * share), BF), shape((8, rows), F32),
        ],
        compiler_params=pltpu.CompilerParams(vmem_limit_bytes=VMEM_BYTES),
        cost_estimate=pl.CostEstimate(flops=40 * rows * width * share, bytes_accessed=16 * rows * width, transcendentals=rows * rows * pairs),
        name="attend",
    )(place, hidden, grad_low, w_qkv, w_qkv, w_qkv, w_out, cosine, sine, cosine, sine, branch_in, g_hid_in, gain, bias)


def weight_kernel(place, *refs):
    out = refs[-1]
    count = (len(refs) - 1) // 2
    total = mm(refs[0][...], refs[count][...], TN)
    for k in range(1, count):
        total += mm(refs[k][...], refs[count + k][...], TN)
    total = total.astype(BF)
    mine = place[2]
    out[mine, 0] = total[: total.shape[0] // 2]
    out[1 - mine, 0] = total[total.shape[0] // 2 :]


def weight_grad(place, lefts, rights):
    rows, width = lefts[0].shape
    units = rights[0].shape[1]
    shards = 8
    size = width // shards
    column = pl.BlockSpec((rows, 2 * size), lambda i, _: (0, i))
    whole = pl.BlockSpec((rows, units), lambda i, _: (0, 0), pipeline_mode=pl.Buffered(1))

    def slot(i, where):
        z = i ^ where[3]
        return (0, 2 * (z & 1) + (z >> 1), 0, 0)

    return pl.pallas_call(
        weight_kernel,
        grid_spec=pltpu.PrefetchScalarGridSpec(
            num_scalar_prefetch=1,
            grid=(shards // 2,),
            in_specs=[column] * len(lefts) + [whole] * len(rights),
            out_specs=pl.BlockSpec((2, 1, size, units), slot),
        ),
        out_shape=jax.ShapeDtypeStruct((2, shards // 2, size, units), BF),
        compiler_params=pltpu.CompilerParams(vmem_limit_bytes=VMEM_BYTES),
        cost_estimate=pl.CostEstimate(flops=2 * len(lefts) * rows * width * units, bytes_accessed=12 * rows * width, transcendentals=0),
        name="weight_grad",
    )(place, *lefts, *rights)


def final_kernel(place, scale, keep_b, core_b, y_b, keep_g, core_g, y_g, x_ref, cot, stats, sums, gain, bias_down,
                 mixed, g_x, col_gain, col_bias):
    step = pl.program_id(0)
    rows, cols = x_ref.shape
    width = 4 * cols
    x = x_ref[...].astype(F32)
    branch = keep_b[0, 0].astype(F32) + core_b[0].astype(F32) + y_b[...].astype(F32)
    mixed[...] = (x + (branch + bias_down[...])).astype(BF)
    g = keep_g[0, 0].astype(F32) + core_g[0].astype(F32) + y_g[...].astype(F32)
    mean = stats[:, 0:1]
    inv_std = stats[:, 1:2]
    x_hat = (x - mean) * inv_std
    totals = jnp.concatenate([sums[...], jnp.zeros((120, rows), F32)], axis=0).T
    row = step * rows + lax.broadcasted_iota(jnp.int32, (rows, 1), 0)
    weight = jnp.where(row < place[1], scale[0], 0.0)
    g_out = weight * cot[...].astype(F32)
    inner = g * gain[...] - totals[:, 0:1] * (1.0 / width) - x_hat * (totals[:, 1:2] * (1.0 / width))
    g_x[...] = g_out + inv_std * inner
    col_gain[...] = jnp.sum((g * x_hat).reshape(rows // 8, 8, cols), axis=0)
    col_bias[...] = jnp.sum(g.reshape(rows // 8, 8, cols), axis=0)


def finish_rows(place, scale, keep_b, core_b, y_b, keep_g, core_g, y_g, x, cot, stats, sums, gain, bias_down):
    rows, cols = x.shape
    tile = min(256, rows)
    tiles = rows // tile
    rowed = pl.BlockSpec((tile, cols), lambda i: (i, 0))
    kept = pl.BlockSpec((1, 1, tile, cols), lambda i: (0, 0, i, 0))
    cored = pl.BlockSpec((1, tile, cols), lambda i: (0, i, 0))
    flat = pl.BlockSpec((1, cols), lambda i: (0, 0))
    eight = pl.BlockSpec((8, cols), lambda i: (i, 0))
    scalar = pl.BlockSpec(memory_space=pltpu.SMEM)
    shape = jax.ShapeDtypeStruct
    return pl.pallas_call(
        final_kernel,
        grid=(tiles,),
        in_specs=[scalar, scalar, kept, cored, rowed, kept, cored, rowed, rowed, rowed,
                  pl.BlockSpec((tile, 128), lambda i: (i, 0)), pl.BlockSpec((8, tile), lambda i: (0, i)), flat, flat],
        out_specs=[rowed, rowed, eight, eight],
        out_shape=[shape((rows, cols), BF), shape((rows, cols), F32), shape((8 * tiles, cols), F32), shape((8 * tiles, cols), F32)],
        compiler_params=pltpu.CompilerParams(vmem_limit_bytes=VMEM_BYTES),
        cost_estimate=pl.CostEstimate(flops=20 * rows * cols, bytes_accessed=24 * rows * cols, transcendentals=0),
        name="finish_rows",
    )(place, scale, keep_b, core_b, y_b, keep_g, core_g, y_g, x, cot, stats, sums, gain, bias_down)


def swap(value, axis, bit):
    size = lax.axis_size(axis)
    return lax.ppermute(value, axis, [(i, i ^ bit) for i in range(size)])


def sum_small(value, axis):
    bit = 1
    while bit < lax.axis_size(axis):
        value = value + swap(value, axis, bit)
        bit *= 2
    return value


def scatter_wide(slots):
    low = slots[0] + swap(slots[1], "wide", 1)
    low = low[:2] + swap(low[2:], "wide", 2)
    return low[0].astype(F32) + swap(low[1], "wide", 4).astype(F32)


def on_device_fast(inputs, cotangent, lengths, ln_gain, ln_bias, w_qkv, w_out, w_in, b_in, w_down, b_down):
    groups = lax.axis_size("wide")
    column = lax.axis_index("narrow")
    place_wide = lax.axis_index("wide")
    rows_all, cols = inputs.shape
    pad_len = rows_all // 2
    width = w_qkv.shape[0]
    units = w_in.shape[1]
    count = 2.0 * jnp.sum(lengths.astype(F32))
    scale = (groups * count / sum_small(count.reshape(1, 1), "wide")).reshape(1)
    place = jnp.stack([column, lengths[0], place_wide & 1, place_wide >> 1]).astype(jnp.int32)
    gain = ln_gain.reshape(1, width)
    bias = ln_bias.reshape(1, width)
    cosine, sine = turn_tables(pad_len)
    fields = []
    for s in range(2):
        pieces = []
        for whole in (inputs, cotangent):
            own = whole[s * pad_len : (s + 1) * pad_len]
            across = swap(own, "narrow", 2)
            pieces.append((own, swap(own, "narrow", 1), across, swap(across, "narrow", 1)))
        fields.append(pieces)
    mlps = []
    for s in range(2):
        mlps.append(norm_mlp(place, scale, fields[s][0], fields[s][1], gain, bias, w_in, b_in.reshape(1, units), w_down))
    hidden = [m[0] for m in mlps]
    grad_low = [m[1] for m in mlps]
    g_in_slots = weight_grad(place, hidden, [m[3] for m in mlps])
    g_down_slots = weight_grad(place, grad_low, [m[2] for m in mlps])
    atts = []
    for s in range(2):
        atts.append(attend(place, hidden[s], grad_low[s], w_qkv, w_out, cosine, sine, mlps[s][4], mlps[s][5], gain, bias))
    g_qkv_slots = weight_grad(place, hidden, [a[3] for a in atts])
    g_out_slots = weight_grad(place, grad_low, [a[2] for a in atts])
    own_gain = lax.dynamic_slice_in_dim(ln_gain, column * cols, cols, 0).reshape(1, cols)
    ends = []
    for s in range(2):
        branch, g_hid, _, _, sums = atts[s]
        core_b = swap(branch[1], "narrow", 1)
        core_g = swap(g_hid[1], "narrow", 1)
        y_b = swap(branch[0, 1] + core_b[1], "narrow", 2)
        y_g = swap(g_hid[0, 1] + core_g[1], "narrow", 2)
        sums = sum_small(sums, "narrow")
        ends.append(finish_rows(place, scale, branch, core_b, y_b, g_hid, core_g, y_g, fields[s][0][0], fields[s][1][0],
                                mlps[s][6], sums, own_gain, b_down.reshape(1, cols)))
    g_in = scatter_wide(g_in_slots)
    g_down = scatter_wide(g_down_slots)
    g_qkv = scatter_wide(g_qkv_slots)
    g_out = scatter_wide(g_out_slots)
    small = jnp.concatenate([
        jnp.sum(ends[0][2] + ends[1][2], axis=0), jnp.sum(ends[0][3] + ends[1][3], axis=0),
        jnp.sum(mlps[0][7] + mlps[1][7], axis=0), jnp.sum(mlps[0][8] + mlps[1][8], axis=0),
    ])
    small = sum_small(small, "wide")
    return (
        jnp.concatenate([ends[0][0], ends[1][0]], axis=0),
        jnp.concatenate([ends[0][1], ends[1][1]], axis=0),
        small[:cols],
        small[cols : 2 * cols],
        g_qkv.reshape(g_qkv.shape[0], 3, cols),
        g_out.T,
        g_in,
        small[2 * cols : 2 * cols + units],
        g_down.T,
        small[2 * cols + units :],
    )


def turn_tables(length):
    position = np.arange(length, dtype=np.float32)[:, None]
    frequency = (10000.0 ** (-2.0 * np.arange(ROT // 2, dtype=np.float32) / ROT)).astype(np.float32)
    angles = (position * frequency[None, :]).astype(np.float32)
    cosine = np.ones((length, HEAD_DIM), np.float32)
    sine = np.zeros((length, HEAD_DIM), np.float32)
    cosine[:, :ROT] = np.repeat(np.cos(angles), 2, axis=1)
    sine[:, 0:ROT:2] = -np.sin(angles)
    sine[:, 1:ROT:2] = np.sin(angles)
    return jnp.asarray(np.tile(cosine, (1, 2))), jnp.asarray(np.tile(sine, (1, 2)))


def solution(mesh):
    placed = (
        P("wide", "narrow"),
        P("wide", "narrow"),
        P("wide"),
        P(),
        P(),
        P(),
        P(),
        P(None, "narrow"),
        P("narrow"),
        P("narrow", None),
        P("narrow"),
    )
    paired = mesh.shape["narrow"] == 4 and mesh.shape["wide"] == 8
    return jax.shard_map(
        on_device_fast if paired else on_device,
        mesh=mesh,
        in_specs=placed,
        out_specs=(
            P("wide", "narrow"),
            P("wide", "narrow"),
            P("narrow"),
            P("narrow"),
            P("wide", None, "narrow"),
            P("narrow", "wide"),
            P("wide", "narrow"),
            P("narrow"),
            P("narrow", "wide"),
            P("narrow"),
        ),
        check_vma=False,
    )
```

```python
import functools

import jax
import jax.numpy as jnp
import numpy as np
from jax import lax
from jax.experimental import pallas as pl
from jax.experimental.pallas import tpu as pltpu
from jax.sharding import PartitionSpec as P

HEAD_DIM = 64
ROT = 32
GELU_A = 0.7978845608028654
GELU_B = 0.044715
VMEM_BYTES = 24 * 1024 * 1024
F32 = jnp.float32
BF = jnp.bfloat16
NN = (((1,), (0,)), ((), ()))
NT = (((1,), (1,)), ((), ()))
TN = (((0,), (0,)), ((), ()))


norm_eps = 1e-05


def gelu_tanh(value_in):
    return (
        0.5
        * value_in
        * (
            1.0
            + jnp.tanh(0.7978845608028654 * (value_in + 0.044715 * value_in * value_in * value_in))
        )
    )


def rotary_tables(seq_len, rot_dims):
    position = jnp.arange(seq_len).astype(jnp.float32)[:, None]
    freq_index = jnp.arange(rot_dims // 2).astype(jnp.float32)[None, :]
    angles = position * 10000.0 ** (-2.0 * freq_index / rot_dims)
    return (jnp.cos(angles), jnp.sin(angles))


def rotate(field_in, cosine, sine_table, rot_dims):
    rotated = field_in[..., :rot_dims]
    others = field_in[..., rot_dims:]
    pair_view = rotated.reshape(rotated.shape[:-1] + (rot_dims // 2, 2))
    first_half = pair_view[..., 0]
    second_half = pair_view[..., 1]
    cos_table = cosine[:, None, :]
    sin_table = sine_table[:, None, :]
    new_first = first_half * cos_table - second_half * sin_table
    new_second = second_half * cos_table + first_half * sin_table
    joined = jnp.stack([new_first, new_second], axis=-1).reshape(rotated.shape)
    return jnp.concatenate([joined, others], axis=-1)


def causal_mask(first_row, block_rows, last_row, length):
    query_pos = first_row + jnp.arange(block_rows)[:, None]
    key_pos = jnp.arange(last_row)[None, :]
    return (key_pos <= query_pos) & (key_pos < length)


def block_scores(queries, key_rows, first_row, last_row, length):
    score_scale = HEAD_DIM ** (-0.5)
    scores = (
        jnp.einsum(
            "qhd,khd->hqk",
            queries[first_row:last_row],
            key_rows[:last_row],
            preferred_element_type=jnp.float32,
        )
        * score_scale
    )
    allowed = causal_mask(first_row, last_row - first_row, last_row, length)
    return jnp.where(allowed[None], scores, -1e30)


def attend_forward(queries, key_rows, values, length, block_rows):
    seq_len = queries.shape[0]
    queries = queries.reshape(seq_len, -1, HEAD_DIM)
    key_rows = key_rows.reshape(seq_len, -1, HEAD_DIM)
    values = values.reshape(seq_len, -1, HEAD_DIM)
    outputs = []
    lse_parts = []
    for first_row in range(0, seq_len, block_rows):
        last_row = first_row + block_rows
        scores = block_scores(queries, key_rows, first_row, last_row, length)
        row_max = jnp.max(scores, axis=-1, keepdims=True)
        exp_scores = jnp.exp(scores - row_max)
        row_total = jnp.sum(exp_scores, axis=-1, keepdims=True)
        probs_low = (exp_scores / row_total).astype(jnp.bfloat16)
        outputs.append(
            jnp.einsum(
                "hqk,khd->qhd", probs_low, values[:last_row], preferred_element_type=jnp.float32
            )
        )
        lse_parts.append((row_max + jnp.log(row_total))[..., 0])
    return (
        jnp.concatenate(outputs, axis=0).reshape(seq_len, -1),
        jnp.concatenate(lse_parts, axis=1),
    )


def attend_backward(queries, key_rows, values, grad_att, lse_rows, length, block_rows):
    seq_len = queries.shape[0]
    score_scale = HEAD_DIM ** (-0.5)
    queries = queries.reshape(seq_len, -1, HEAD_DIM)
    key_rows = key_rows.reshape(seq_len, -1, HEAD_DIM)
    values = values.reshape(seq_len, -1, HEAD_DIM)
    grad_att = grad_att.reshape(seq_len, -1, HEAD_DIM)
    key_grads = jnp.zeros(key_rows.shape, jnp.float32)
    value_grads = jnp.zeros(values.shape, jnp.float32)
    query_grads = []
    for first_row in range(0, seq_len, block_rows):
        last_row = first_row + block_rows
        scores = block_scores(queries, key_rows, first_row, last_row, length)
        probs = jnp.exp(scores - lse_rows[:, first_row:last_row, None])
        probs_low = probs.astype(jnp.bfloat16)
        grad_block = grad_att[first_row:last_row]
        grad_probs = jnp.einsum(
            "qhd,khd->hqk", grad_block, values[:last_row], preferred_element_type=jnp.float32
        )
        row_inner = jnp.sum(probs * grad_probs, axis=-1, keepdims=True)
        grad_scores = (probs * (grad_probs - row_inner)).astype(jnp.bfloat16)
        query_grads.append(
            jnp.einsum(
                "hqk,khd->qhd", grad_scores, key_rows[:last_row], preferred_element_type=jnp.float32
            )
            * score_scale
        )
        key_grads = key_grads.at[:last_row].add(
            jnp.einsum(
                "hqk,qhd->khd",
                grad_scores,
                queries[first_row:last_row],
                preferred_element_type=jnp.float32,
            )
            * score_scale
        )
        value_grads = value_grads.at[:last_row].add(
            jnp.einsum("hqk,qhd->khd", probs_low, grad_block, preferred_element_type=jnp.float32)
        )
    return (jnp.concatenate(query_grads, axis=0), key_grads, value_grads)


def on_device(
    inputs, cotangent, lengths, ln_gain, ln_bias, w_qkv, w_out, w_in, b_in, w_down, b_down
):
    groups = lax.axis_size("wide")
    narrow_size = lax.axis_size("narrow")
    column = lax.axis_index("narrow")
    seq_count = 2 * lengths.shape[0]
    rows_all = inputs.shape[0]
    pad_len = rows_all // seq_count
    model_width = w_qkv.shape[0]
    share_cols = model_width // narrow_size
    block_rows = min(512, pad_len)
    col_start = column * share_cols
    token_count = 2.0 * jnp.sum(lengths.astype(jnp.float32))
    token_sum = lax.psum(token_count, "wide")
    group_scale = groups * token_count / token_sum
    full_x, full_cot = (
        lax.all_gather(inputs, "narrow", axis=1, tiled=True),
        lax.all_gather(cotangent, "narrow", axis=1, tiled=True),
    )
    seq_lengths = jnp.repeat(lengths, 2)
    valid_rows = (
        (jnp.arange(pad_len)[None, :] < seq_lengths[:, None])
        .astype(jnp.float32)
        .reshape(rows_all, 1)
    )
    x_full = full_x.astype(jnp.float32)
    row_mean = jnp.mean(x_full, axis=-1, keepdims=True)
    centered = x_full - row_mean
    inv_std = lax.rsqrt(jnp.mean(centered * centered, axis=-1, keepdims=True) + norm_eps)
    x_hat = centered * inv_std
    hidden = (x_hat * ln_gain + ln_bias).astype(jnp.bfloat16)
    qkv_proj = jnp.dot(hidden, w_qkv, preferred_element_type=jnp.float32)
    qkv_proj = qkv_proj.reshape(seq_count, pad_len, 3, -1, HEAD_DIM)
    cosine, sine_table = rotary_tables(pad_len, ROT)
    q_seq = (
        rotate(qkv_proj[:, :, 0], cosine, sine_table, ROT)
        .astype(jnp.bfloat16)
        .reshape(seq_count, pad_len, -1)
    )
    k_seq = (
        rotate(qkv_proj[:, :, 1], cosine, sine_table, ROT)
        .astype(jnp.bfloat16)
        .reshape(seq_count, pad_len, -1)
    )
    v_seq = qkv_proj[:, :, 2].astype(jnp.bfloat16).reshape(seq_count, pad_len, -1)
    att_width = q_seq.shape[2]
    up_proj = jnp.dot(hidden, w_in, preferred_element_type=jnp.float32) + b_in
    activation = gelu_tanh(up_proj).astype(jnp.bfloat16)
    mlp_part = jnp.dot(activation, w_down, preferred_element_type=jnp.float32)

    def forward_one(packed):
        return attend_forward(packed[0], packed[1], packed[2], packed[3], block_rows)

    att_rows, lse_all = lax.map(forward_one, (q_seq, k_seq, v_seq, seq_lengths))
    attended = att_rows.astype(jnp.bfloat16).reshape(rows_all, att_width)
    branch_share = lax.psum_scatter(
        mlp_part.astype(jnp.bfloat16), "narrow", scatter_dimension=1, tiled=True
    ).astype(jnp.float32)
    w_out_cols = lax.dynamic_slice_in_dim(w_out, col_start, share_cols, 1)
    attn_share = jnp.dot(attended, w_out_cols, preferred_element_type=jnp.float32)
    mixed = (inputs.astype(jnp.float32) + (attn_share + (branch_share + b_down))).astype(
        jnp.bfloat16
    )
    grad_share = group_scale * valid_rows * cotangent.astype(jnp.float32)
    grad_share_low = grad_share.astype(jnp.bfloat16)
    grad_low = (group_scale * valid_rows * full_cot.astype(jnp.float32)).astype(jnp.bfloat16)
    g_b_down = jnp.sum(grad_share_low.astype(jnp.float32), axis=0)
    g_w_down = jnp.einsum("rf,rd->fd", activation, grad_low, preferred_element_type=jnp.float32)
    g_act = jnp.dot(grad_low, w_down.T, preferred_element_type=jnp.float32)
    gelu_value, gelu_pull = jax.vjp(gelu_tanh, up_proj)
    g_up = gelu_pull(g_act)[0].astype(jnp.bfloat16)
    g_b_in = jnp.sum(g_up.astype(jnp.float32), axis=0)
    g_w_in = jnp.einsum("rd,rf->df", hidden, g_up, preferred_element_type=jnp.float32)
    g_hidden_mlp = jnp.dot(g_up, w_in.T, preferred_element_type=jnp.float32)
    g_w_out_rows = jnp.einsum("rd,re->de", attended, grad_low, preferred_element_type=jnp.float32)
    g_att = jnp.dot(grad_low, w_out.T, preferred_element_type=jnp.float32).astype(jnp.bfloat16)

    def backward_one(packed):
        return attend_backward(
            packed[0], packed[1], packed[2], packed[3], packed[4], packed[5], block_rows
        )

    g_qrot, g_krot, g_val = lax.map(
        backward_one,
        (q_seq, k_seq, v_seq, g_att.reshape(seq_count, pad_len, att_width), lse_all, seq_lengths),
    )
    g_query = rotate(g_qrot, cosine, -sine_table, ROT)
    g_key = rotate(g_krot, cosine, -sine_table, ROT)
    g_qkv = (
        jnp.stack([g_query, g_key, g_val], axis=2)
        .reshape(rows_all, 3 * att_width)
        .astype(jnp.bfloat16)
    )
    g_w_qkv = jnp.einsum("rd,rc->dc", hidden, g_qkv, preferred_element_type=jnp.float32)
    g_hidden_attn = jnp.dot(g_qkv, w_qkv.T, preferred_element_type=jnp.float32)
    g_hidden = g_hidden_attn + lax.psum(g_hidden_mlp.astype(jnp.bfloat16), "narrow").astype(
        jnp.float32
    )
    d_hat = g_hidden * ln_gain
    g_x_full = inv_std * (
        d_hat
        - jnp.mean(d_hat, axis=-1, keepdims=True)
        - x_hat * jnp.mean(d_hat * x_hat, axis=-1, keepdims=True)
    )
    g_x_share = lax.dynamic_slice_in_dim(g_x_full, col_start, share_cols, 1)
    g_gain = lax.dynamic_slice_in_dim(jnp.sum(g_hidden * x_hat, axis=0), col_start, share_cols, 0)
    g_bias = lax.dynamic_slice_in_dim(jnp.sum(g_hidden, axis=0), col_start, share_cols, 0)
    g_inputs = grad_share + g_x_share
    qkv_three = g_w_qkv.reshape(model_width, 3, att_width)
    summed = (
        lax.psum_scatter(qkv_three, "wide", scatter_dimension=0, tiled=True),
        lax.psum_scatter(g_w_out_rows, "wide", scatter_dimension=1, tiled=True),
        lax.psum_scatter(g_w_in, "wide", scatter_dimension=0, tiled=True),
        lax.psum_scatter(g_w_down, "wide", scatter_dimension=1, tiled=True),
    )
    g_qkv_part = lax.dynamic_slice_in_dim(summed[0], col_start, share_cols, 2)
    g_out_part = lax.dynamic_slice_in_dim(summed[1], col_start, share_cols, 0)
    small = lax.psum((g_gain, g_bias, g_b_in, g_b_down), "wide")
    return (
        mixed,
        g_inputs,
        small[0],
        small[1],
        g_qkv_part,
        g_out_part,
        summed[2],
        small[2],
        summed[3],
        small[3],
    )


LOG2E = 1.4426950408889634


def inside(value):
    return pltpu.with_memory_space_constraint(value, pltpu.VMEM)


def outside(value):
    return pltpu.with_memory_space_constraint(value, pltpu.HBM)


def mm(left, right, dims=NN):
    return lax.dot_general(left, right, dims, preferred_element_type=F32)


COST_SCALE = 0.1


def cost(micros):
    return pl.CostEstimate(flops=int(COST_SCALE * micros * 1e9), bytes_accessed=1000000, transcendentals=0)


def load_kernel(place, w_qkv, w_out, w_in, w_down, cosine, sine, *refs):
    outs, sems = refs[:-1], refs[-1]
    share = outs[0].shape[1]
    own = place[0]
    sources = [w_qkv.at[:, pl.ds(pl.multiple_of((4 * j + own) * share, 128), share)] for j in range(3)]
    sources += [w_out.at[pl.ds(pl.multiple_of(own * share, 128), share), :], w_in, w_down, cosine, sine]
    copies = [pltpu.make_async_copy(src, dst, sems.at[k]) for k, (src, dst) in enumerate(zip(sources, outs))]
    for copy in copies:
        copy.start()
    for copy in copies:
        copy.wait()


def load_weights(place, w_qkv, w_out, w_in, w_down, cosine, sine):
    width = w_qkv.shape[0]
    share = width // 4
    shapes = [(width, share)] * 3 + [(share, width), w_in.shape, w_down.shape]
    any_place = pl.BlockSpec(memory_space=pl.ANY)
    return pl.pallas_call(
        load_kernel,
        in_specs=[pl.BlockSpec(memory_space=pltpu.SMEM)] + [any_place] * 6,
        out_specs=[any_place] * 8,
        out_shape=[pltpu.VMEM(shape, BF) for shape in shapes] + [pltpu.VMEM(cosine.shape, F32)] * 2,
        scratch_shapes=[pltpu.SemaphoreType.DMA((8,))],
        compiler_params=pltpu.CompilerParams(vmem_limit_bytes=VMEM_BYTES),
        cost_estimate=cost(3),
        name="load_weights",
    )(place, *[outside(value) for value in (w_qkv, w_out, w_in, w_down, cosine, sine)])


def norm_mlp_kernel(place, x0, x1, x2, x3, c0, c1, c2, c3, gain, bias, w_in, b_in, w_down, *refs, first_row):
    left, right, stats, sum_up, sum_grad = refs[-5:]
    step = pl.program_id(0)
    rows, cols = x0.shape
    width, units = w_in.shape
    own = place[0]
    xs = [ref[...].astype(F32) for ref in (x0, x1, x2, x3)]
    mean = jnp.sum(xs[0] + xs[1] + xs[2] + xs[3], axis=1, keepdims=True) * (1.0 / width)
    cs = [x - mean for x in xs]
    squares = cs[0] * cs[0] + cs[1] * cs[1] + cs[2] * cs[2] + cs[3] * cs[3]
    inv_std = lax.rsqrt(jnp.sum(squares, axis=1, keepdims=True) * (1.0 / width) + norm_eps)
    row = first_row + step * rows + lax.broadcasted_iota(jnp.int32, (rows, 1), 0)
    for j, (centered, cot) in enumerate(zip(cs, (c0, c1, c2, c3))):
        here = pl.ds(pl.multiple_of((own ^ j) * cols, cols), cols)
        left[0, :, here] = (centered * inv_std * gain[:, here] + bias[:, here]).astype(BF)
        low = jnp.where(row < place[1], cot[...], jnp.zeros_like(cot))
        left[1, :, here] = low
        if j == 0:
            sum_grad[...] = jnp.sum(low.astype(F32).reshape(rows // 8, 8, cols), axis=0)
    lane = lax.broadcasted_iota(jnp.int32, (rows, 128), 1)
    stats[...] = jnp.where(lane == 0, mean, inv_std)
    h = left[0]
    g = left[1]
    part = min(512, units)
    for first in range(0, units, part):
        here = pl.ds(first, part)
        up = mm(h, w_in[:, here]) + b_in[:, here]
        g_act = mm(g, w_down[here, :], NT)
        square = up * up
        tanh = jnp.tanh(up * (GELU_A + GELU_A * GELU_B * square))
        half = 0.5 * up
        plus = 1.0 + tanh
        slope = 0.5 * plus + (half * (1.0 - tanh * tanh)) * (GELU_A + 3.0 * GELU_A * GELU_B * square)
        g_up = slope * g_act
        right[0, :, here] = g_up.astype(BF)
        right[1, :, here] = (half * plus).astype(BF)
        sum_up[:, here] = jnp.sum(g_up.reshape(rows // 8, 8, part), axis=0)


def norm_mlp(place, near, far, gain, bias, w_in, b_in, w_down, start_row, first_row, total, before=None):
    rows, cols = far[0].shape
    rows //= 2
    width, units = w_in.shape
    tile = min(256, rows)
    tiles = rows // tile
    offset = first_row // tile
    begin = start_row // tile

    def part(j):
        return [pl.BlockSpec((tile, cols), lambda i: (i + begin, 0))] * 2 + [pl.BlockSpec((tile, cols), lambda i: (i + j * tiles, 0))] * 2

    def rowed(size):
        return pl.BlockSpec((tile, size), lambda i: (i + offset, 0))

    def paired(size):
        return pl.BlockSpec((2, tile, size), lambda i: (0, i + offset, 0))

    def eight(size):
        return pl.BlockSpec((8, size), lambda i: (i + offset, 0))

    def whole(shape):
        return pl.BlockSpec(memory_space=pltpu.VMEM)

    shape = jax.ShapeDtypeStruct
    outs = [pltpu.VMEM((2, total, width), BF), pltpu.VMEM((2, total, units), BF), shape((total, 128), F32),
            shape((total // tile * 8, units), F32), shape((total // tile * 8, cols), F32)]
    before = [] if before is None else [inside(before[0]), inside(before[1]), *before[2:]]
    return pl.pallas_call(
        functools.partial(norm_mlp_kernel, first_row=first_row),
        grid=(tiles,),
        in_specs=[pl.BlockSpec(memory_space=pltpu.SMEM)]
        + part(0) + part(1)
        + [whole((1, width)), whole((1, width)), whole((width, units)), whole((1, units)), whole((units, width))]
        + [pl.BlockSpec(memory_space=pl.ANY)] * len(before),
        out_specs=[paired(width), paired(units), rowed(128), eight(units), eight(cols)],
        out_shape=outs,
        input_output_aliases={14 + k: k for k in range(len(before))},
        compiler_params=pltpu.CompilerParams(vmem_limit_bytes=VMEM_BYTES),
        cost_estimate=cost(0.010 * rows),
        name="norm_mlp",
    )(place, near[0], near[1], *far, near[2], near[3], *far, gain, bias, inside(w_in), b_in, inside(w_down), *before)


def turn(field, cosine, sine):
    lane = lax.broadcasted_iota(jnp.int32, field.shape, 1)
    size = field.shape[1]
    other = jnp.where(lane % 2 == 0, pltpu.roll(field, size - 1, 1), pltpu.roll(field, 1, 1))
    return field * cosine + other * sine


def attend_kernel(
    place, left, w_q, w_k, w_v, w_o, cosine, sine, cos_all, sin_all, attended, g_qkv,
    k_aug, k_t, v_nat, v_t, q_nat, q_aug, d_out, gk_acc, gv_acc, *, tiles, tile, pairs,
):
    step = pl.program_id(0)
    length = place[1]
    share = 128 * pairs

    @pl.when(step < tiles)
    def project():
        h = left[0]
        cos = cosine[...]
        sin = sine[...]
        q_all = mm(h, w_q[...])
        k_all = mm(h, w_k[...])
        v_all = mm(h, w_v[...])
        g_all = mm(left[1], w_o[...], NT)
        start = pl.multiple_of(step * tile, tile)
        here = pl.ds(start, tile)
        lane = lax.broadcasted_iota(jnp.int32, (tile, 128), 1)
        key_row = start + lax.broadcasted_iota(jnp.int32, (tile, 128), 0)
        closed = jnp.where(key_row < length, 0.0, -1e30)
        first = lane < HEAD_DIM
        sub = lax.broadcasted_iota(jnp.int32, (128, tile), 0)
        for p in range(pairs):
            cut = slice(128 * p, 128 * (p + 1))
            q = turn(q_all[:, cut], cos, sin) * HEAD_DIM ** (-0.5)
            k = turn(k_all[:, cut], cos, sin)
            v = v_all[:, cut]
            q_nat[p, here, :] = q.astype(BF)
            v_nat[p, here, :] = v.astype(BF)
            k_aug[2 * p, here, :] = jnp.where(first, k, jnp.where(lane == HEAD_DIM, closed, 0.0)).astype(BF)
            k_aug[2 * p + 1, here, :] = jnp.where(first, jnp.where(lane == 0, closed, 0.0), k).astype(BF)
            q_t = q.T
            q_aug[2 * p, :, here] = jnp.where(sub < HEAD_DIM, q_t, jnp.where(sub == HEAD_DIM, 1.0, 0.0)).astype(BF)
            q_aug[2 * p + 1, :, here] = jnp.where(sub < HEAD_DIM, jnp.where(sub == 0, 1.0, 0.0), q_t).astype(BF)
            k_t[p, :, here] = k.T.astype(BF)
            v_t[p, :, here] = v.T.astype(BF)
            d_out[p, :, here] = g_all[:, cut].T

    @pl.when(step == tiles)
    def attend():
        lane = lax.broadcasted_iota(jnp.int32, (tile, 128), 1)
        sub = lax.broadcasted_iota(jnp.int32, (128, tile), 0)
        later = lax.broadcasted_iota(jnp.int32, (tile, tile), 0) > lax.broadcasted_iota(jnp.int32, (tile, tile), 1)
        heads = range(2 * pairs)
        mine = [lane < HEAD_DIM, lane >= HEAD_DIM]
        mine_t = [sub < HEAD_DIM, sub >= HEAD_DIM]
        cuts = [slice(0, HEAD_DIM), slice(HEAD_DIM, 2 * HEAD_DIM)]
        def score(i):
            n = (i + 1) * tile
            return [mm(k_aug[h, :n, :], q_aug[h, :, i * tile : n]) for h in heads]

        for i in range(tiles):
            n = (i + 1) * tile
            here = slice(i * tile, n)
            old = slice(0, i * tile)
            scores = ahead if i else score(0)
            weights, inverses = [], []
            for h in heads:
                s = scores[h]
                tail = jnp.where(later, -1e30, s[n - tile :])
                s = tail if i == 0 else jnp.concatenate([s[: n - tile], tail], axis=0)
                e = jnp.exp(s - jnp.max(s, axis=0, keepdims=True))
                inverses.append(1.0 / jnp.sum(e, axis=0, keepdims=True))
                weights.append(e)
            lows = [e.astype(BF) for e in weights]
            outs = [mm(v_t[h // 2, cuts[h % 2], :n], lows[h]) * inverses[h] for h in heads]
            scaled, inner = [], []
            for h in heads:
                d = d_out[h // 2, cuts[h % 2], here]
                inner.append(jnp.sum(d * outs[h], axis=0, keepdims=True) * inverses[h])
                scaled.append(d * inverses[h])
            g_scores = []
            for h in heads:
                p, half = divmod(h, 2)
                zero = jnp.zeros((HEAD_DIM, tile), BF)
                d_t = scaled[h].astype(BF)
                d_t = jnp.concatenate([d_t, zero] if half == 0 else [zero, d_t], axis=0)
                g_scores.append((weights[h] * (mm(v_nat[p, :n, :], d_t) - inner[h])).astype(BF))
            if i + 1 < tiles:
                ahead = score(i + 1)
            for p in range(pairs):
                cut = slice(p * 128, p * 128 + 128)
                pair = (2 * p, 2 * p + 1)
                attended[here, cut] = jnp.concatenate([outs[h] for h in pair], axis=0).T.astype(BF)
                d_nat = jnp.concatenate([scaled[h] for h in pair], axis=0).T
                q_here = q_nat[p, here, :]
                g_q = jnp.concatenate([mm(k_t[p, cuts[h % 2], :n], g_scores[h]) for h in pair], axis=0).T * HEAD_DIM ** (-0.5)
                g_qkv[here, cut] = turn(g_q, cos_all[here, :], -sin_all[here, :]).astype(BF)
                add_v = sum(mm(lows[h], jnp.where(mine[h % 2], d_nat, 0.0).astype(BF)) for h in pair)
                add_k = sum(mm(g_scores[h], jnp.where(mine[h % 2], q_here, jnp.zeros_like(q_here))) for h in pair)
                if i > 0:
                    gv_acc[p, old] += add_v[: n - tile]
                    gk_acc[p, old] += add_k[: n - tile]
                gv_acc[p, here] = add_v[n - tile :]
                gk_acc[p, here] = add_k[n - tile :]
        for p in range(pairs):
            for j, acc in ((1, gk_acc), (2, gv_acc)):
                cut = slice(j * share + p * 128, j * share + p * 128 + 128)
                total = acc[p]
                if j == 1:
                    total = turn(total, cos_all[...], -sin_all[...])
                g_qkv[:, cut] = total.astype(BF)


def attend(place, left, weights):
    _, rows, width = left.shape
    share = width // 4
    pairs = share // 128
    tile = min(256, rows)
    tiles = rows // tile

    def early(i, _):
        return (jnp.minimum(i, tiles - 1), 0)

    def whole(shape):
        return pl.BlockSpec(shape, lambda i, _: (0, 0), pipeline_mode=pl.Buffered(1))

    w_q, w_k, w_v, w_o, _, _, cosine, sine = [inside(value) for value in weights]
    return pl.pallas_call(
        functools.partial(attend_kernel, tiles=tiles, tile=tile, pairs=pairs),
        grid_spec=pltpu.PrefetchScalarGridSpec(
            num_scalar_prefetch=1,
            grid=(tiles + 1,),
            in_specs=[
                pl.BlockSpec((2, tile, width), lambda i, _: (0, jnp.minimum(i, tiles - 1), 0)),
                whole(w_q.shape), whole(w_k.shape), whole(w_v.shape), whole(w_o.shape),
                pl.BlockSpec((tile, 128), early),
                pl.BlockSpec((tile, 128), early),
                whole((rows, 128)), whole((rows, 128)),
            ],
            out_specs=[whole((rows, share)), whole((rows, 3 * share))],
            scratch_shapes=[
                pltpu.VMEM((2 * pairs, rows, 128), BF),
                pltpu.VMEM((pairs, 128, rows), BF),
                pltpu.VMEM((pairs, rows, 128), BF),
                pltpu.VMEM((pairs, 128, rows), BF),
                pltpu.VMEM((pairs, rows, 128), BF),
                pltpu.VMEM((2 * pairs, 128, rows), BF),
                pltpu.VMEM((pairs, 128, rows), F32),
                pltpu.VMEM((pairs, rows, 128), F32),
                pltpu.VMEM((pairs, rows, 128), F32),
            ],
        ),
        out_shape=[pltpu.VMEM((rows, share), BF), pltpu.VMEM((rows, 3 * share), BF)],
        compiler_params=pltpu.CompilerParams(vmem_limit_bytes=VMEM_BYTES),
        cost_estimate=cost(0.014 * rows),
        name="attend",
    )(place, inside(left), w_q, w_k, w_v, w_o, cosine, sine, cosine, sine)


def weight_mlp_kernel(place, scale, left_0, left_1, right_0, right_1, keep, send):
    total = (scale[0] * (mm(left_0[0], right_0[0], TN) + mm(left_1[0], right_1[0], TN))).astype(BF)
    half = total.shape[0] // 2
    odd = place[2] == 1
    keep[0] = jnp.where(odd, total[half:], total[:half])
    send[0] = jnp.where(odd, total[:half], total[half:])


def weight_att_kernel(place, scale, left_0, left_1, qkv_0, qkv_1, att_0, att_1, keep, send, both):
    odd = place[2] == 1
    size = att_0.shape[1]
    first = (scale[0] * (mm(left_0[0], qkv_0[...], TN) + mm(left_1[0], qkv_1[...], TN))).astype(BF)
    second = (scale[0] * (mm(left_0[1], att_0[...], TN) + mm(left_1[1], att_1[...], TN))).astype(BF)
    half = first.shape[0] // 2
    mine = jnp.where(odd, first[half:], first[:half])
    other = jnp.where(odd, first[:half], first[half:])
    keep[0] = mine[:, : 2 * size]
    send[0] = other[:, : 2 * size]
    both[0, 0, :, :size] = mine[:, 2 * size :]
    both[0, 1, :, :size] = other[:, 2 * size :]
    both[0, 0, :, size:] = jnp.where(odd, second[half:], second[:half])
    both[0, 1, :, size:] = jnp.where(odd, second[:half], second[half:])


def slot_of(z):
    return 2 * (z & 1) + (z >> 1)


def weight_mlp(place, scale, lefts, rights, kind):
    _, rows, width = lefts[0].shape
    units = rights[0].shape[2]
    size = width // 8
    column = pl.BlockSpec((1, rows, 2 * size), lambda i, where: (kind, 0, i))
    whole = pl.BlockSpec((1, rows, units), lambda i, where: (kind, 0, 0), pipeline_mode=pl.Buffered(1))
    slot = pl.BlockSpec((1, size, units), lambda i, where: (slot_of(i ^ where[3]), 0, 0))
    out = pltpu.HBM((4, size, units), BF)
    return pl.pallas_call(
        weight_mlp_kernel,
        grid_spec=pltpu.PrefetchScalarGridSpec(
            num_scalar_prefetch=1, grid=(4,),
            in_specs=[pl.BlockSpec(memory_space=pltpu.SMEM), column, column, whole, whole], out_specs=[slot, slot],
        ),
        out_shape=[out, out],
        compiler_params=pltpu.CompilerParams(vmem_limit_bytes=VMEM_BYTES),
        cost_estimate=cost(0.0065 * rows),
        name="weight_mlp",
    )(place, scale, *[inside(value) for value in (*lefts, *rights)])


def weight_att(place, scale, lefts, qkvs, atts):
    _, rows, width = lefts[0].shape
    units = 2 * atts[0].shape[1]
    size = width // 8
    column = pl.BlockSpec((2, rows, 2 * size), lambda i, where: (0, 0, i))

    def whole(ref):
        return pl.BlockSpec(ref.shape, lambda i, where: (0, 0), pipeline_mode=pl.Buffered(1))

    slot = pl.BlockSpec((1, size, units), lambda i, where: (slot_of(i ^ where[3]), 0, 0))
    pair = pl.BlockSpec((1, 2, size, units), lambda i, where: (slot_of(i ^ where[3]), 0, 0, 0))
    out = pltpu.HBM((4, size, units), BF)
    return pl.pallas_call(
        weight_att_kernel,
        grid_spec=pltpu.PrefetchScalarGridSpec(
            num_scalar_prefetch=1, grid=(4,),
            in_specs=[pl.BlockSpec(memory_space=pltpu.SMEM), column, column] + [whole(r) for r in (*qkvs, *atts)],
            out_specs=[slot, slot, pair],
        ),
        out_shape=[out, out, pltpu.HBM((4, 2, size, units), BF)],
        compiler_params=pltpu.CompilerParams(vmem_limit_bytes=VMEM_BYTES),
        cost_estimate=cost(0.007 * rows),
        name="weight_att",
    )(place, scale, *[inside(value) for value in (*lefts, *qkvs, *atts)])


def branch_kernel(place, left, right, att, g_qkv, w_q, w_k, w_v, w_o, w_in, w_down, gain, bias,
                  keep, send_near, send_far, sums, column_sums):
    own = place[0]
    rows, share = att.shape
    total = mm(right[1], w_down[...]) + mm(att[...], w_o[...])
    g_total = mm(right[0], w_in[...], NT)
    for j, w in enumerate((w_q, w_k, w_v)):
        g_total += mm(g_qkv[:, j * share : (j + 1) * share], w[...], NT)
    odd = (own & 1) == 1
    up = (own >> 1) == 1
    for kind, whole in enumerate((total, g_total)):
        cuts = [whole[:, j * share : (j + 1) * share].astype(BF) for j in range(4)]
        low = [jnp.where(odd, cuts[2 * y + 1], cuts[2 * y]) for y in range(2)]
        high = [jnp.where(odd, cuts[2 * y], cuts[2 * y + 1]) for y in range(2)]
        keep[0, kind] = jnp.where(up, low[1], low[0])
        keep[1, kind] = jnp.where(up, low[0], low[1])
        send_near[kind] = jnp.where(up, high[1], high[0])
        send_far[kind] = jnp.where(up, high[0], high[1])
    turned = g_total * (left[0].astype(F32) - bias[...])
    mean_part = jnp.sum(g_total * gain[...], axis=1, keepdims=True)
    inner_part = jnp.sum(turned, axis=1, keepdims=True)
    lane = lax.broadcasted_iota(jnp.int32, (rows, 128), 1)
    sums[...] = jnp.where(lane == 0, mean_part, inner_part).T[:8, :]

    @pl.when(pl.program_id(0) == 0)
    def clear():
        column_sums[...] = jnp.zeros_like(column_sums)

    column_sums[0:1, :] += jnp.sum(g_total, axis=0, keepdims=True)
    column_sums[1:2, :] += jnp.sum(turned, axis=0, keepdims=True)


def branch_parts(place, left, right, att, g_qkv, weights, gain, bias, first_row, rows):
    _, _, width = left.shape
    units = right.shape[2]
    share = att.shape[1]
    tile = min(256, rows)
    tiles = rows // tile
    offset = first_row // tile

    def paired(k, size):
        return pl.BlockSpec((k, tile, size), lambda i, _: (0, i + offset, 0))

    def rowed(size):
        return pl.BlockSpec((tile, size), lambda i, _: (i + offset, 0))

    def whole(shape):
        return pl.BlockSpec(shape, lambda i, _: (0, 0), pipeline_mode=pl.Buffered(1))

    weights = [inside(value) for value in weights[:6]]
    shape = jax.ShapeDtypeStruct
    slots = pl.BlockSpec((2, 2, tile, share), lambda i, _: (0, 0, i, 0))
    sent = pl.BlockSpec((2, tile, share), lambda i, _: (0, i, 0))
    return pl.pallas_call(
        branch_kernel,
        grid_spec=pltpu.PrefetchScalarGridSpec(
            num_scalar_prefetch=1,
            grid=(tiles,),
            in_specs=[
                paired(1, width), paired(2, units), rowed(share), rowed(3 * share),
                *[whole(value.shape) for value in weights],
                whole((1, width)), whole((1, width)),
            ],
            out_specs=[slots, sent, sent, pl.BlockSpec((8, tile), lambda i, _: (0, i)), pl.BlockSpec((8, width), lambda i, _: (0, 0))],
        ),
        out_shape=[pltpu.HBM((2, 2, rows, share), BF), pltpu.HBM((2, rows, share), BF), pltpu.HBM((2, rows, share), BF), shape((8, rows), F32),
                   shape((8, width), F32)],
        compiler_params=pltpu.CompilerParams(vmem_limit_bytes=VMEM_BYTES),
        cost_estimate=cost(0.010 * rows),
        name="branch_parts",
    )(place, inside(left), inside(right), inside(att), inside(g_qkv), *weights, gain, bias)


def final_kernel(place, scale, keep, near, far, x_ref, cot, stats, sums, gain, bias_down, *refs, first_row):
    mixed, g_x = refs[-2:]
    step = pl.program_id(0)
    rows, cols = x_ref.shape
    width = 4 * cols
    x = x_ref[...].astype(F32)
    branch = keep[0, 0].astype(F32) + near[0].astype(F32) + far[0].astype(F32)
    mixed[...] = (x + (branch + bias_down[...])).astype(BF)
    g = scale[0] * (keep[0, 1].astype(F32) + near[1].astype(F32) + far[1].astype(F32))
    inv_std = stats[:, 1:2]
    x_hat = (x - stats[:, 0:1]) * inv_std
    totals = (scale[0] / width) * jnp.concatenate([sums[...], jnp.zeros((120, rows), F32)], axis=0).T
    row = first_row + step * rows + lax.broadcasted_iota(jnp.int32, (rows, 1), 0)
    weight = jnp.where(row < place[1], scale[0], 0.0)
    g_out = weight * cot[...].astype(F32)
    g_x[...] = g_out + inv_std * (g * gain[...] - totals[:, 0:1] - x_hat * totals[:, 1:2])


def finish_rows(place, scale, keep, near, far, x, cot, stats, sums, gain, bias_down, sequence, first_row, before=None):
    _, rows, cols = far.shape
    tile = min(512, rows)
    tiles = rows // tile
    pad_len = stats.shape[0]
    begin = (sequence * pad_len + first_row) // tile
    inner = first_row // tile
    part = pl.BlockSpec((tile, cols), lambda i: (i + begin, 0))
    kept = pl.BlockSpec((1, 2, tile, cols), lambda i: (0, 0, i, 0))
    both = pl.BlockSpec((2, tile, cols), lambda i: (0, i, 0))
    flat = pl.BlockSpec((1, cols), lambda i: (0, 0))
    scalar = pl.BlockSpec(memory_space=pltpu.SMEM)
    shape = jax.ShapeDtypeStruct
    before = [] if before is None else list(before)
    return pl.pallas_call(
        functools.partial(final_kernel, first_row=first_row),
        grid=(tiles,),
        in_specs=[scalar, scalar, kept, both, both, part, part,
                  pl.BlockSpec((tile, 128), lambda i: (i + inner, 0)), pl.BlockSpec((8, tile), lambda i: (0, i + begin)), flat, flat]
        + [pl.BlockSpec(memory_space=pl.ANY)] * len(before),
        out_specs=[part, part],
        out_shape=[shape(x.shape, BF), shape(x.shape, F32)],
        input_output_aliases={11 + k: k for k in range(len(before))},
        compiler_params=pltpu.CompilerParams(vmem_limit_bytes=VMEM_BYTES),
        cost_estimate=cost(0.003 * rows),
        name="finish_rows",
    )(place, scale, keep, near, far, x, cot, stats, sums, gain, bias_down, *before)


def swap(value, axis, bit):
    size = lax.axis_size(axis)
    return lax.ppermute(value, axis, [(i, i ^ bit) for i in range(size)])


def sum_small(value, axis):
    bit = 1
    while bit < lax.axis_size(axis):
        value = value + swap(value, axis, bit)
        bit *= 2
    return value


def after(value, *others):
    return lax.optimization_barrier((value, *others))[0]


def on_device_fast(inputs, cotangent, lengths, ln_gain, ln_bias, w_qkv, w_out, w_in, b_in, w_down, b_down):
    groups = lax.axis_size("wide")
    column = lax.axis_index("narrow")
    place_wide = lax.axis_index("wide")
    rows_all, cols = inputs.shape
    pad_len = rows_all // 2
    width = w_qkv.shape[0]
    units = w_in.shape[1]
    place = jnp.stack([column, lengths[0], place_wide & 1, place_wide >> 1]).astype(jnp.int32)
    gain = ln_gain.reshape(1, width)
    bias = ln_bias.reshape(1, width)
    b_up = b_in.reshape(1, units)
    half = pad_len // 2
    cuts = ((0, half), (half, pad_len), (pad_len, rows_all))
    own_gain = lax.dynamic_slice_in_dim(ln_gain, column * cols, cols, 0).reshape(1, cols)
    b_row = b_down.reshape(1, cols)

    across = [swap(jnp.concatenate([inputs[low:high], cotangent[low:high]], axis=0), "narrow", 2) for low, high in cuts]
    near = (inputs, swap(inputs, "narrow", 1), cotangent, swap(cotangent, "narrow", 1))
    count = 2.0 * jnp.sum(lengths.astype(F32))
    scale = (groups * count / sum_small(count.reshape(1, 1), "wide")).reshape(1)

    def far(k, *earlier):
        rows = after(across[k], *earlier)
        return rows, swap(rows, "narrow", 1)

    def branch(place, mlp, att, first_row, rows):
        return branch_parts(place, mlp[0], mlp[1], *att, weights, gain, bias, first_row, rows)

    weights = load_weights(place, w_qkv, w_out, w_in, w_down, *turn_tables(pad_len))
    up_in, up_down = weights[4:6]
    first = norm_mlp(place, near, far(0, scale, weights[0]), gain, bias, up_in, b_up, up_down, 0, 0, pad_len)
    place = after(place, first[3])
    mlp_0 = norm_mlp(place, near, far(1, first[3]), gain, bias, up_in, b_up, up_down, half, half, pad_len, first)
    place = after(place, mlp_0[3])
    att_0 = attend(place, mlp_0[0], weights)
    place = after(place, att_0[0])
    mlp_1 = norm_mlp(place, near, far(2, att_0[0]), gain, bias, up_in, b_up, up_down, pad_len, 0, pad_len)
    place = after(place, mlp_1[3])
    lefts = (mlp_0[0], mlp_1[0])
    rights = (mlp_0[1], mlp_1[1])
    keep_in, send_in = weight_mlp(place, scale, lefts, rights, 0)
    place = after(place, keep_in)
    x_in = swap(send_in, "wide", 1)
    kept_0, near_0, far_0, sums_0, columns_0 = branch(place, mlp_0, att_0, 0, pad_len)
    place = after(place, sums_0)
    core_0 = swap(far_0, "narrow", 1)
    keep_down, send_down = weight_mlp(place, scale, lefts, rights, 1)
    x_down = swap(send_down, "wide", 1)
    chip_0 = kept_0[1] + after(core_0, keep_down)
    y_0 = swap(chip_0, "narrow", 2)
    place = after(place, keep_down, chip_0)
    near_0 = swap(after(near_0, chip_0), "narrow", 1)
    att_1 = attend(place, mlp_1[0], weights)
    x_in = after(x_in, att_1[0], near_0)
    low_in = keep_in[:2] + x_in[:2]
    z_in = swap(keep_in[2:] + x_in[2:], "wide", 2)
    place = after(place, low_in, att_1[0])
    kept_1, near_1, far_1, sums_1, columns_1 = branch(place, mlp_1, att_1, 0, half)
    core_1 = swap(far_1, "narrow", 1)
    place = after(place, sums_1)
    keep_a, send_a, both_a = weight_att(place, scale, lefts, (att_0[1], att_1[1]), (att_0[0], att_1[0]))
    chip_1 = kept_1[1] + after(core_1, keep_a)
    y_1 = swap(chip_1, "narrow", 2)
    x_a = swap(send_a, "wide", 1)
    z_b = swap(both_a[2:], "wide", 2)
    y_0, z_in, x_down = lax.optimization_barrier((y_0, z_in, x_down, chip_1))[:3]
    zz_in = swap(low_in[1] + z_in[1], "wide", 4)
    low_in = low_in[0] + z_in[0]
    low_down = keep_down[:2] + x_down[:2]
    z_down = swap(keep_down[2:] + x_down[2:], "wide", 2)
    place = after(place, chip_1, low_in, low_down)
    kept_2, near_2, far_2, sums_2, columns_2 = branch(place, mlp_1, att_1, half, half)
    core_2 = swap(far_2, "narrow", 1)
    x_a, z_b = lax.optimization_barrier((x_a, z_b, sums_2))[:2]
    low_a = keep_a[:2] + x_a[:2]
    z_a = swap(keep_a[2:] + x_a[2:], "wide", 2)
    low_b = both_a[0] + z_b[0]
    zz_b = swap(both_a[1] + z_b[1], "wide", 4)
    core_2 = after(core_2, low_a, low_b)
    chip_2 = kept_2[1] + core_2
    y_2 = swap(chip_2, "narrow", 2)
    near_1, near_2, z_down, y_1 = lax.optimization_barrier((near_1, near_2, z_down, y_1, chip_2))[:4]
    zz_down = swap(low_down[1] + z_down[1], "wide", 4)
    low_down = low_down[0] + z_down[0]
    near_1 = swap(near_1, "narrow", 1)
    near_2 = swap(near_2, "narrow", 1)
    sums = jnp.concatenate([sums_0, sums_1, sums_2, columns_0 + columns_1 + columns_2], axis=1)
    sums = sum_small(after(sums, low_down), "narrow")
    columns = lax.dynamic_slice_in_dim(sums[:2, rows_all:], column * cols, cols, 1)
    small = scale * jnp.concatenate([
        columns[1] / own_gain[0], columns[0],
        jnp.sum(mlp_0[3] + mlp_1[3], axis=0), jnp.sum(mlp_0[4] + mlp_1[4], axis=0),
    ])
    g_in = low_in.astype(F32) + zz_in.astype(F32)
    zz_a = swap(low_a[1] + z_a[1], "wide", 4)
    low_a = low_a[0] + z_a[0]
    x_b = swap(low_b[1] + zz_b[1], "wide", 1)
    low_b = low_b[0] + zz_b[0]
    g_down = (low_down.astype(F32) + zz_down.astype(F32)).T
    small = sum_small(small, "wide")
    ends = finish_rows(place, scale, kept_0, near_0, y_0, inputs, cotangent, mlp_0[2], sums, own_gain, b_row, 0, 0)
    ends = finish_rows(place, scale, kept_1, near_1, y_1, inputs, cotangent, mlp_1[2], sums, own_gain, b_row, 1, 0, ends)
    g_a = low_a.astype(F32) + zz_a.astype(F32)
    g_b = low_b.astype(F32) + x_b.astype(F32)
    ends = finish_rows(place, scale, kept_2, near_2, y_2, inputs, cotangent, mlp_1[2], sums, own_gain, b_row, 1, half, ends)
    return (
        ends[0],
        ends[1],
        small[:cols],
        small[cols : 2 * cols],
        jnp.concatenate([g_a, g_b[:, :cols]], axis=1).reshape(g_a.shape[0], 3, cols),
        g_b[:, cols:].T,
        g_in,
        small[2 * cols : 2 * cols + units],
        g_down,
        small[2 * cols + units :],
    )


def turn_tables(length):
    position = np.arange(length, dtype=np.float32)[:, None]
    frequency = (10000.0 ** (-2.0 * np.arange(ROT // 2, dtype=np.float32) / ROT)).astype(np.float32)
    angles = (position * frequency[None, :]).astype(np.float32)
    cosine = np.ones((length, HEAD_DIM), np.float32)
    sine = np.zeros((length, HEAD_DIM), np.float32)
    cosine[:, :ROT] = np.repeat(np.cos(angles), 2, axis=1)
    sine[:, 0:ROT:2] = -np.sin(angles)
    sine[:, 1:ROT:2] = np.sin(angles)
    return jnp.asarray(np.tile(cosine, (1, 2))), jnp.asarray(np.tile(sine, (1, 2)))


def solution(mesh):
    placed = (
        P("wide", "narrow"),
        P("wide", "narrow"),
        P("wide"),
        P(),
        P(),
        P(),
        P(),
        P(None, "narrow"),
        P("narrow"),
        P("narrow", None),
        P("narrow"),
    )
    paired = mesh.shape["narrow"] == 4 and mesh.shape["wide"] == 8
    return jax.shard_map(
        on_device_fast if paired else on_device,
        mesh=mesh,
        in_specs=placed,
        out_specs=(
            P("wide", "narrow"),
            P("wide", "narrow"),
            P("narrow"),
            P("narrow"),
            P("wide", None, "narrow"),
            P("narrow", "wide"),
            P("wide", "narrow"),
            P("narrow"),
            P("narrow", "wide"),
            P("narrow"),
        ),
        check_vma=False,
    )
```

```python
import functools

import jax
import jax.numpy as jnp
import numpy as np
from jax import lax
from jax.experimental import pallas as pl
from jax.experimental.pallas import tpu as pltpu
from jax.sharding import PartitionSpec as P

HEAD_DIM = 64
ROT = 32
GELU_A = 0.7978845608028654
GELU_B = 0.044715
VMEM_BYTES = 24 * 1024 * 1024
F32 = jnp.float32
BF = jnp.bfloat16
NN = (((1,), (0,)), ((), ()))
NT = (((1,), (1,)), ((), ()))
TN = (((0,), (0,)), ((), ()))


norm_eps = 1e-05


def gelu_tanh(value_in):
    return (
        0.5
        * value_in
        * (
            1.0
            + jnp.tanh(0.7978845608028654 * (value_in + 0.044715 * value_in * value_in * value_in))
        )
    )


def rotary_tables(seq_len, rot_dims):
    position = jnp.arange(seq_len).astype(jnp.float32)[:, None]
    freq_index = jnp.arange(rot_dims // 2).astype(jnp.float32)[None, :]
    angles = position * 10000.0 ** (-2.0 * freq_index / rot_dims)
    return (jnp.cos(angles), jnp.sin(angles))


def rotate(field_in, cosine, sine_table, rot_dims):
    rotated = field_in[..., :rot_dims]
    others = field_in[..., rot_dims:]
    pair_view = rotated.reshape(rotated.shape[:-1] + (rot_dims // 2, 2))
    first_half = pair_view[..., 0]
    second_half = pair_view[..., 1]
    cos_table = cosine[:, None, :]
    sin_table = sine_table[:, None, :]
    new_first = first_half * cos_table - second_half * sin_table
    new_second = second_half * cos_table + first_half * sin_table
    joined = jnp.stack([new_first, new_second], axis=-1).reshape(rotated.shape)
    return jnp.concatenate([joined, others], axis=-1)


def causal_mask(first_row, block_rows, last_row, length):
    query_pos = first_row + jnp.arange(block_rows)[:, None]
    key_pos = jnp.arange(last_row)[None, :]
    return (key_pos <= query_pos) & (key_pos < length)


def block_scores(queries, key_rows, first_row, last_row, length):
    score_scale = HEAD_DIM ** (-0.5)
    scores = (
        jnp.einsum(
            "qhd,khd->hqk",
            queries[first_row:last_row],
            key_rows[:last_row],
            preferred_element_type=jnp.float32,
        )
        * score_scale
    )
    allowed = causal_mask(first_row, last_row - first_row, last_row, length)
    return jnp.where(allowed[None], scores, -1e30)


def attend_forward(queries, key_rows, values, length, block_rows):
    seq_len = queries.shape[0]
    queries = queries.reshape(seq_len, -1, HEAD_DIM)
    key_rows = key_rows.reshape(seq_len, -1, HEAD_DIM)
    values = values.reshape(seq_len, -1, HEAD_DIM)
    outputs = []
    lse_parts = []
    for first_row in range(0, seq_len, block_rows):
        last_row = first_row + block_rows
        scores = block_scores(queries, key_rows, first_row, last_row, length)
        row_max = jnp.max(scores, axis=-1, keepdims=True)
        exp_scores = jnp.exp(scores - row_max)
        row_total = jnp.sum(exp_scores, axis=-1, keepdims=True)
        probs_low = (exp_scores / row_total).astype(jnp.bfloat16)
        outputs.append(
            jnp.einsum(
                "hqk,khd->qhd", probs_low, values[:last_row], preferred_element_type=jnp.float32
            )
        )
        lse_parts.append((row_max + jnp.log(row_total))[..., 0])
    return (
        jnp.concatenate(outputs, axis=0).reshape(seq_len, -1),
        jnp.concatenate(lse_parts, axis=1),
    )


def attend_backward(queries, key_rows, values, grad_att, lse_rows, length, block_rows):
    seq_len = queries.shape[0]
    score_scale = HEAD_DIM ** (-0.5)
    queries = queries.reshape(seq_len, -1, HEAD_DIM)
    key_rows = key_rows.reshape(seq_len, -1, HEAD_DIM)
    values = values.reshape(seq_len, -1, HEAD_DIM)
    grad_att = grad_att.reshape(seq_len, -1, HEAD_DIM)
    key_grads = jnp.zeros(key_rows.shape, jnp.float32)
    value_grads = jnp.zeros(values.shape, jnp.float32)
    query_grads = []
    for first_row in range(0, seq_len, block_rows):
        last_row = first_row + block_rows
        scores = block_scores(queries, key_rows, first_row, last_row, length)
        probs = jnp.exp(scores - lse_rows[:, first_row:last_row, None])
        probs_low = probs.astype(jnp.bfloat16)
        grad_block = grad_att[first_row:last_row]
        grad_probs = jnp.einsum(
            "qhd,khd->hqk", grad_block, values[:last_row], preferred_element_type=jnp.float32
        )
        row_inner = jnp.sum(probs * grad_probs, axis=-1, keepdims=True)
        grad_scores = (probs * (grad_probs - row_inner)).astype(jnp.bfloat16)
        query_grads.append(
            jnp.einsum(
                "hqk,khd->qhd", grad_scores, key_rows[:last_row], preferred_element_type=jnp.float32
            )
            * score_scale
        )
        key_grads = key_grads.at[:last_row].add(
            jnp.einsum(
                "hqk,qhd->khd",
                grad_scores,
                queries[first_row:last_row],
                preferred_element_type=jnp.float32,
            )
            * score_scale
        )
        value_grads = value_grads.at[:last_row].add(
            jnp.einsum("hqk,qhd->khd", probs_low, grad_block, preferred_element_type=jnp.float32)
        )
    return (jnp.concatenate(query_grads, axis=0), key_grads, value_grads)


def on_device(
    inputs, cotangent, lengths, ln_gain, ln_bias, w_qkv, w_out, w_in, b_in, w_down, b_down
):
    groups = lax.axis_size("wide")
    narrow_size = lax.axis_size("narrow")
    column = lax.axis_index("narrow")
    seq_count = 2 * lengths.shape[0]
    rows_all = inputs.shape[0]
    pad_len = rows_all // seq_count
    model_width = w_qkv.shape[0]
    share_cols = model_width // narrow_size
    block_rows = min(512, pad_len)
    col_start = column * share_cols
    token_count = 2.0 * jnp.sum(lengths.astype(jnp.float32))
    token_sum = lax.psum(token_count, "wide")
    group_scale = groups * token_count / token_sum
    full_x, full_cot = (
        lax.all_gather(inputs, "narrow", axis=1, tiled=True),
        lax.all_gather(cotangent, "narrow", axis=1, tiled=True),
    )
    seq_lengths = jnp.repeat(lengths, 2)
    valid_rows = (
        (jnp.arange(pad_len)[None, :] < seq_lengths[:, None])
        .astype(jnp.float32)
        .reshape(rows_all, 1)
    )
    x_full = full_x.astype(jnp.float32)
    row_mean = jnp.mean(x_full, axis=-1, keepdims=True)
    centered = x_full - row_mean
    inv_std = lax.rsqrt(jnp.mean(centered * centered, axis=-1, keepdims=True) + norm_eps)
    x_hat = centered * inv_std
    hidden = (x_hat * ln_gain + ln_bias).astype(jnp.bfloat16)
    qkv_proj = jnp.dot(hidden, w_qkv, preferred_element_type=jnp.float32)
    qkv_proj = qkv_proj.reshape(seq_count, pad_len, 3, -1, HEAD_DIM)
    cosine, sine_table = rotary_tables(pad_len, ROT)
    q_seq = (
        rotate(qkv_proj[:, :, 0], cosine, sine_table, ROT)
        .astype(jnp.bfloat16)
        .reshape(seq_count, pad_len, -1)
    )
    k_seq = (
        rotate(qkv_proj[:, :, 1], cosine, sine_table, ROT)
        .astype(jnp.bfloat16)
        .reshape(seq_count, pad_len, -1)
    )
    v_seq = qkv_proj[:, :, 2].astype(jnp.bfloat16).reshape(seq_count, pad_len, -1)
    att_width = q_seq.shape[2]
    up_proj = jnp.dot(hidden, w_in, preferred_element_type=jnp.float32) + b_in
    activation = gelu_tanh(up_proj).astype(jnp.bfloat16)
    mlp_part = jnp.dot(activation, w_down, preferred_element_type=jnp.float32)

    def forward_one(packed):
        return attend_forward(packed[0], packed[1], packed[2], packed[3], block_rows)

    att_rows, lse_all = lax.map(forward_one, (q_seq, k_seq, v_seq, seq_lengths))
    attended = att_rows.astype(jnp.bfloat16).reshape(rows_all, att_width)
    branch_share = lax.psum_scatter(
        mlp_part.astype(jnp.bfloat16), "narrow", scatter_dimension=1, tiled=True
    ).astype(jnp.float32)
    w_out_cols = lax.dynamic_slice_in_dim(w_out, col_start, share_cols, 1)
    attn_share = jnp.dot(attended, w_out_cols, preferred_element_type=jnp.float32)
    mixed = (inputs.astype(jnp.float32) + (attn_share + (branch_share + b_down))).astype(
        jnp.bfloat16
    )
    grad_share = group_scale * valid_rows * cotangent.astype(jnp.float32)
    grad_share_low = grad_share.astype(jnp.bfloat16)
    grad_low = (group_scale * valid_rows * full_cot.astype(jnp.float32)).astype(jnp.bfloat16)
    g_b_down = jnp.sum(grad_share_low.astype(jnp.float32), axis=0)
    g_w_down = jnp.einsum("rf,rd->fd", activation, grad_low, preferred_element_type=jnp.float32)
    g_act = jnp.dot(grad_low, w_down.T, preferred_element_type=jnp.float32)
    gelu_value, gelu_pull = jax.vjp(gelu_tanh, up_proj)
    g_up = gelu_pull(g_act)[0].astype(jnp.bfloat16)
    g_b_in = jnp.sum(g_up.astype(jnp.float32), axis=0)
    g_w_in = jnp.einsum("rd,rf->df", hidden, g_up, preferred_element_type=jnp.float32)
    g_hidden_mlp = jnp.dot(g_up, w_in.T, preferred_element_type=jnp.float32)
    g_w_out_rows = jnp.einsum("rd,re->de", attended, grad_low, preferred_element_type=jnp.float32)
    g_att = jnp.dot(grad_low, w_out.T, preferred_element_type=jnp.float32).astype(jnp.bfloat16)

    def backward_one(packed):
        return attend_backward(
            packed[0], packed[1], packed[2], packed[3], packed[4], packed[5], block_rows
        )

    g_qrot, g_krot, g_val = lax.map(
        backward_one,
        (q_seq, k_seq, v_seq, g_att.reshape(seq_count, pad_len, att_width), lse_all, seq_lengths),
    )
    g_query = rotate(g_qrot, cosine, -sine_table, ROT)
    g_key = rotate(g_krot, cosine, -sine_table, ROT)
    g_qkv = (
        jnp.stack([g_query, g_key, g_val], axis=2)
        .reshape(rows_all, 3 * att_width)
        .astype(jnp.bfloat16)
    )
    g_w_qkv = jnp.einsum("rd,rc->dc", hidden, g_qkv, preferred_element_type=jnp.float32)
    g_hidden_attn = jnp.dot(g_qkv, w_qkv.T, preferred_element_type=jnp.float32)
    g_hidden = g_hidden_attn + lax.psum(g_hidden_mlp.astype(jnp.bfloat16), "narrow").astype(
        jnp.float32
    )
    d_hat = g_hidden * ln_gain
    g_x_full = inv_std * (
        d_hat
        - jnp.mean(d_hat, axis=-1, keepdims=True)
        - x_hat * jnp.mean(d_hat * x_hat, axis=-1, keepdims=True)
    )
    g_x_share = lax.dynamic_slice_in_dim(g_x_full, col_start, share_cols, 1)
    g_gain = lax.dynamic_slice_in_dim(jnp.sum(g_hidden * x_hat, axis=0), col_start, share_cols, 0)
    g_bias = lax.dynamic_slice_in_dim(jnp.sum(g_hidden, axis=0), col_start, share_cols, 0)
    g_inputs = grad_share + g_x_share
    qkv_three = g_w_qkv.reshape(model_width, 3, att_width)
    summed = (
        lax.psum_scatter(qkv_three, "wide", scatter_dimension=0, tiled=True),
        lax.psum_scatter(g_w_out_rows, "wide", scatter_dimension=1, tiled=True),
        lax.psum_scatter(g_w_in, "wide", scatter_dimension=0, tiled=True),
        lax.psum_scatter(g_w_down, "wide", scatter_dimension=1, tiled=True),
    )
    g_qkv_part = lax.dynamic_slice_in_dim(summed[0], col_start, share_cols, 2)
    g_out_part = lax.dynamic_slice_in_dim(summed[1], col_start, share_cols, 0)
    small = lax.psum((g_gain, g_bias, g_b_in, g_b_down), "wide")
    return (
        mixed,
        g_inputs,
        small[0],
        small[1],
        g_qkv_part,
        g_out_part,
        summed[2],
        small[2],
        summed[3],
        small[3],
    )


LOG2E = 1.4426950408889634


def inside(value):
    return pltpu.with_memory_space_constraint(value, pltpu.VMEM)


def outside(value):
    return pltpu.with_memory_space_constraint(value, pltpu.HBM)


def mm(left, right, dims=NN):
    return lax.dot_general(left, right, dims, preferred_element_type=F32)


COST_SCALE = 0.1


def cost(micros):
    return pl.CostEstimate(flops=int(COST_SCALE * micros * 1e9), bytes_accessed=1000000, transcendentals=0)


def load_kernel(place, w_qkv, w_out, w_in, w_down, cosine, sine, *refs):
    outs, sems = refs[:-1], refs[-1]
    share = outs[0].shape[1]
    own = place[0]
    sources = [w_qkv.at[:, pl.ds(pl.multiple_of((4 * j + own) * share, 128), share)] for j in range(3)]
    sources += [w_out.at[pl.ds(pl.multiple_of(own * share, 128), share), :], w_in, w_down, cosine, sine]
    copies = [pltpu.make_async_copy(src, dst, sems.at[k]) for k, (src, dst) in enumerate(zip(sources, outs))]
    for copy in copies:
        copy.start()
    for copy in copies:
        copy.wait()


def load_weights(place, w_qkv, w_out, w_in, w_down, cosine, sine):
    width = w_qkv.shape[0]
    share = width // 4
    shapes = [(width, share)] * 3 + [(share, width), w_in.shape, w_down.shape]
    any_place = pl.BlockSpec(memory_space=pl.ANY)
    return pl.pallas_call(
        load_kernel,
        in_specs=[pl.BlockSpec(memory_space=pltpu.SMEM)] + [any_place] * 6,
        out_specs=[any_place] * 8,
        out_shape=[pltpu.VMEM(shape, BF) for shape in shapes] + [pltpu.VMEM(cosine.shape, F32)] * 2,
        scratch_shapes=[pltpu.SemaphoreType.DMA((8,))],
        compiler_params=pltpu.CompilerParams(vmem_limit_bytes=VMEM_BYTES),
        cost_estimate=cost(3),
        name="load_weights",
    )(place, *[outside(value) for value in (w_qkv, w_out, w_in, w_down, cosine, sine)])


def norm_mlp_kernel(place, x0, x1, x2, x3, c0, c1, c2, c3, gain, bias, w_in, b_in, w_down, *refs, first_row):
    left, right, stats, sum_up, sum_grad = refs[-5:]
    step = pl.program_id(0)
    rows, cols = x0.shape
    width, units = w_in.shape
    own = place[0]
    xs = [ref[...].astype(F32) for ref in (x0, x1, x2, x3)]
    mean = jnp.sum(xs[0] + xs[1] + xs[2] + xs[3], axis=1, keepdims=True) * (1.0 / width)
    cs = [x - mean for x in xs]
    squares = cs[0] * cs[0] + cs[1] * cs[1] + cs[2] * cs[2] + cs[3] * cs[3]
    inv_std = lax.rsqrt(jnp.sum(squares, axis=1, keepdims=True) * (1.0 / width) + norm_eps)
    row = first_row + step * rows + lax.broadcasted_iota(jnp.int32, (rows, 1), 0)
    for j, (centered, cot) in enumerate(zip(cs, (c0, c1, c2, c3))):
        here = pl.ds(pl.multiple_of((own ^ j) * cols, cols), cols)
        left[0, :, here] = (centered * inv_std * gain[:, here] + bias[:, here]).astype(BF)
        low = jnp.where(row < place[1], cot[...], jnp.zeros_like(cot))
        left[1, :, here] = low
        if j == 0:
            sum_grad[...] = jnp.sum(low.astype(F32).reshape(rows // 8, 8, cols), axis=0)
    lane = lax.broadcasted_iota(jnp.int32, (rows, 128), 1)
    stats[...] = jnp.where(lane == 0, mean, inv_std)
    h = left[0]
    g = left[1]
    part = min(512, units)
    for first in range(0, units, part):
        here = pl.ds(first, part)
        up = mm(h, w_in[:, here]) + b_in[:, here]
        g_act = mm(g, w_down[here, :], NT)
        square = up * up
        tanh = jnp.tanh(up * (GELU_A + GELU_A * GELU_B * square))
        half = 0.5 * up
        plus = 1.0 + tanh
        slope = 0.5 * plus + (half * (1.0 - tanh * tanh)) * (GELU_A + 3.0 * GELU_A * GELU_B * square)
        g_up = slope * g_act
        right[0, :, here] = g_up.astype(BF)
        right[1, :, here] = (half * plus).astype(BF)
        sum_up[:, here] = jnp.sum(g_up.reshape(rows // 8, 8, part), axis=0)


def norm_mlp(place, near, far, gain, bias, w_in, b_in, w_down, start_row, first_row, total, before=None):
    rows, cols = far[0].shape
    rows //= 2
    width, units = w_in.shape
    tile = min(256, rows)
    tiles = rows // tile
    offset = first_row // tile
    begin = start_row // tile

    def part(j):
        return [pl.BlockSpec((tile, cols), lambda i: (i + begin, 0))] * 2 + [pl.BlockSpec((tile, cols), lambda i: (i + j * tiles, 0))] * 2

    def rowed(size):
        return pl.BlockSpec((tile, size), lambda i: (i + offset, 0))

    def paired(size):
        return pl.BlockSpec((2, tile, size), lambda i: (0, i + offset, 0))

    def eight(size):
        return pl.BlockSpec((8, size), lambda i: (i + offset, 0))

    def whole(shape):
        return pl.BlockSpec(memory_space=pltpu.VMEM)

    shape = jax.ShapeDtypeStruct
    outs = [pltpu.VMEM((2, total, width), BF), pltpu.VMEM((2, total, units), BF), shape((total, 128), F32),
            shape((total // tile * 8, units), F32), shape((total // tile * 8, cols), F32)]
    before = [] if before is None else [inside(before[0]), inside(before[1]), *before[2:]]
    return pl.pallas_call(
        functools.partial(norm_mlp_kernel, first_row=first_row),
        grid=(tiles,),
        in_specs=[pl.BlockSpec(memory_space=pltpu.SMEM)]
        + part(0) + part(1)
        + [whole((1, width)), whole((1, width)), whole((width, units)), whole((1, units)), whole((units, width))]
        + [pl.BlockSpec(memory_space=pl.ANY)] * len(before),
        out_specs=[paired(width), paired(units), rowed(128), eight(units), eight(cols)],
        out_shape=outs,
        input_output_aliases={14 + k: k for k in range(len(before))},
        compiler_params=pltpu.CompilerParams(vmem_limit_bytes=VMEM_BYTES),
        cost_estimate=cost(0.010 * rows),
        name="norm_mlp",
    )(place, near[0], near[1], *far, near[2], near[3], *far, gain, bias, inside(w_in), b_in, inside(w_down), *before)


def turn(field, cosine, sine):
    lane = lax.broadcasted_iota(jnp.int32, field.shape, 1)
    size = field.shape[1]
    other = jnp.where(lane % 2 == 0, pltpu.roll(field, size - 1, 1), pltpu.roll(field, 1, 1))
    return field * cosine + other * sine


def attend_kernel(
    place, left, w_q, w_k, w_v, w_o, cosine, sine, cos_all, sin_all, attended, g_qkv,
    k_aug, k_t, v_nat, v_t, q_nat, q_aug, d_out, gk_acc, gv_acc, *, tiles, tile, pairs,
):
    step = pl.program_id(0)
    length = place[1]
    share = 128 * pairs

    @pl.when(step < tiles)
    def project():
        h = left[0]
        cos = cosine[...]
        sin = sine[...]
        q_all = mm(h, w_q[...])
        k_all = mm(h, w_k[...])
        v_all = mm(h, w_v[...])
        g_all = mm(left[1], w_o[...], NT)
        start = pl.multiple_of(step * tile, tile)
        here = pl.ds(start, tile)
        lane = lax.broadcasted_iota(jnp.int32, (tile, 128), 1)
        key_row = start + lax.broadcasted_iota(jnp.int32, (tile, 128), 0)
        closed = jnp.where(key_row < length, 0.0, -1e30)
        first = lane < HEAD_DIM
        sub = lax.broadcasted_iota(jnp.int32, (128, tile), 0)
        for p in range(pairs):
            cut = slice(128 * p, 128 * (p + 1))
            q = turn(q_all[:, cut], cos, sin) * HEAD_DIM ** (-0.5)
            k = turn(k_all[:, cut], cos, sin)
            v = v_all[:, cut]
            q_nat[p, here, :] = q.astype(BF)
            v_nat[p, here, :] = v.astype(BF)
            k_aug[2 * p, here, :] = jnp.where(first, k, jnp.where(lane == HEAD_DIM, closed, 0.0)).astype(BF)
            k_aug[2 * p + 1, here, :] = jnp.where(first, jnp.where(lane == 0, closed, 0.0), k).astype(BF)
            q_t = q.T
            q_aug[2 * p, :, here] = jnp.where(sub < HEAD_DIM, q_t, jnp.where(sub == HEAD_DIM, 1.0, 0.0)).astype(BF)
            q_aug[2 * p + 1, :, here] = jnp.where(sub < HEAD_DIM, jnp.where(sub == 0, 1.0, 0.0), q_t).astype(BF)
            k_t[p, :, here] = k.T.astype(BF)
            v_t[p, :, here] = v.T.astype(BF)
            d_out[p, :, here] = g_all[:, cut].T

    @pl.when(step == tiles)
    def attend():
        lane = lax.broadcasted_iota(jnp.int32, (tile, 128), 1)
        sub = lax.broadcasted_iota(jnp.int32, (128, tile), 0)
        later = lax.broadcasted_iota(jnp.int32, (tile, tile), 0) > lax.broadcasted_iota(jnp.int32, (tile, tile), 1)
        heads = range(2 * pairs)
        mine = [lane < HEAD_DIM, lane >= HEAD_DIM]
        mine_t = [sub < HEAD_DIM, sub >= HEAD_DIM]
        cuts = [slice(0, HEAD_DIM), slice(HEAD_DIM, 2 * HEAD_DIM)]
        def score(i):
            n = (i + 1) * tile
            return [mm(k_aug[h, :n, :], q_aug[h, :, i * tile : n]) for h in heads]

        for i in range(tiles):
            n = (i + 1) * tile
            here = slice(i * tile, n)
            old = slice(0, i * tile)
            scores = ahead if i else score(0)
            weights, inverses = [], []
            for h in heads:
                s = scores[h]
                tail = jnp.where(later, -1e30, s[n - tile :])
                s = tail if i == 0 else jnp.concatenate([s[: n - tile], tail], axis=0)
                e = jnp.exp(s - jnp.max(s, axis=0, keepdims=True))
                inverses.append(1.0 / jnp.sum(e, axis=0, keepdims=True))
                weights.append(e)
            lows = [e.astype(BF) for e in weights]
            outs = [mm(v_t[h // 2, cuts[h % 2], :n], lows[h]) * inverses[h] for h in heads]
            scaled, inner = [], []
            for h in heads:
                d = d_out[h // 2, cuts[h % 2], here]
                inner.append(jnp.sum(d * outs[h], axis=0, keepdims=True) * inverses[h])
                scaled.append(d * inverses[h])
            g_scores = []
            for h in heads:
                p, half = divmod(h, 2)
                zero = jnp.zeros((HEAD_DIM, tile), BF)
                d_t = scaled[h].astype(BF)
                d_t = jnp.concatenate([d_t, zero] if half == 0 else [zero, d_t], axis=0)
                g_scores.append((weights[h] * (mm(v_nat[p, :n, :], d_t) - inner[h])).astype(BF))
            if i + 1 < tiles:
                ahead = score(i + 1)
            for p in range(pairs):
                cut = slice(p * 128, p * 128 + 128)
                pair = (2 * p, 2 * p + 1)
                attended[here, cut] = jnp.concatenate([outs[h] for h in pair], axis=0).T.astype(BF)
                d_nat = jnp.concatenate([scaled[h] for h in pair], axis=0).T
                q_here = q_nat[p, here, :]
                g_q = jnp.concatenate([mm(k_t[p, cuts[h % 2], :n], g_scores[h]) for h in pair], axis=0).T * HEAD_DIM ** (-0.5)
                g_qkv[here, cut] = turn(g_q, cos_all[here, :], -sin_all[here, :]).astype(BF)
                add_v = sum(mm(lows[h], jnp.where(mine[h % 2], d_nat, 0.0).astype(BF)) for h in pair)
                add_k = sum(mm(g_scores[h], jnp.where(mine[h % 2], q_here, jnp.zeros_like(q_here))) for h in pair)
                if i > 0:
                    gv_acc[p, old] += add_v[: n - tile]
                    gk_acc[p, old] += add_k[: n - tile]
                gv_acc[p, here] = add_v[n - tile :]
                gk_acc[p, here] = add_k[n - tile :]
        for p in range(pairs):
            for j, acc in ((1, gk_acc), (2, gv_acc)):
                cut = slice(j * share + p * 128, j * share + p * 128 + 128)
                total = acc[p]
                if j == 1:
                    total = turn(total, cos_all[...], -sin_all[...])
                g_qkv[:, cut] = total.astype(BF)


def attend(place, left, weights):
    _, rows, width = left.shape
    share = width // 4
    pairs = share // 128
    tile = min(256, rows)
    tiles = rows // tile

    def early(i, _):
        return (jnp.minimum(i, tiles - 1), 0)

    def whole(shape):
        return pl.BlockSpec(shape, lambda i, _: (0, 0), pipeline_mode=pl.Buffered(1))

    w_q, w_k, w_v, w_o, _, _, cosine, sine = [inside(value) for value in weights]
    return pl.pallas_call(
        functools.partial(attend_kernel, tiles=tiles, tile=tile, pairs=pairs),
        grid_spec=pltpu.PrefetchScalarGridSpec(
            num_scalar_prefetch=1,
            grid=(tiles + 1,),
            in_specs=[
                pl.BlockSpec((2, tile, width), lambda i, _: (0, jnp.minimum(i, tiles - 1), 0)),
                whole(w_q.shape), whole(w_k.shape), whole(w_v.shape), whole(w_o.shape),
                pl.BlockSpec((tile, 128), early),
                pl.BlockSpec((tile, 128), early),
                whole((rows, 128)), whole((rows, 128)),
            ],
            out_specs=[whole((rows, share)), whole((rows, 3 * share))],
            scratch_shapes=[
                pltpu.VMEM((2 * pairs, rows, 128), BF),
                pltpu.VMEM((pairs, 128, rows), BF),
                pltpu.VMEM((pairs, rows, 128), BF),
                pltpu.VMEM((pairs, 128, rows), BF),
                pltpu.VMEM((pairs, rows, 128), BF),
                pltpu.VMEM((2 * pairs, 128, rows), BF),
                pltpu.VMEM((pairs, 128, rows), F32),
                pltpu.VMEM((pairs, rows, 128), F32),
                pltpu.VMEM((pairs, rows, 128), F32),
            ],
        ),
        out_shape=[pltpu.VMEM((rows, share), BF), pltpu.VMEM((rows, 3 * share), BF)],
        compiler_params=pltpu.CompilerParams(vmem_limit_bytes=VMEM_BYTES),
        cost_estimate=cost(0.014 * rows),
        name="attend",
    )(place, inside(left), w_q, w_k, w_v, w_o, cosine, sine, cosine, sine)


def weight_mlp_kernel(place, scale, left_0, left_1, right_0, right_1, keep, send):
    total = (scale[0] * (mm(left_0[0], right_0[0], TN) + mm(left_1[0], right_1[0], TN))).astype(BF)
    half = total.shape[0] // 2
    odd = place[2] == 1
    keep[0] = jnp.where(odd, total[half:], total[:half])
    send[0] = jnp.where(odd, total[:half], total[half:])


def weight_att_kernel(place, scale, left_0, left_1, qkv_0, qkv_1, att_0, att_1, keep, send):
    odd = place[2] == 1
    size = qkv_0.shape[1]
    first = (scale[0] * (mm(left_0[0], qkv_0[...], TN) + mm(left_1[0], qkv_1[...], TN))).astype(BF)
    second = (scale[0] * (mm(left_0[1], att_0[...], TN) + mm(left_1[1], att_1[...], TN))).astype(BF)
    half = first.shape[0] // 2
    keep[0, :, :size] = jnp.where(odd, first[half:], first[:half])
    send[0, :, :size] = jnp.where(odd, first[:half], first[half:])
    keep[0, :, size:] = jnp.where(odd, second[half:], second[:half])
    send[0, :, size:] = jnp.where(odd, second[:half], second[half:])


def weight_hold_kernel(place, scale, left_0, left_1, right_0, right_1, hold, ship):
    total = (scale[0] * (mm(left_0[0], right_0[0], TN) + mm(left_1[0], right_1[0], TN))).astype(BF)
    half = total.shape[0] // 2
    odd = place[2] == 1
    mine = jnp.where(odd, total[half:], total[:half])
    other = jnp.where(odd, total[:half], total[half:])

    @pl.when(pl.program_id(0) < 2)
    def near():
        hold[0, 0] = mine
        hold[0, 1] = other

    @pl.when(pl.program_id(0) >= 2)
    def far():
        ship[0, 0] = mine
        ship[0, 1] = other


def chip_of(slot, place):
    return (2 * (slot & 1) + (slot >> 1)) ^ place[3]


def weight_mlp(place, scale, lefts, rights, kind):
    _, rows, width = lefts[0].shape
    units = rights[0].shape[2]
    size = width // 8
    column = pl.BlockSpec((1, rows, 2 * size), lambda i, where: (kind, 0, chip_of(i, where)))
    whole = pl.BlockSpec((1, rows, units), lambda i, where: (kind, 0, 0), pipeline_mode=pl.Buffered(1))
    if kind == 0:
        kernel = weight_mlp_kernel
        slot = pl.BlockSpec((1, size, units), lambda i, where: (i, 0, 0))
        outs = [slot, slot]
        out = [pltpu.HBM((4, size, units), BF)] * 2
    else:
        kernel = weight_hold_kernel
        outs = [pl.BlockSpec((1, 2, size, units), lambda i, where: (jnp.minimum(i, 1), 0, 0, 0)),
                pl.BlockSpec((1, 2, size, units), lambda i, where: (jnp.maximum(i - 2, 0), 0, 0, 0))]
        out = [pltpu.HBM((2, 2, size, units), BF)] * 2
    return pl.pallas_call(
        kernel,
        grid_spec=pltpu.PrefetchScalarGridSpec(
            num_scalar_prefetch=1, grid=(4,),
            in_specs=[pl.BlockSpec(memory_space=pltpu.SMEM), column, column, whole, whole], out_specs=outs,
        ),
        out_shape=out,
        compiler_params=pltpu.CompilerParams(vmem_limit_bytes=VMEM_BYTES),
        cost_estimate=cost(0.0065 * rows),
        name="weight_mlp",
    )(place, scale, *[inside(value) for value in (*lefts, *rights)])


def weight_att(place, scale, lefts, qkvs, atts):
    _, rows, width = lefts[0].shape
    units = qkvs[0].shape[1] + atts[0].shape[1]
    size = width // 8
    column = pl.BlockSpec((2, rows, 2 * size), lambda i, where: (0, 0, chip_of(i, where)))

    def whole(ref):
        return pl.BlockSpec(ref.shape, lambda i, where: (0, 0), pipeline_mode=pl.Buffered(1))

    slot = pl.BlockSpec((1, size, units), lambda i, where: (i, 0, 0))
    out = pltpu.HBM((4, size, units), BF)
    return pl.pallas_call(
        weight_att_kernel,
        grid_spec=pltpu.PrefetchScalarGridSpec(
            num_scalar_prefetch=1, grid=(4,),
            in_specs=[pl.BlockSpec(memory_space=pltpu.SMEM), column, column] + [whole(r) for r in (*qkvs, *atts)],
            out_specs=[slot, slot],
        ),
        out_shape=[out, out],
        compiler_params=pltpu.CompilerParams(vmem_limit_bytes=VMEM_BYTES),
        cost_estimate=cost(0.007 * rows),
        name="weight_att",
    )(place, scale, *[inside(value) for value in (*lefts, *qkvs, *atts)])


def branch_kernel(place, left, right, att, g_qkv, w_q, w_k, w_v, w_o, w_in, w_down, gain, bias,
                  keep, near, far_b, far_g, sums, column_sums):
    own = place[0]
    rows, share = att.shape
    total = mm(right[1], w_down[...]) + mm(att[...], w_o[...])
    g_total = mm(right[0], w_in[...], NT)
    for j, w in enumerate((w_q, w_k, w_v)):
        g_total += mm(g_qkv[:, j * share : (j + 1) * share], w[...], NT)
    odd = (own & 1) == 1
    up = (own >> 1) == 1
    for kind, (whole, far) in enumerate(((total, far_b), (g_total, far_g))):
        cuts = [whole[:, j * share : (j + 1) * share].astype(BF) for j in range(4)]
        low = [jnp.where(odd, cuts[2 * y + 1], cuts[2 * y]) for y in range(2)]
        high = [jnp.where(odd, cuts[2 * y], cuts[2 * y + 1]) for y in range(2)]
        keep[0, kind] = jnp.where(up, low[1], low[0])
        keep[1, kind] = jnp.where(up, low[0], low[1])
        near[kind] = jnp.where(up, high[1], high[0])
        far[...] = jnp.where(up, high[0], high[1])
    turned = g_total * (left[0].astype(F32) - bias[...])
    mean_part = jnp.sum(g_total * gain[...], axis=1, keepdims=True)
    inner_part = jnp.sum(turned, axis=1, keepdims=True)
    lane = lax.broadcasted_iota(jnp.int32, (rows, 128), 1)
    sums[...] = jnp.where(lane == 0, mean_part, inner_part).T[:8, :]

    @pl.when(pl.program_id(0) == 0)
    def clear():
        column_sums[...] = jnp.zeros_like(column_sums)

    column_sums[0:1, :] += jnp.sum(g_total, axis=0, keepdims=True)
    column_sums[1:2, :] += jnp.sum(turned, axis=0, keepdims=True)


def branch_parts(place, left, right, att, g_qkv, weights, gain, bias, first_row, rows):
    _, _, width = left.shape
    units = right.shape[2]
    share = att.shape[1]
    tile = min(256, rows)
    tiles = rows // tile
    offset = first_row // tile

    def paired(k, size):
        return pl.BlockSpec((k, tile, size), lambda i, _: (0, i + offset, 0))

    def rowed(size):
        return pl.BlockSpec((tile, size), lambda i, _: (i + offset, 0))

    def whole(shape):
        return pl.BlockSpec(shape, lambda i, _: (0, 0), pipeline_mode=pl.Buffered(1))

    weights = [inside(value) for value in weights[:6]]
    shape = jax.ShapeDtypeStruct
    slots = pl.BlockSpec((2, 2, tile, share), lambda i, _: (0, 0, i, 0))
    sent = pl.BlockSpec((2, tile, share), lambda i, _: (0, i, 0))
    rowed_out = pl.BlockSpec((tile, share), lambda i, _: (i, 0))
    return pl.pallas_call(
        branch_kernel,
        grid_spec=pltpu.PrefetchScalarGridSpec(
            num_scalar_prefetch=1,
            grid=(tiles,),
            in_specs=[
                paired(1, width), paired(2, units), rowed(share), rowed(3 * share),
                *[whole(value.shape) for value in weights],
                whole((1, width)), whole((1, width)),
            ],
            out_specs=[slots, sent, rowed_out, rowed_out, pl.BlockSpec((8, tile), lambda i, _: (0, i)), pl.BlockSpec((8, width), lambda i, _: (0, 0))],
        ),
        out_shape=[pltpu.HBM((2, 2, rows, share), BF)] + [pltpu.HBM((2, rows, share), BF)] + [pltpu.HBM((rows, share), BF)] * 2 + [shape((8, rows), F32),
                   shape((8, width), F32)],
        compiler_params=pltpu.CompilerParams(vmem_limit_bytes=VMEM_BYTES),
        cost_estimate=cost(0.010 * rows),
        name="branch_parts",
    )(place, inside(left), inside(right), inside(att), inside(g_qkv), *weights, gain, bias)


def combine_kernel(count, keep_in, x_in, hold, z_down, kept, core_b, core_g, z_in, low_in, zz_down, low_down, chip):
    size, units = keep_in.shape[1:]
    for k in range(2):
        z_in[k * size : (k + 1) * size] = keep_in[2 + k] + x_in[2 + k]
        low_in[k] = keep_in[k] + x_in[k]
        zz_down[k] = hold[1, k] + z_down[1, k]
        low_down[k] = hold[0, k] + z_down[0, k]
    rows = z_in.shape[0] - 2 * size
    row = lax.broadcasted_iota(jnp.int32, (rows, units), 0)
    value = jnp.full((rows, units), count[0], F32)
    high = value.astype(BF).astype(F32)
    z_in[2 * size :] = jnp.where(row == 0, high, jnp.where(row == 1, value - high, 0.0)).astype(BF)
    chip[0] = kept[1, 0] + core_b[...]
    chip[1] = kept[1, 1] + core_g[...]


def combine(count, keep_in, x_in, hold, z_down, kept, core):
    _, size, units = keep_in.shape
    _, _, rows, cols = kept.shape
    inner = pl.BlockSpec(memory_space=pltpu.VMEM)
    shapes = [(2 * size + 16, units), (2, size, units), (2, size, units), (2, size, units), (2, rows, cols)]
    return pl.pallas_call(
        combine_kernel,
        in_specs=[pl.BlockSpec(memory_space=pltpu.SMEM)] + [inner] * 7,
        out_specs=[inner] * 5,
        out_shape=[pltpu.HBM(shape, BF) for shape in shapes],
        compiler_params=pltpu.CompilerParams(vmem_limit_bytes=VMEM_BYTES),
        cost_estimate=cost(3),
        name="combine",
    )(count, *[outside(value) for value in (keep_in, x_in, hold, z_down, kept, *core)])


def final_kernel(place, scale, keep, near, far, x_ref, cot, stats, sums, gain, bias_down, *refs, first_row):
    mixed, g_x = refs[-2:]
    step = pl.program_id(0)
    rows, cols = x_ref.shape
    width = 4 * cols
    x = x_ref[...].astype(F32)
    branch = keep[0, 0].astype(F32) + near[0].astype(F32) + far[0].astype(F32)
    mixed[...] = (x + (branch + bias_down[...])).astype(BF)
    g = scale[0] * (keep[0, 1].astype(F32) + near[1].astype(F32) + far[1].astype(F32))
    inv_std = stats[:, 1:2]
    x_hat = (x - stats[:, 0:1]) * inv_std
    totals = (scale[0] / width) * jnp.concatenate([sums[...], jnp.zeros((126, rows), F32)], axis=0).T
    row = first_row + step * rows + lax.broadcasted_iota(jnp.int32, (rows, 1), 0)
    weight = jnp.where(row < place[1], scale[0], 0.0)
    g_out = weight * cot[...].astype(F32)
    g_x[...] = g_out + inv_std * (g * gain[...] - totals[:, 0:1] - x_hat * totals[:, 1:2])


def finish_rows(place, scale, keep, near, far, x, cot, stats, sums, gain, bias_down, sequence, first_row, before=None):
    _, rows, cols = far.shape
    tile = min(512, rows)
    tiles = rows // tile
    pad_len = stats.shape[0]
    begin = (sequence * pad_len + first_row) // tile
    inner = first_row // tile
    part = pl.BlockSpec((tile, cols), lambda i: (i + begin, 0))
    cored = pl.BlockSpec((1, tile, cols), lambda i: (0, i, 0))
    kept = pl.BlockSpec((1, 2, tile, cols), lambda i: (0, 0, i, 0))
    both = pl.BlockSpec((2, tile, cols), lambda i: (0, i, 0))
    flat = pl.BlockSpec((1, cols), lambda i: (0, 0))
    scalar = pl.BlockSpec(memory_space=pltpu.SMEM)
    shape = jax.ShapeDtypeStruct
    before = [] if before is None else list(before)
    return pl.pallas_call(
        functools.partial(final_kernel, first_row=first_row),
        grid=(tiles,),
        in_specs=[scalar, scalar, kept, both, both, part, part,
                  pl.BlockSpec((tile, 128), lambda i: (i + inner, 0)), pl.BlockSpec((2, tile), lambda i: (0, i + begin)), flat, flat]
        + [pl.BlockSpec(memory_space=pl.ANY)] * len(before),
        out_specs=[part, part],
        out_shape=[shape(x.shape, BF), shape(x.shape, F32)],
        input_output_aliases={11 + k: k for k in range(len(before))},
        compiler_params=pltpu.CompilerParams(vmem_limit_bytes=VMEM_BYTES),
        cost_estimate=cost(0.003 * rows),
        name="finish_rows",
    )(place, scale, *[outside(value) for value in (keep, near, far, x, cot, stats)], sums, gain, bias_down, *before)


def final_weight_kernel(factor, low_in, far_in, low_down, far_down, low_a, far_a, g_in, g_down, g_qkv, g_out):
    scale = factor[0]
    _, size, cols = g_qkv.shape
    g_in[...] = scale * (low_in[...].astype(F32) + far_in[:size].astype(F32))
    g_down[...] = (scale * (low_down[...].astype(F32) + far_down[...].astype(F32))).T
    for j in range(3):
        cut = slice(j * cols, (j + 1) * cols)
        g_qkv[j] = scale * (low_a[:, cut].astype(F32) + far_a[:size, cut].astype(F32))
    cut = slice(3 * cols, 4 * cols)
    g_out[...] = (scale * (low_a[:, cut].astype(F32) + far_a[:size, cut].astype(F32))).T


def finish_weights(factor, low_in, far_in, low_down, far_down, low_a, far_a):
    size, units = low_in.shape
    cols = low_a.shape[1] // 4
    shape = jax.ShapeDtypeStruct
    return pl.pallas_call(
        final_weight_kernel,
        in_specs=[pl.BlockSpec(memory_space=pltpu.SMEM)] + [pl.BlockSpec(memory_space=pltpu.VMEM)] * 6,
        out_specs=[pl.BlockSpec(memory_space=pltpu.VMEM)] * 4,
        out_shape=[shape((size, units), F32), shape((units, size), F32), shape((3, size, cols), F32), shape((cols, size), F32)],
        compiler_params=pltpu.CompilerParams(vmem_limit_bytes=VMEM_BYTES),
        cost_estimate=cost(3),
        name="finish_weights",
    )(factor, low_in, far_in, low_down, far_down, low_a, far_a)


def swap(value, axis, bit):
    size = lax.axis_size(axis)
    return lax.ppermute(value, axis, [(i, i ^ bit) for i in range(size)])


def sum_small(value, axis):
    bit = 1
    while bit < lax.axis_size(axis):
        value = value + swap(value, axis, bit)
        bit *= 2
    return value


def add_core(kept, core):
    return kept[1] + jnp.stack(core)


def pack(values, units):
    padded = jnp.concatenate([values, jnp.zeros((-values.shape[0] % units,), F32)]).reshape(-1, units)
    high = lax.reduce_precision(padded, 8, 7)
    rows = jnp.concatenate([high, padded - high], axis=0).astype(BF)
    return jnp.concatenate([rows, jnp.zeros((-rows.shape[0] % 16, units), BF)], axis=0)


def unpack(rows, count):
    part = -(-count // rows.shape[1])
    high, low = rows[:part].astype(F32), rows[part : 2 * part].astype(F32)
    return (high + low).reshape(-1)[:count]


def after(value, *others):
    return lax.optimization_barrier((value, *others))[0]


def on_device_fast(inputs, cotangent, lengths, ln_gain, ln_bias, w_qkv, w_out, w_in, b_in, w_down, b_down):
    groups = lax.axis_size("wide")
    column = lax.axis_index("narrow")
    place_wide = lax.axis_index("wide")
    rows_all, cols = inputs.shape
    pad_len = rows_all // 2
    width = w_qkv.shape[0]
    units = w_in.shape[1]
    place = jnp.stack([column, lengths[0], place_wide & 1, place_wide >> 1]).astype(jnp.int32)
    gain = ln_gain.reshape(1, width)
    bias = ln_bias.reshape(1, width)
    b_up = b_in.reshape(1, units)
    half = pad_len // 2
    cuts = ((0, half), (half, pad_len), (pad_len, rows_all))
    own_gain = lax.dynamic_slice_in_dim(ln_gain, column * cols, cols, 0).reshape(1, cols)
    b_row = b_down.reshape(1, cols)

    across = [swap(jnp.concatenate([inputs[low:high], cotangent[low:high]], axis=0), "narrow", 2) for low, high in cuts]
    near = (inputs, swap(inputs, "narrow", 1), cotangent, swap(cotangent, "narrow", 1))
    count = (2.0 * jnp.sum(lengths.astype(F32))).reshape(1)
    count_x = count + swap(count, "wide", 1)
    weights = load_weights(place, w_qkv, w_out, w_in, w_down, *turn_tables(pad_len))
    up_in, up_down = weights[4:6]

    def far(k, *earlier):
        rows = after(across[k], *earlier)
        return rows, swap(rows, "narrow", 1)

    def branch(place, mlp, att, first_row, rows):
        kept, near, far_b, far_g, sums, columns = branch_parts(
            place, mlp[0], mlp[1], *att, weights, gain, bias, first_row, rows)
        return kept, near, (far_b, far_g), sums, columns

    first = norm_mlp(place, near, far(0, weights[0], count_x), gain, bias, up_in, b_up, up_down, 0, 0, pad_len)
    place = after(place, first[3])
    mlp_0 = norm_mlp(place, near, far(1, first[3]), gain, bias, up_in, b_up, up_down, half, half, pad_len, first)
    place = after(place, mlp_0[3])
    att_0 = attend(place, mlp_0[0], weights)
    place = after(place, att_0[0])
    mlp_1 = norm_mlp(place, near, far(2, att_0[0]), gain, bias, up_in, b_up, up_down, pad_len, 0, pad_len)
    place = after(place, mlp_1[3])
    lefts = (mlp_0[0], mlp_1[0])
    rights = (mlp_0[1], mlp_1[1])
    keep_in, send_in = weight_mlp(place, count, lefts, rights, 0)
    place = after(place, keep_in)
    x_in = swap(send_in, "wide", 1)
    hold_down, ship_down = weight_mlp(place, count, lefts, rights, 1)
    place = after(place, hold_down)
    z_down = swap(ship_down, "wide", 2)
    kept_0, near_0, sent_0, sums_0, columns_0 = branch(place, mlp_0, att_0, 0, pad_len)
    core_0 = [swap(part, "narrow", 1) for part in sent_0]
    place = after(place, sums_0)
    att_1 = attend(place, mlp_1[0], weights)
    size = keep_in.shape[1]
    x_in, z_down, count_x, *core_0 = lax.optimization_barrier((x_in, z_down, count_x, *core_0, att_1[0]))[:5]
    z_in, low_in, zz_down, low_down, chip_0 = combine(count_x, keep_in, x_in, hold_down, z_down, kept_0, core_0)
    z_in = swap(z_in, "wide", 2)
    zz_down = swap(zz_down, "wide", 4)
    y_0 = swap(chip_0, "narrow", 2)
    near_0 = swap(after(near_0, chip_0), "narrow", 1)
    place = after(place, low_in, low_down, chip_0, att_1[0])
    keep_a, send_a = weight_att(place, count, lefts, (att_0[1], att_1[1]), (att_0[0], att_1[0]))
    x_a = swap(send_a, "wide", 1)
    place = after(place, keep_a, near_0)
    kept_1, near_1, sent_1, sums_1, columns_1 = branch(place, mlp_1, att_1, 0, pad_len)
    core_1 = [swap(part, "narrow", 1) for part in sent_1]
    z_in, zz_down, y_0, sums_0, columns_0 = lax.optimization_barrier((z_in, zz_down, y_0, sums_0, columns_0, sums_1))[:5]
    count_row = count_x + unpack(z_in[2 * size :], units)[:128]
    zz_in = swap(jnp.concatenate([low_in[1] + z_in[size : 2 * size], pack(jnp.broadcast_to(count_row[:1], (units,)), units)], axis=0), "wide", 4)
    low_in = low_in[0] + z_in[:size]
    x_d = swap(low_down[1] + zz_down[1], "wide", 1)
    low_down = low_down[0] + zz_down[0]
    sums = jnp.concatenate([sums_0[:2], sums_1[:2], columns_0[:2] + columns_1[:2]], axis=1)
    sums = after(sums, y_0)
    sums = sums + swap(sums, "narrow", 1)
    core_1 = [after(part, sums, low_down, low_in) for part in core_1]
    chip_1 = add_core(kept_1, core_1)
    y_1 = swap(chip_1, "narrow", 2)
    far_sums = swap(after(sums, chip_1), "narrow", 2)
    near_1 = swap(after(near_1, chip_1), "narrow", 1)
    x_a = after(x_a, chip_1)
    z_a = swap(keep_a[2:] + x_a[2:], "wide", 2)
    low_a = keep_a[:2] + x_a[:2]
    z_a = after(z_a, low_a)
    zz_a = swap(low_a[1] + z_a[1], "wide", 4)
    low_a = low_a[0] + z_a[0]
    y_1, far_sums, near_1, zz_in = lax.optimization_barrier((y_1, far_sums, near_1, zz_in, low_a))[:4]
    count_row = count_row + unpack(zz_in[size:], units)[:128]
    per_count = groups / count_row[:1]
    scale = count * per_count
    sums = sums + far_sums
    columns = lax.dynamic_slice_in_dim(sums[:, rows_all:], column * cols, cols, 1)
    sum_up, sum_down = [after(mlp_0[k], y_1) + mlp_1[k] for k in (3, 4)]
    small = count * jnp.concatenate([columns[1] / own_gain[0], columns[0], jnp.sum(sum_up, axis=0), jnp.sum(sum_down, axis=0)])
    small = small + swap(small, "wide", 1)
    ends = finish_rows(place, scale, kept_0, near_0, y_0, inputs, cotangent, mlp_0[2], sums, own_gain, b_row, 0, 0)
    small = small + swap(small, "wide", 2)
    ends = finish_rows(place, scale, kept_1, near_1, y_1, inputs, cotangent, mlp_1[2], sums, own_gain, b_row, 1, 0, ends)
    small = per_count * (small + swap(small, "wide", 4))
    zz_a, x_d = lax.optimization_barrier((zz_a, x_d, ends[0]))[:2]
    g_in, g_down, g_qkv, g_out = finish_weights(per_count, low_in, zz_in, low_down, x_d, low_a, zz_a)
    return (
        ends[0],
        ends[1],
        small[:cols],
        small[cols : 2 * cols],
        jnp.transpose(g_qkv, (1, 0, 2)),
        g_out,
        g_in,
        small[2 * cols : 2 * cols + units],
        g_down,
        small[2 * cols + units :],
    )


def turn_tables(length):
    position = np.arange(length, dtype=np.float32)[:, None]
    frequency = (10000.0 ** (-2.0 * np.arange(ROT // 2, dtype=np.float32) / ROT)).astype(np.float32)
    angles = (position * frequency[None, :]).astype(np.float32)
    cosine = np.ones((length, HEAD_DIM), np.float32)
    sine = np.zeros((length, HEAD_DIM), np.float32)
    cosine[:, :ROT] = np.repeat(np.cos(angles), 2, axis=1)
    sine[:, 0:ROT:2] = -np.sin(angles)
    sine[:, 1:ROT:2] = np.sin(angles)
    return jnp.asarray(np.tile(cosine, (1, 2))), jnp.asarray(np.tile(sine, (1, 2)))


def solution(mesh):
    placed = (
        P("wide", "narrow"),
        P("wide", "narrow"),
        P("wide"),
        P(),
        P(),
        P(),
        P(),
        P(None, "narrow"),
        P("narrow"),
        P("narrow", None),
        P("narrow"),
    )
    paired = mesh.shape["narrow"] == 4 and mesh.shape["wide"] == 8
    return jax.shard_map(
        on_device_fast if paired else on_device,
        mesh=mesh,
        in_specs=placed,
        out_specs=(
            P("wide", "narrow"),
            P("wide", "narrow"),
            P("narrow"),
            P("narrow"),
            P("wide", None, "narrow"),
            P("narrow", "wide"),
            P("wide", "narrow"),
            P("narrow"),
            P("narrow", "wide"),
            P("narrow"),
        ),
        check_vma=False,
    )
```

```python
import functools

import jax
import jax.numpy as jnp
import numpy as np
from jax import lax
from jax.experimental import pallas as pl
from jax.experimental.pallas import tpu as pltpu
from jax.sharding import PartitionSpec as P

HEAD_DIM = 64
ROT = 32
GELU_A = 0.7978845608028654
GELU_B = 0.044715
VMEM_BYTES = 24 * 1024 * 1024
F32 = jnp.float32
BF = jnp.bfloat16
NN = (((1,), (0,)), ((), ()))
NT = (((1,), (1,)), ((), ()))
TN = (((0,), (0,)), ((), ()))


norm_eps = 1e-05


def gelu_tanh(value_in):
    return (
        0.5
        * value_in
        * (
            1.0
            + jnp.tanh(0.7978845608028654 * (value_in + 0.044715 * value_in * value_in * value_in))
        )
    )


def rotary_tables(seq_len, rot_dims):
    position = jnp.arange(seq_len).astype(jnp.float32)[:, None]
    freq_index = jnp.arange(rot_dims // 2).astype(jnp.float32)[None, :]
    angles = position * 10000.0 ** (-2.0 * freq_index / rot_dims)
    return (jnp.cos(angles), jnp.sin(angles))


def rotate(field_in, cosine, sine_table, rot_dims):
    rotated = field_in[..., :rot_dims]
    others = field_in[..., rot_dims:]
    pair_view = rotated.reshape(rotated.shape[:-1] + (rot_dims // 2, 2))
    first_half = pair_view[..., 0]
    second_half = pair_view[..., 1]
    cos_table = cosine[:, None, :]
    sin_table = sine_table[:, None, :]
    new_first = first_half * cos_table - second_half * sin_table
    new_second = second_half * cos_table + first_half * sin_table
    joined = jnp.stack([new_first, new_second], axis=-1).reshape(rotated.shape)
    return jnp.concatenate([joined, others], axis=-1)


def causal_mask(first_row, block_rows, last_row, length):
    query_pos = first_row + jnp.arange(block_rows)[:, None]
    key_pos = jnp.arange(last_row)[None, :]
    return (key_pos <= query_pos) & (key_pos < length)


def block_scores(queries, key_rows, first_row, last_row, length):
    score_scale = HEAD_DIM ** (-0.5)
    scores = (
        jnp.einsum(
            "qhd,khd->hqk",
            queries[first_row:last_row],
            key_rows[:last_row],
            preferred_element_type=jnp.float32,
        )
        * score_scale
    )
    allowed = causal_mask(first_row, last_row - first_row, last_row, length)
    return jnp.where(allowed[None], scores, -1e30)


def attend_forward(queries, key_rows, values, length, block_rows):
    seq_len = queries.shape[0]
    queries = queries.reshape(seq_len, -1, HEAD_DIM)
    key_rows = key_rows.reshape(seq_len, -1, HEAD_DIM)
    values = values.reshape(seq_len, -1, HEAD_DIM)
    outputs = []
    lse_parts = []
    for first_row in range(0, seq_len, block_rows):
        last_row = first_row + block_rows
        scores = block_scores(queries, key_rows, first_row, last_row, length)
        row_max = jnp.max(scores, axis=-1, keepdims=True)
        exp_scores = jnp.exp(scores - row_max)
        row_total = jnp.sum(exp_scores, axis=-1, keepdims=True)
        probs_low = (exp_scores / row_total).astype(jnp.bfloat16)
        outputs.append(
            jnp.einsum(
                "hqk,khd->qhd", probs_low, values[:last_row], preferred_element_type=jnp.float32
            )
        )
        lse_parts.append((row_max + jnp.log(row_total))[..., 0])
    return (
        jnp.concatenate(outputs, axis=0).reshape(seq_len, -1),
        jnp.concatenate(lse_parts, axis=1),
    )


def attend_backward(queries, key_rows, values, grad_att, lse_rows, length, block_rows):
    seq_len = queries.shape[0]
    score_scale = HEAD_DIM ** (-0.5)
    queries = queries.reshape(seq_len, -1, HEAD_DIM)
    key_rows = key_rows.reshape(seq_len, -1, HEAD_DIM)
    values = values.reshape(seq_len, -1, HEAD_DIM)
    grad_att = grad_att.reshape(seq_len, -1, HEAD_DIM)
    key_grads = jnp.zeros(key_rows.shape, jnp.float32)
    value_grads = jnp.zeros(values.shape, jnp.float32)
    query_grads = []
    for first_row in range(0, seq_len, block_rows):
        last_row = first_row + block_rows
        scores = block_scores(queries, key_rows, first_row, last_row, length)
        probs = jnp.exp(scores - lse_rows[:, first_row:last_row, None])
        probs_low = probs.astype(jnp.bfloat16)
        grad_block = grad_att[first_row:last_row]
        grad_probs = jnp.einsum(
            "qhd,khd->hqk", grad_block, values[:last_row], preferred_element_type=jnp.float32
        )
        row_inner = jnp.sum(probs * grad_probs, axis=-1, keepdims=True)
        grad_scores = (probs * (grad_probs - row_inner)).astype(jnp.bfloat16)
        query_grads.append(
            jnp.einsum(
                "hqk,khd->qhd", grad_scores, key_rows[:last_row], preferred_element_type=jnp.float32
            )
            * score_scale
        )
        key_grads = key_grads.at[:last_row].add(
            jnp.einsum(
                "hqk,qhd->khd",
                grad_scores,
                queries[first_row:last_row],
                preferred_element_type=jnp.float32,
            )
            * score_scale
        )
        value_grads = value_grads.at[:last_row].add(
            jnp.einsum("hqk,qhd->khd", probs_low, grad_block, preferred_element_type=jnp.float32)
        )
    return (jnp.concatenate(query_grads, axis=0), key_grads, value_grads)


def on_device(
    inputs, cotangent, lengths, ln_gain, ln_bias, w_qkv, w_out, w_in, b_in, w_down, b_down
):
    groups = lax.axis_size("wide")
    narrow_size = lax.axis_size("narrow")
    column = lax.axis_index("narrow")
    seq_count = 2 * lengths.shape[0]
    rows_all = inputs.shape[0]
    pad_len = rows_all // seq_count
    model_width = w_qkv.shape[0]
    share_cols = model_width // narrow_size
    block_rows = min(512, pad_len)
    col_start = column * share_cols
    token_count = 2.0 * jnp.sum(lengths.astype(jnp.float32))
    token_sum = lax.psum(token_count, "wide")
    group_scale = groups * token_count / token_sum
    full_x, full_cot = (
        lax.all_gather(inputs, "narrow", axis=1, tiled=True),
        lax.all_gather(cotangent, "narrow", axis=1, tiled=True),
    )
    seq_lengths = jnp.repeat(lengths, 2)
    valid_rows = (
        (jnp.arange(pad_len)[None, :] < seq_lengths[:, None])
        .astype(jnp.float32)
        .reshape(rows_all, 1)
    )
    x_full = full_x.astype(jnp.float32)
    row_mean = jnp.mean(x_full, axis=-1, keepdims=True)
    centered = x_full - row_mean
    inv_std = lax.rsqrt(jnp.mean(centered * centered, axis=-1, keepdims=True) + norm_eps)
    x_hat = centered * inv_std
    hidden = (x_hat * ln_gain + ln_bias).astype(jnp.bfloat16)
    qkv_proj = jnp.dot(hidden, w_qkv, preferred_element_type=jnp.float32)
    qkv_proj = qkv_proj.reshape(seq_count, pad_len, 3, -1, HEAD_DIM)
    cosine, sine_table = rotary_tables(pad_len, ROT)
    q_seq = (
        rotate(qkv_proj[:, :, 0], cosine, sine_table, ROT)
        .astype(jnp.bfloat16)
        .reshape(seq_count, pad_len, -1)
    )
    k_seq = (
        rotate(qkv_proj[:, :, 1], cosine, sine_table, ROT)
        .astype(jnp.bfloat16)
        .reshape(seq_count, pad_len, -1)
    )
    v_seq = qkv_proj[:, :, 2].astype(jnp.bfloat16).reshape(seq_count, pad_len, -1)
    att_width = q_seq.shape[2]
    up_proj = jnp.dot(hidden, w_in, preferred_element_type=jnp.float32) + b_in
    activation = gelu_tanh(up_proj).astype(jnp.bfloat16)
    mlp_part = jnp.dot(activation, w_down, preferred_element_type=jnp.float32)

    def forward_one(packed):
        return attend_forward(packed[0], packed[1], packed[2], packed[3], block_rows)

    att_rows, lse_all = lax.map(forward_one, (q_seq, k_seq, v_seq, seq_lengths))
    attended = att_rows.astype(jnp.bfloat16).reshape(rows_all, att_width)
    branch_share = lax.psum_scatter(
        mlp_part.astype(jnp.bfloat16), "narrow", scatter_dimension=1, tiled=True
    ).astype(jnp.float32)
    w_out_cols = lax.dynamic_slice_in_dim(w_out, col_start, share_cols, 1)
    attn_share = jnp.dot(attended, w_out_cols, preferred_element_type=jnp.float32)
    mixed = (inputs.astype(jnp.float32) + (attn_share + (branch_share + b_down))).astype(
        jnp.bfloat16
    )
    grad_share = group_scale * valid_rows * cotangent.astype(jnp.float32)
    grad_share_low = grad_share.astype(jnp.bfloat16)
    grad_low = (group_scale * valid_rows * full_cot.astype(jnp.float32)).astype(jnp.bfloat16)
    g_b_down = jnp.sum(grad_share_low.astype(jnp.float32), axis=0)
    g_w_down = jnp.einsum("rf,rd->fd", activation, grad_low, preferred_element_type=jnp.float32)
    g_act = jnp.dot(grad_low, w_down.T, preferred_element_type=jnp.float32)
    gelu_value, gelu_pull = jax.vjp(gelu_tanh, up_proj)
    g_up = gelu_pull(g_act)[0].astype(jnp.bfloat16)
    g_b_in = jnp.sum(g_up.astype(jnp.float32), axis=0)
    g_w_in = jnp.einsum("rd,rf->df", hidden, g_up, preferred_element_type=jnp.float32)
    g_hidden_mlp = jnp.dot(g_up, w_in.T, preferred_element_type=jnp.float32)
    g_w_out_rows = jnp.einsum("rd,re->de", attended, grad_low, preferred_element_type=jnp.float32)
    g_att = jnp.dot(grad_low, w_out.T, preferred_element_type=jnp.float32).astype(jnp.bfloat16)

    def backward_one(packed):
        return attend_backward(
            packed[0], packed[1], packed[2], packed[3], packed[4], packed[5], block_rows
        )

    g_qrot, g_krot, g_val = lax.map(
        backward_one,
        (q_seq, k_seq, v_seq, g_att.reshape(seq_count, pad_len, att_width), lse_all, seq_lengths),
    )
    g_query = rotate(g_qrot, cosine, -sine_table, ROT)
    g_key = rotate(g_krot, cosine, -sine_table, ROT)
    g_qkv = (
        jnp.stack([g_query, g_key, g_val], axis=2)
        .reshape(rows_all, 3 * att_width)
        .astype(jnp.bfloat16)
    )
    g_w_qkv = jnp.einsum("rd,rc->dc", hidden, g_qkv, preferred_element_type=jnp.float32)
    g_hidden_attn = jnp.dot(g_qkv, w_qkv.T, preferred_element_type=jnp.float32)
    g_hidden = g_hidden_attn + lax.psum(g_hidden_mlp.astype(jnp.bfloat16), "narrow").astype(
        jnp.float32
    )
    d_hat = g_hidden * ln_gain
    g_x_full = inv_std * (
        d_hat
        - jnp.mean(d_hat, axis=-1, keepdims=True)
        - x_hat * jnp.mean(d_hat * x_hat, axis=-1, keepdims=True)
    )
    g_x_share = lax.dynamic_slice_in_dim(g_x_full, col_start, share_cols, 1)
    g_gain = lax.dynamic_slice_in_dim(jnp.sum(g_hidden * x_hat, axis=0), col_start, share_cols, 0)
    g_bias = lax.dynamic_slice_in_dim(jnp.sum(g_hidden, axis=0), col_start, share_cols, 0)
    g_inputs = grad_share + g_x_share
    qkv_three = g_w_qkv.reshape(model_width, 3, att_width)
    summed = (
        lax.psum_scatter(qkv_three, "wide", scatter_dimension=0, tiled=True),
        lax.psum_scatter(g_w_out_rows, "wide", scatter_dimension=1, tiled=True),
        lax.psum_scatter(g_w_in, "wide", scatter_dimension=0, tiled=True),
        lax.psum_scatter(g_w_down, "wide", scatter_dimension=1, tiled=True),
    )
    g_qkv_part = lax.dynamic_slice_in_dim(summed[0], col_start, share_cols, 2)
    g_out_part = lax.dynamic_slice_in_dim(summed[1], col_start, share_cols, 0)
    small = lax.psum((g_gain, g_bias, g_b_in, g_b_down), "wide")
    return (
        mixed,
        g_inputs,
        small[0],
        small[1],
        g_qkv_part,
        g_out_part,
        summed[2],
        small[2],
        summed[3],
        small[3],
    )


LOG2E = 1.4426950408889634


def inside(value):
    return pltpu.with_memory_space_constraint(value, pltpu.VMEM)


def outside(value):
    return pltpu.with_memory_space_constraint(value, pltpu.HBM)


def mm(left, right, dims=NN):
    return lax.dot_general(left, right, dims, preferred_element_type=F32)


COST_SCALE = 0.1


def cost(micros):
    return pl.CostEstimate(flops=int(COST_SCALE * micros * 1e9), bytes_accessed=1000000, transcendentals=0)


def load_kernel(place, w_qkv, w_out, w_in, w_down, cosine, sine, *refs):
    outs, sems = refs[:-1], refs[-1]
    share = outs[0].shape[1]
    own = place[0]
    sources = [w_qkv.at[:, pl.ds(pl.multiple_of((4 * j + own) * share, 128), share)] for j in range(3)]
    sources += [w_out.at[pl.ds(pl.multiple_of(own * share, 128), share), :], w_in, w_down, cosine, sine]
    copies = [pltpu.make_async_copy(src, dst, sems.at[k]) for k, (src, dst) in enumerate(zip(sources, outs))]
    for copy in copies:
        copy.start()
    for copy in copies:
        copy.wait()


def load_weights(place, w_qkv, w_out, w_in, w_down, cosine, sine):
    width = w_qkv.shape[0]
    share = width // 4
    shapes = [(width, share)] * 3 + [(share, width), w_in.shape, w_down.shape]
    any_place = pl.BlockSpec(memory_space=pl.ANY)
    return pl.pallas_call(
        load_kernel,
        in_specs=[pl.BlockSpec(memory_space=pltpu.SMEM)] + [any_place] * 6,
        out_specs=[any_place] * 8,
        out_shape=[pltpu.VMEM(shape, BF) for shape in shapes] + [pltpu.VMEM(cosine.shape, F32)] * 2,
        scratch_shapes=[pltpu.SemaphoreType.DMA((8,))],
        compiler_params=pltpu.CompilerParams(vmem_limit_bytes=VMEM_BYTES),
        cost_estimate=cost(3),
        name="load_weights",
    )(place, *[outside(value) for value in (w_qkv, w_out, w_in, w_down, cosine, sine)])


def norm_mlp_kernel(place, x0, x1, x2, x3, c0, c1, c2, c3, gain, bias, w_in, b_in, w_down, *refs, first_row):
    left, right, stats, sum_up, sum_grad = refs[-5:]
    step = pl.program_id(0)
    rows, cols = x0.shape
    width, units = w_in.shape
    own = place[0]
    xs = [ref[...].astype(F32) for ref in (x0, x1, x2, x3)]
    mean = jnp.sum(xs[0] + xs[1] + xs[2] + xs[3], axis=1, keepdims=True) * (1.0 / width)
    cs = [x - mean for x in xs]
    squares = cs[0] * cs[0] + cs[1] * cs[1] + cs[2] * cs[2] + cs[3] * cs[3]
    inv_std = lax.rsqrt(jnp.sum(squares, axis=1, keepdims=True) * (1.0 / width) + norm_eps)
    row = first_row + step * rows + lax.broadcasted_iota(jnp.int32, (rows, 1), 0)
    for j, (centered, cot) in enumerate(zip(cs, (c0, c1, c2, c3))):
        here = pl.ds(pl.multiple_of((own ^ j) * cols, cols), cols)
        left[0, :, here] = (centered * inv_std * gain[:, here] + bias[:, here]).astype(BF)
        low = jnp.where(row < place[1], cot[...], jnp.zeros_like(cot))
        left[1, :, here] = low
        if j == 0:
            sum_grad[...] = jnp.sum(low.astype(F32).reshape(rows // 8, 8, cols), axis=0)
    lane = lax.broadcasted_iota(jnp.int32, (rows, 128), 1)
    stats[...] = jnp.where(lane == 0, mean, inv_std)
    h = left[0]
    g = left[1]
    part = min(512, units)
    for first in range(0, units, part):
        here = pl.ds(first, part)
        up = mm(h, w_in[:, here]) + b_in[:, here]
        g_act = mm(g, w_down[here, :], NT)
        square = up * up
        tanh = jnp.tanh(up * (GELU_A + GELU_A * GELU_B * square))
        half = 0.5 * up
        plus = 1.0 + tanh
        slope = 0.5 * plus + (half * (1.0 - tanh * tanh)) * (GELU_A + 3.0 * GELU_A * GELU_B * square)
        g_up = slope * g_act
        right[0, :, here] = g_up.astype(BF)
        right[1, :, here] = (half * plus).astype(BF)
        sum_up[:, here] = jnp.sum(g_up.reshape(rows // 8, 8, part), axis=0)


def norm_mlp(place, near, far, gain, bias, w_in, b_in, w_down, start_row, first_row, total, before=None):
    rows, cols = far[0].shape
    rows //= 2
    width, units = w_in.shape
    tile = min(256, rows)
    tiles = rows // tile
    offset = first_row // tile
    begin = start_row // tile

    def part(j):
        return [pl.BlockSpec((tile, cols), lambda i: (i + begin, 0))] * 2 + [pl.BlockSpec((tile, cols), lambda i: (i + j * tiles, 0))] * 2

    def rowed(size):
        return pl.BlockSpec((tile, size), lambda i: (i + offset, 0))

    def paired(size):
        return pl.BlockSpec((2, tile, size), lambda i: (0, i + offset, 0))

    def eight(size):
        return pl.BlockSpec((8, size), lambda i: (i + offset, 0))

    def whole(shape):
        return pl.BlockSpec(memory_space=pltpu.VMEM)

    shape = jax.ShapeDtypeStruct
    outs = [pltpu.VMEM((2, total, width), BF), pltpu.VMEM((2, total, units), BF), shape((total, 128), F32),
            shape((total // tile * 8, units), F32), shape((total // tile * 8, cols), F32)]
    before = [] if before is None else [inside(before[0]), inside(before[1]), *before[2:]]
    return pl.pallas_call(
        functools.partial(norm_mlp_kernel, first_row=first_row),
        grid=(tiles,),
        in_specs=[pl.BlockSpec(memory_space=pltpu.SMEM)]
        + part(0) + part(1)
        + [whole((1, width)), whole((1, width)), whole((width, units)), whole((1, units)), whole((units, width))]
        + [pl.BlockSpec(memory_space=pl.ANY)] * len(before),
        out_specs=[paired(width), paired(units), rowed(128), eight(units), eight(cols)],
        out_shape=outs,
        input_output_aliases={14 + k: k for k in range(len(before))},
        compiler_params=pltpu.CompilerParams(vmem_limit_bytes=VMEM_BYTES),
        cost_estimate=cost(0.010 * rows),
        name="norm_mlp",
    )(place, near[0], near[1], *far, near[2], near[3], *far, gain, bias, inside(w_in), b_in, inside(w_down), *before)


def turn(field, cosine, sine):
    lane = lax.broadcasted_iota(jnp.int32, field.shape, 1)
    size = field.shape[1]
    other = jnp.where(lane % 2 == 0, pltpu.roll(field, size - 1, 1), pltpu.roll(field, 1, 1))
    return field * cosine + other * sine


def attend_kernel(
    place, left, w_q, w_k, w_v, w_o, cosine, sine, cos_all, sin_all, attended, g_qkv,
    k_aug, k_t, v_nat, v_t, q_nat, q_aug, d_out, gk_acc, gv_acc, *, tiles, tile, pairs,
):
    step = pl.program_id(0)
    length = place[1]
    share = 128 * pairs

    @pl.when(step < tiles)
    def project():
        h = left[0]
        cos = cosine[...]
        sin = sine[...]
        q_all = mm(h, w_q[...])
        k_all = mm(h, w_k[...])
        v_all = mm(h, w_v[...])
        g_all = mm(left[1], w_o[...], NT)
        start = pl.multiple_of(step * tile, tile)
        here = pl.ds(start, tile)
        lane = lax.broadcasted_iota(jnp.int32, (tile, 128), 1)
        key_row = start + lax.broadcasted_iota(jnp.int32, (tile, 128), 0)
        closed = jnp.where(key_row < length, 0.0, -1e30)
        first = lane < HEAD_DIM
        sub = lax.broadcasted_iota(jnp.int32, (128, tile), 0)
        for p in range(pairs):
            cut = slice(128 * p, 128 * (p + 1))
            q = turn(q_all[:, cut], cos, sin) * HEAD_DIM ** (-0.5)
            k = turn(k_all[:, cut], cos, sin)
            v = v_all[:, cut]
            q_nat[p, here, :] = q.astype(BF)
            v_nat[p, here, :] = v.astype(BF)
            k_aug[2 * p, here, :] = jnp.where(first, k, jnp.where(lane == HEAD_DIM, closed, 0.0)).astype(BF)
            k_aug[2 * p + 1, here, :] = jnp.where(first, jnp.where(lane == 0, closed, 0.0), k).astype(BF)
            q_t = q.T
            q_aug[2 * p, :, here] = jnp.where(sub < HEAD_DIM, q_t, jnp.where(sub == HEAD_DIM, 1.0, 0.0)).astype(BF)
            q_aug[2 * p + 1, :, here] = jnp.where(sub < HEAD_DIM, jnp.where(sub == 0, 1.0, 0.0), q_t).astype(BF)
            k_t[p, :, here] = k.T.astype(BF)
            v_t[p, :, here] = v.T.astype(BF)
            d_out[p, :, here] = g_all[:, cut].T

    @pl.when(step >= tiles)
    def attend():
        p = step - tiles
        lane = lax.broadcasted_iota(jnp.int32, (tile, 128), 1)
        later = lax.broadcasted_iota(jnp.int32, (tile, tile), 0) > lax.broadcasted_iota(jnp.int32, (tile, tile), 1)
        heads = range(2)
        mine = [lane < HEAD_DIM, lane >= HEAD_DIM]
        cuts = [slice(0, HEAD_DIM), slice(HEAD_DIM, 2 * HEAD_DIM)]

        def cut_of(j):
            return pl.ds(pl.multiple_of(j * share + p * 128, 128), 128)

        def score(i):
            n = (i + 1) * tile
            return [mm(k_aug[2 * p + h, :n, :], q_aug[2 * p + h, :, i * tile : n]) for h in heads]

        for i in range(tiles):
            n = (i + 1) * tile
            here = slice(i * tile, n)
            old = slice(0, i * tile)
            scores = ahead if i else score(0)
            weights, inverses = [], []
            for h in heads:
                s = scores[h]
                tail = jnp.where(later, -1e30, s[n - tile :])
                s = tail if i == 0 else jnp.concatenate([s[: n - tile], tail], axis=0)
                e = jnp.exp(s - jnp.max(s, axis=0, keepdims=True))
                inverses.append(1.0 / jnp.sum(e, axis=0, keepdims=True))
                weights.append(e)
            lows = [e.astype(BF) for e in weights]
            outs = [mm(v_t[p, cuts[h], :n], lows[h]) * inverses[h] for h in heads]
            scaled, inner = [], []
            for h in heads:
                d = d_out[p, cuts[h], here]
                inner.append(jnp.sum(d * outs[h], axis=0, keepdims=True) * inverses[h])
                scaled.append(d * inverses[h])
            g_scores = []
            for h in heads:
                zero = jnp.zeros((HEAD_DIM, tile), BF)
                d_t = scaled[h].astype(BF)
                d_t = jnp.concatenate([d_t, zero] if h == 0 else [zero, d_t], axis=0)
                g_scores.append((weights[h] * (mm(v_nat[p, :n, :], d_t) - inner[h])).astype(BF))
            if i + 1 < tiles:
                ahead = score(i + 1)
            attended[here, cut_of(0)] = jnp.concatenate(outs, axis=0).T.astype(BF)
            d_nat = jnp.concatenate(scaled, axis=0).T
            q_here = q_nat[p, here, :]
            g_q = jnp.concatenate([mm(k_t[p, cuts[h], :n], g_scores[h]) for h in heads], axis=0).T * HEAD_DIM ** (-0.5)
            g_qkv[here, cut_of(0)] = turn(g_q, cos_all[here, :], -sin_all[here, :]).astype(BF)
            add_v = sum(mm(lows[h], jnp.where(mine[h], d_nat, 0.0).astype(BF)) for h in heads)
            add_k = sum(mm(g_scores[h], jnp.where(mine[h], q_here, jnp.zeros_like(q_here))) for h in heads)
            if i > 0:
                gv_acc[old] += add_v[: n - tile]
                gk_acc[old] += add_k[: n - tile]
            gv_acc[here] = add_v[n - tile :]
            gk_acc[here] = add_k[n - tile :]
        g_qkv[:, cut_of(1)] = turn(gk_acc[...], cos_all[...], -sin_all[...]).astype(BF)
        g_qkv[:, cut_of(2)] = gv_acc[...].astype(BF)


def attend(place, left, weights):
    _, rows, width = left.shape
    share = width // 4
    pairs = share // 128
    tile = min(256, rows)
    tiles = rows // tile

    def early(i, _):
        return (jnp.minimum(i, tiles - 1), 0)

    def whole(shape):
        return pl.BlockSpec(shape, lambda i, _: (0, 0), pipeline_mode=pl.Buffered(1))

    w_q, w_k, w_v, w_o, _, _, cosine, sine = [inside(value) for value in weights]
    return pl.pallas_call(
        functools.partial(attend_kernel, tiles=tiles, tile=tile, pairs=pairs),
        grid_spec=pltpu.PrefetchScalarGridSpec(
            num_scalar_prefetch=1,
            grid=(tiles + pairs,),
            in_specs=[
                pl.BlockSpec((2, tile, width), lambda i, _: (0, jnp.minimum(i, tiles - 1), 0)),
                whole(w_q.shape), whole(w_k.shape), whole(w_v.shape), whole(w_o.shape),
                pl.BlockSpec((tile, 128), early),
                pl.BlockSpec((tile, 128), early),
                whole((rows, 128)), whole((rows, 128)),
            ],
            out_specs=[whole((rows, share)), whole((rows, 3 * share))],
            scratch_shapes=[
                pltpu.VMEM((2 * pairs, rows, 128), BF),
                pltpu.VMEM((pairs, 128, rows), BF),
                pltpu.VMEM((pairs, rows, 128), BF),
                pltpu.VMEM((pairs, 128, rows), BF),
                pltpu.VMEM((pairs, rows, 128), BF),
                pltpu.VMEM((2 * pairs, 128, rows), BF),
                pltpu.VMEM((pairs, 128, rows), F32),
                pltpu.VMEM((rows, 128), F32),
                pltpu.VMEM((rows, 128), F32),
            ],
        ),
        out_shape=[pltpu.VMEM((rows, share), BF), pltpu.VMEM((rows, 3 * share), BF)],
        compiler_params=pltpu.CompilerParams(vmem_limit_bytes=VMEM_BYTES),
        cost_estimate=cost(0.014 * rows),
        name="attend",
    )(place, inside(left), w_q, w_k, w_v, w_o, cosine, sine, cosine, sine)


def weight_mlp_kernel(place, scale, left_0, left_1, right_0, right_1, keep, send):
    total = (scale[0] * (mm(left_0[0], right_0[0], TN) + mm(left_1[0], right_1[0], TN))).astype(BF)
    half = total.shape[0] // 2
    odd = place[2] == 1
    keep[0] = jnp.where(odd, total[half:], total[:half])
    send[0] = jnp.where(odd, total[:half], total[half:])


def weight_att_kernel(place, scale, left_0, left_1, qkv_0, qkv_1, att_0, att_1, keep, send):
    odd = place[2] == 1
    size = qkv_0.shape[1]
    first = (scale[0] * (mm(left_0[0], qkv_0[...], TN) + mm(left_1[0], qkv_1[...], TN))).astype(BF)
    second = (scale[0] * (mm(left_0[1], att_0[...], TN) + mm(left_1[1], att_1[...], TN))).astype(BF)
    half = first.shape[0] // 2
    keep[0, :, :size] = jnp.where(odd, first[half:], first[:half])
    send[0, :, :size] = jnp.where(odd, first[:half], first[half:])
    keep[0, :, size:] = jnp.where(odd, second[half:], second[:half])
    send[0, :, size:] = jnp.where(odd, second[:half], second[half:])


def weight_hold_kernel(place, scale, left_0, left_1, right_0, right_1, hold, ship):
    total = (scale[0] * (mm(left_0[0], right_0[0], TN) + mm(left_1[0], right_1[0], TN))).astype(BF)
    half = total.shape[0] // 2
    odd = place[2] == 1
    mine = jnp.where(odd, total[half:], total[:half])
    other = jnp.where(odd, total[:half], total[half:])

    @pl.when(pl.program_id(0) < 2)
    def near():
        hold[0, 0] = mine
        hold[0, 1] = other

    @pl.when(pl.program_id(0) >= 2)
    def far():
        ship[0, 0] = mine
        ship[0, 1] = other


def chip_of(slot, place):
    return (2 * (slot & 1) + (slot >> 1)) ^ place[3]


def weight_mlp(place, scale, lefts, rights, kind):
    _, rows, width = lefts[0].shape
    units = rights[0].shape[2]
    size = width // 8
    column = pl.BlockSpec((1, rows, 2 * size), lambda i, where: (kind, 0, chip_of(i, where)))
    whole = pl.BlockSpec((1, rows, units), lambda i, where: (kind, 0, 0), pipeline_mode=pl.Buffered(1))
    if kind == 0:
        kernel = weight_mlp_kernel
        slot = pl.BlockSpec((1, size, units), lambda i, where: (i, 0, 0))
        outs = [slot, slot]
        out = [pltpu.HBM((4, size, units), BF)] * 2
    else:
        kernel = weight_hold_kernel
        outs = [pl.BlockSpec((1, 2, size, units), lambda i, where: (jnp.minimum(i, 1), 0, 0, 0)),
                pl.BlockSpec((1, 2, size, units), lambda i, where: (jnp.maximum(i - 2, 0), 0, 0, 0))]
        out = [pltpu.HBM((2, 2, size, units), BF)] * 2
    return pl.pallas_call(
        kernel,
        grid_spec=pltpu.PrefetchScalarGridSpec(
            num_scalar_prefetch=1, grid=(4,),
            in_specs=[pl.BlockSpec(memory_space=pltpu.SMEM), column, column, whole, whole], out_specs=outs,
        ),
        out_shape=out,
        compiler_params=pltpu.CompilerParams(vmem_limit_bytes=VMEM_BYTES),
        cost_estimate=cost(0.0065 * rows),
        name="weight_mlp",
    )(place, scale, *[inside(value) for value in (*lefts, *rights)])


def weight_att(place, scale, lefts, qkvs, atts):
    _, rows, width = lefts[0].shape
    units = qkvs[0].shape[1] + atts[0].shape[1]
    size = width // 8
    column = pl.BlockSpec((2, rows, 2 * size), lambda i, where: (0, 0, chip_of(i, where)))

    def whole(ref):
        return pl.BlockSpec(ref.shape, lambda i, where: (0, 0), pipeline_mode=pl.Buffered(1))

    slot = pl.BlockSpec((1, size, units), lambda i, where: (i, 0, 0))
    out = pltpu.HBM((4, size, units), BF)
    return pl.pallas_call(
        weight_att_kernel,
        grid_spec=pltpu.PrefetchScalarGridSpec(
            num_scalar_prefetch=1, grid=(4,),
            in_specs=[pl.BlockSpec(memory_space=pltpu.SMEM), column, column] + [whole(r) for r in (*qkvs, *atts)],
            out_specs=[slot, slot],
        ),
        out_shape=[out, out],
        compiler_params=pltpu.CompilerParams(vmem_limit_bytes=VMEM_BYTES),
        cost_estimate=cost(0.007 * rows),
        name="weight_att",
    )(place, scale, *[inside(value) for value in (*lefts, *qkvs, *atts)])


def branch_kernel(place, left, right, att, g_qkv, w_q, w_k, w_v, w_o, w_in, w_down, gain, bias,
                  keep, near, far_b, far_g, sums, column_sums):
    own = place[0]
    rows, share = att.shape
    total = mm(right[1], w_down[...]) + mm(att[...], w_o[...])
    g_total = mm(right[0], w_in[...], NT)
    for j, w in enumerate((w_q, w_k, w_v)):
        g_total += mm(g_qkv[:, j * share : (j + 1) * share], w[...], NT)
    odd = (own & 1) == 1
    up = (own >> 1) == 1
    for kind, (whole, far) in enumerate(((total, far_b), (g_total, far_g))):
        cuts = [whole[:, j * share : (j + 1) * share].astype(BF) for j in range(4)]
        low = [jnp.where(odd, cuts[2 * y + 1], cuts[2 * y]) for y in range(2)]
        high = [jnp.where(odd, cuts[2 * y], cuts[2 * y + 1]) for y in range(2)]
        keep[0, kind] = jnp.where(up, low[1], low[0])
        keep[1, kind] = jnp.where(up, low[0], low[1])
        near[kind] = jnp.where(up, high[1], high[0])
        far[...] = jnp.where(up, high[0], high[1])
    turned = g_total * (left[0].astype(F32) - bias[...])
    mean_part = jnp.sum(g_total * gain[...], axis=1, keepdims=True)
    inner_part = jnp.sum(turned, axis=1, keepdims=True)
    lane = lax.broadcasted_iota(jnp.int32, (rows, 128), 1)
    sums[...] = jnp.where(lane == 0, mean_part, inner_part).T[:8, :]

    @pl.when(pl.program_id(0) == 0)
    def clear():
        column_sums[...] = jnp.zeros_like(column_sums)

    column_sums[0:1, :] += jnp.sum(g_total, axis=0, keepdims=True)
    column_sums[1:2, :] += jnp.sum(turned, axis=0, keepdims=True)


def branch_parts(place, left, right, att, g_qkv, weights, gain, bias, first_row, rows):
    _, _, width = left.shape
    units = right.shape[2]
    share = att.shape[1]
    tile = min(256, rows)
    tiles = rows // tile
    offset = first_row // tile

    def paired(k, size):
        return pl.BlockSpec((k, tile, size), lambda i, _: (0, i + offset, 0))

    def rowed(size):
        return pl.BlockSpec((tile, size), lambda i, _: (i + offset, 0))

    def whole(shape):
        return pl.BlockSpec(shape, lambda i, _: (0, 0), pipeline_mode=pl.Buffered(1))

    weights = [inside(value) for value in weights[:6]]
    shape = jax.ShapeDtypeStruct
    slots = pl.BlockSpec((2, 2, tile, share), lambda i, _: (0, 0, i, 0))
    sent = pl.BlockSpec((2, tile, share), lambda i, _: (0, i, 0))
    rowed_out = pl.BlockSpec((tile, share), lambda i, _: (i, 0))
    return pl.pallas_call(
        branch_kernel,
        grid_spec=pltpu.PrefetchScalarGridSpec(
            num_scalar_prefetch=1,
            grid=(tiles,),
            in_specs=[
                paired(1, width), paired(2, units), rowed(share), rowed(3 * share),
                *[whole(value.shape) for value in weights],
                whole((1, width)), whole((1, width)),
            ],
            out_specs=[slots, sent, rowed_out, rowed_out, pl.BlockSpec((8, tile), lambda i, _: (0, i)), pl.BlockSpec((8, width), lambda i, _: (0, 0))],
        ),
        out_shape=[pltpu.HBM((2, 2, rows, share), BF)] + [pltpu.HBM((2, rows, share), BF)] + [pltpu.HBM((rows, share), BF)] * 2 + [shape((8, rows), F32),
                   shape((8, width), F32)],
        compiler_params=pltpu.CompilerParams(vmem_limit_bytes=VMEM_BYTES),
        cost_estimate=cost(0.010 * rows),
        name="branch_parts",
    )(place, inside(left), inside(right), inside(att), inside(g_qkv), *weights, gain, bias)


def combine_kernel(count, keep_in, x_in, hold, z_down, kept, core_b, core_g, z_in, low_in, zz_down, low_down, chip):
    size, units = keep_in.shape[1:]
    for k in range(2):
        z_in[k * size : (k + 1) * size] = keep_in[2 + k] + x_in[2 + k]
        low_in[k] = keep_in[k] + x_in[k]
        zz_down[k] = hold[1, k] + z_down[1, k]
        low_down[k] = hold[0, k] + z_down[0, k]
    rows = z_in.shape[0] - 2 * size
    row = lax.broadcasted_iota(jnp.int32, (rows, units), 0)
    value = jnp.full((rows, units), count[0], F32)
    high = value.astype(BF).astype(F32)
    z_in[2 * size :] = jnp.where(row == 0, high, jnp.where(row == 1, value - high, 0.0)).astype(BF)
    chip[0] = kept[1, 0] + core_b[...]
    chip[1] = kept[1, 1] + core_g[...]


def combine(count, keep_in, x_in, hold, z_down, kept, core):
    _, size, units = keep_in.shape
    _, _, rows, cols = kept.shape
    inner = pl.BlockSpec(memory_space=pltpu.VMEM)
    shapes = [(2 * size + 16, units), (2, size, units), (2, size, units), (2, size, units), (2, rows, cols)]
    return pl.pallas_call(
        combine_kernel,
        in_specs=[pl.BlockSpec(memory_space=pltpu.SMEM)] + [inner] * 7,
        out_specs=[inner] * 5,
        out_shape=[pltpu.HBM(shape, BF) for shape in shapes],
        compiler_params=pltpu.CompilerParams(vmem_limit_bytes=VMEM_BYTES),
        cost_estimate=cost(3),
        name="combine",
    )(count, *[outside(value) for value in (keep_in, x_in, hold, z_down, kept, *core)])


def final_kernel(place, scale, keep, near, far, x_ref, cot, stats, sums, gain, bias_down, *refs, first_row):
    mixed, g_x = refs[-2:]
    step = pl.program_id(0)
    rows, cols = x_ref.shape
    width = 4 * cols
    x = x_ref[...].astype(F32)
    branch = keep[0, 0].astype(F32) + near[0].astype(F32) + far[0].astype(F32)
    mixed[...] = (x + (branch + bias_down[...])).astype(BF)
    g = scale[0] * (keep[0, 1].astype(F32) + near[1].astype(F32) + far[1].astype(F32))
    inv_std = stats[:, 1:2]
    x_hat = (x - stats[:, 0:1]) * inv_std
    totals = (scale[0] / width) * jnp.concatenate([sums[...], jnp.zeros((126, rows), F32)], axis=0).T
    row = first_row + step * rows + lax.broadcasted_iota(jnp.int32, (rows, 1), 0)
    weight = jnp.where(row < place[1], scale[0], 0.0)
    g_out = weight * cot[...].astype(F32)
    g_x[...] = g_out + inv_std * (g * gain[...] - totals[:, 0:1] - x_hat * totals[:, 1:2])


def finish_rows(place, scale, keep, near, far, x, cot, stats, sums, gain, bias_down, sequence, first_row, before=None):
    _, rows, cols = far.shape
    tile = min(512, rows)
    tiles = rows // tile
    pad_len = stats.shape[0]
    begin = (sequence * pad_len + first_row) // tile
    inner = first_row // tile
    part = pl.BlockSpec((tile, cols), lambda i: (i + begin, 0))
    cored = pl.BlockSpec((1, tile, cols), lambda i: (0, i, 0))
    kept = pl.BlockSpec((1, 2, tile, cols), lambda i: (0, 0, i, 0))
    both = pl.BlockSpec((2, tile, cols), lambda i: (0, i, 0))
    flat = pl.BlockSpec((1, cols), lambda i: (0, 0))
    scalar = pl.BlockSpec(memory_space=pltpu.SMEM)
    shape = jax.ShapeDtypeStruct
    before = [] if before is None else list(before)
    return pl.pallas_call(
        functools.partial(final_kernel, first_row=first_row),
        grid=(tiles,),
        in_specs=[scalar, scalar, kept, both, both, part, part,
                  pl.BlockSpec((tile, 128), lambda i: (i + inner, 0)), pl.BlockSpec((2, tile), lambda i: (0, i + begin)), flat, flat]
        + [pl.BlockSpec(memory_space=pl.ANY)] * len(before),
        out_specs=[part, part],
        out_shape=[shape(x.shape, BF), shape(x.shape, F32)],
        input_output_aliases={11 + k: k for k in range(len(before))},
        compiler_params=pltpu.CompilerParams(vmem_limit_bytes=VMEM_BYTES),
        cost_estimate=cost(0.003 * rows),
        name="finish_rows",
    )(place, scale, *[outside(value) for value in (keep, near, far, x, cot, stats)], sums, gain, bias_down, *before)


def final_weight_kernel(factor, low_in, far_in, low_down, far_down, low_a, far_a, g_in, g_down, g_qkv, g_out):
    scale = factor[0]
    _, size, cols = g_qkv.shape
    g_in[...] = scale * (low_in[...].astype(F32) + far_in[:size].astype(F32))
    g_down[...] = (scale * (low_down[...].astype(F32) + far_down[...].astype(F32))).T
    for j in range(3):
        cut = slice(j * cols, (j + 1) * cols)
        g_qkv[j] = scale * (low_a[:, cut].astype(F32) + far_a[:size, cut].astype(F32))
    cut = slice(3 * cols, 4 * cols)
    g_out[...] = (scale * (low_a[:, cut].astype(F32) + far_a[:size, cut].astype(F32))).T


def finish_weights(factor, low_in, far_in, low_down, far_down, low_a, far_a):
    size, units = low_in.shape
    cols = low_a.shape[1] // 4
    shape = jax.ShapeDtypeStruct
    return pl.pallas_call(
        final_weight_kernel,
        in_specs=[pl.BlockSpec(memory_space=pltpu.SMEM)] + [pl.BlockSpec(memory_space=pltpu.VMEM)] * 6,
        out_specs=[pl.BlockSpec(memory_space=pltpu.VMEM)] * 4,
        out_shape=[shape((size, units), F32), shape((units, size), F32), shape((3, size, cols), F32), shape((cols, size), F32)],
        compiler_params=pltpu.CompilerParams(vmem_limit_bytes=VMEM_BYTES),
        cost_estimate=cost(3),
        name="finish_weights",
    )(factor, low_in, far_in, low_down, far_down, low_a, far_a)


def swap(value, axis, bit):
    size = lax.axis_size(axis)
    return lax.ppermute(value, axis, [(i, i ^ bit) for i in range(size)])


def sum_small(value, axis):
    bit = 1
    while bit < lax.axis_size(axis):
        value = value + swap(value, axis, bit)
        bit *= 2
    return value


def add_core(kept, core):
    return kept[1] + jnp.stack(core)


def pack(values, units):
    padded = jnp.concatenate([values, jnp.zeros((-values.shape[0] % units,), F32)]).reshape(-1, units)
    high = lax.reduce_precision(padded, 8, 7)
    rows = jnp.concatenate([high, padded - high], axis=0).astype(BF)
    return jnp.concatenate([rows, jnp.zeros((-rows.shape[0] % 16, units), BF)], axis=0)


def unpack(rows, count):
    part = -(-count // rows.shape[1])
    high, low = rows[:part].astype(F32), rows[part : 2 * part].astype(F32)
    return (high + low).reshape(-1)[:count]


def after(value, *others):
    return lax.optimization_barrier((value, *others))[0]


def on_device_fast(inputs, cotangent, lengths, ln_gain, ln_bias, w_qkv, w_out, w_in, b_in, w_down, b_down):
    groups = lax.axis_size("wide")
    column = lax.axis_index("narrow")
    place_wide = lax.axis_index("wide")
    rows_all, cols = inputs.shape
    pad_len = rows_all // 2
    width = w_qkv.shape[0]
    units = w_in.shape[1]
    place = jnp.stack([column, lengths[0], place_wide & 1, place_wide >> 1]).astype(jnp.int32)
    gain = ln_gain.reshape(1, width)
    bias = ln_bias.reshape(1, width)
    b_up = b_in.reshape(1, units)
    half = pad_len // 2
    cuts = ((0, half), (half, pad_len), (pad_len, rows_all))
    own_gain = lax.dynamic_slice_in_dim(ln_gain, column * cols, cols, 0).reshape(1, cols)
    b_row = b_down.reshape(1, cols)

    across = [swap(jnp.concatenate([inputs[low:high], cotangent[low:high]], axis=0), "narrow", 2) for low, high in cuts]
    near = (inputs, swap(inputs, "narrow", 1), cotangent, swap(cotangent, "narrow", 1))
    count = (2.0 * jnp.sum(lengths.astype(F32))).reshape(1)
    count_x = count + swap(count, "wide", 1)
    weights = load_weights(place, w_qkv, w_out, w_in, w_down, *turn_tables(pad_len))
    up_in, up_down = weights[4:6]

    def far(k, *earlier):
        rows = after(across[k], *earlier)
        return rows, swap(rows, "narrow", 1)

    def branch(place, mlp, att, first_row, rows):
        kept, near, far_b, far_g, sums, columns = branch_parts(
            place, mlp[0], mlp[1], *att, weights, gain, bias, first_row, rows)
        return kept, near, (far_b, far_g), sums, columns

    first = norm_mlp(place, near, far(0, weights[0], count_x), gain, bias, up_in, b_up, up_down, 0, 0, pad_len)
    place = after(place, first[3])
    mlp_0 = norm_mlp(place, near, far(1, first[3]), gain, bias, up_in, b_up, up_down, half, half, pad_len, first)
    place = after(place, mlp_0[3])
    att_0 = attend(place, mlp_0[0], weights)
    place = after(place, att_0[0])
    mlp_1 = norm_mlp(place, near, far(2, att_0[0]), gain, bias, up_in, b_up, up_down, pad_len, 0, pad_len)
    place = after(place, mlp_1[3])
    lefts = (mlp_0[0], mlp_1[0])
    rights = (mlp_0[1], mlp_1[1])
    keep_in, send_in = weight_mlp(place, count, lefts, rights, 0)
    place = after(place, keep_in)
    x_in = swap(send_in, "wide", 1)
    hold_down, ship_down = weight_mlp(place, count, lefts, rights, 1)
    place = after(place, hold_down)
    z_down = swap(ship_down, "wide", 2)
    kept_0, near_0, sent_0, sums_0, columns_0 = branch(place, mlp_0, att_0, 0, pad_len)
    core_0 = [swap(part, "narrow", 1) for part in sent_0]
    place = after(place, sums_0)
    att_1 = attend(place, mlp_1[0], weights)
    size = keep_in.shape[1]
    x_in, z_down, count_x, *core_0 = lax.optimization_barrier((x_in, z_down, count_x, *core_0, att_1[0]))[:5]
    z_in, low_in, zz_down, low_down, chip_0 = combine(count_x, keep_in, x_in, hold_down, z_down, kept_0, core_0)
    z_in = swap(z_in, "wide", 2)
    zz_down = swap(zz_down, "wide", 4)
    y_0 = swap(chip_0, "narrow", 2)
    near_0 = swap(after(near_0, chip_0), "narrow", 1)
    place = after(place, low_in, low_down, chip_0, att_1[0])
    keep_a, send_a = weight_att(place, count, lefts, (att_0[1], att_1[1]), (att_0[0], att_1[0]))
    x_a = swap(send_a, "wide", 1)
    place = after(place, keep_a, near_0)
    kept_1, near_1, sent_1, sums_1, columns_1 = branch(place, mlp_1, att_1, 0, pad_len)
    core_1 = [swap(part, "narrow", 1) for part in sent_1]
    z_in, zz_down, y_0, sums_0, columns_0 = lax.optimization_barrier((z_in, zz_down, y_0, sums_0, columns_0, sums_1))[:5]
    count_row = count_x + unpack(z_in[2 * size :], units)[:128]
    zz_in = swap(jnp.concatenate([low_in[1] + z_in[size : 2 * size], pack(jnp.broadcast_to(count_row[:1], (units,)), units)], axis=0), "wide", 4)
    low_in = low_in[0] + z_in[:size]
    x_d = swap(low_down[1] + zz_down[1], "wide", 1)
    low_down = low_down[0] + zz_down[0]
    sums = jnp.concatenate([sums_0[:2], sums_1[:2], columns_0[:2] + columns_1[:2]], axis=1)
    sums = after(sums, y_0)
    sums = sums + swap(sums, "narrow", 1)
    core_1 = [after(part, sums, low_down, low_in) for part in core_1]
    chip_1 = add_core(kept_1, core_1)
    y_1 = swap(chip_1, "narrow", 2)
    far_sums = swap(after(sums, chip_1), "narrow", 2)
    near_1 = swap(after(near_1, chip_1), "narrow", 1)
    x_a = after(x_a, chip_1)
    z_a = swap(keep_a[2:] + x_a[2:], "wide", 2)
    low_a = keep_a[:2] + x_a[:2]
    z_a = after(z_a, low_a)
    zz_a = swap(low_a[1] + z_a[1], "wide", 4)
    low_a = low_a[0] + z_a[0]
    y_1, far_sums, near_1, zz_in = lax.optimization_barrier((y_1, far_sums, near_1, zz_in, low_a))[:4]
    count_row = count_row + unpack(zz_in[size:], units)[:128]
    per_count = groups / count_row[:1]
    scale = count * per_count
    sums = sums + far_sums
    columns = lax.dynamic_slice_in_dim(sums[:, rows_all:], column * cols, cols, 1)
    sum_up, sum_down = [after(mlp_0[k], y_1) + mlp_1[k] for k in (3, 4)]
    small = count * jnp.concatenate([columns[1] / own_gain[0], columns[0], jnp.sum(sum_up, axis=0), jnp.sum(sum_down, axis=0)])
    small = small + swap(small, "wide", 1)
    ends = finish_rows(place, scale, kept_0, near_0, y_0, inputs, cotangent, mlp_0[2], sums, own_gain, b_row, 0, 0)
    small = small + swap(small, "wide", 2)
    ends = finish_rows(place, scale, kept_1, near_1, y_1, inputs, cotangent, mlp_1[2], sums, own_gain, b_row, 1, 0, ends)
    small = per_count * (small + swap(small, "wide", 4))
    zz_a, x_d = lax.optimization_barrier((zz_a, x_d, ends[0]))[:2]
    g_in, g_down, g_qkv, g_out = finish_weights(per_count, low_in, zz_in, low_down, x_d, low_a, zz_a)
    return (
        ends[0],
        ends[1],
        small[:cols],
        small[cols : 2 * cols],
        jnp.transpose(g_qkv, (1, 0, 2)),
        g_out,
        g_in,
        small[2 * cols : 2 * cols + units],
        g_down,
        small[2 * cols + units :],
    )


def turn_tables(length):
    position = np.arange(length, dtype=np.float32)[:, None]
    frequency = (10000.0 ** (-2.0 * np.arange(ROT // 2, dtype=np.float32) / ROT)).astype(np.float32)
    angles = (position * frequency[None, :]).astype(np.float32)
    cosine = np.ones((length, HEAD_DIM), np.float32)
    sine = np.zeros((length, HEAD_DIM), np.float32)
    cosine[:, :ROT] = np.repeat(np.cos(angles), 2, axis=1)
    sine[:, 0:ROT:2] = -np.sin(angles)
    sine[:, 1:ROT:2] = np.sin(angles)
    return jnp.asarray(np.tile(cosine, (1, 2))), jnp.asarray(np.tile(sine, (1, 2)))


def solution(mesh):
    placed = (
        P("wide", "narrow"),
        P("wide", "narrow"),
        P("wide"),
        P(),
        P(),
        P(),
        P(),
        P(None, "narrow"),
        P("narrow"),
        P("narrow", None),
        P("narrow"),
    )
    paired = mesh.shape["narrow"] == 4 and mesh.shape["wide"] == 8
    return jax.shard_map(
        on_device_fast if paired else on_device,
        mesh=mesh,
        in_specs=placed,
        out_specs=(
            P("wide", "narrow"),
            P("wide", "narrow"),
            P("narrow"),
            P("narrow"),
            P("wide", None, "narrow"),
            P("narrow", "wide"),
            P("wide", "narrow"),
            P("narrow"),
            P("narrow", "wide"),
            P("narrow"),
        ),
        check_vma=False,
    )
```

```python
import functools

import jax
import jax.numpy as jnp
import numpy as np
from jax import lax
from jax.experimental import pallas as pl
from jax.experimental.pallas import tpu as pltpu
from jax.sharding import PartitionSpec as P

HEAD_DIM = 64
ROT = 32
GELU_A = 0.7978845608028654
GELU_B = 0.044715
VMEM_BYTES = 24 * 1024 * 1024
F32 = jnp.float32
BF = jnp.bfloat16
NN = (((1,), (0,)), ((), ()))
NT = (((1,), (1,)), ((), ()))
TN = (((0,), (0,)), ((), ()))


norm_eps = 1e-05


def gelu_tanh(value_in):
    return (
        0.5
        * value_in
        * (
            1.0
            + jnp.tanh(0.7978845608028654 * (value_in + 0.044715 * value_in * value_in * value_in))
        )
    )


def rotary_tables(seq_len, rot_dims):
    position = jnp.arange(seq_len).astype(jnp.float32)[:, None]
    freq_index = jnp.arange(rot_dims // 2).astype(jnp.float32)[None, :]
    angles = position * 10000.0 ** (-2.0 * freq_index / rot_dims)
    return (jnp.cos(angles), jnp.sin(angles))


def rotate(field_in, cosine, sine_table, rot_dims):
    rotated = field_in[..., :rot_dims]
    others = field_in[..., rot_dims:]
    pair_view = rotated.reshape(rotated.shape[:-1] + (rot_dims // 2, 2))
    first_half = pair_view[..., 0]
    second_half = pair_view[..., 1]
    cos_table = cosine[:, None, :]
    sin_table = sine_table[:, None, :]
    new_first = first_half * cos_table - second_half * sin_table
    new_second = second_half * cos_table + first_half * sin_table
    joined = jnp.stack([new_first, new_second], axis=-1).reshape(rotated.shape)
    return jnp.concatenate([joined, others], axis=-1)


def causal_mask(first_row, block_rows, last_row, length):
    query_pos = first_row + jnp.arange(block_rows)[:, None]
    key_pos = jnp.arange(last_row)[None, :]
    return (key_pos <= query_pos) & (key_pos < length)


def block_scores(queries, key_rows, first_row, last_row, length):
    score_scale = HEAD_DIM ** (-0.5)
    scores = (
        jnp.einsum(
            "qhd,khd->hqk",
            queries[first_row:last_row],
            key_rows[:last_row],
            preferred_element_type=jnp.float32,
        )
        * score_scale
    )
    allowed = causal_mask(first_row, last_row - first_row, last_row, length)
    return jnp.where(allowed[None], scores, -1e30)


def attend_forward(queries, key_rows, values, length, block_rows):
    seq_len = queries.shape[0]
    queries = queries.reshape(seq_len, -1, HEAD_DIM)
    key_rows = key_rows.reshape(seq_len, -1, HEAD_DIM)
    values = values.reshape(seq_len, -1, HEAD_DIM)
    outputs = []
    lse_parts = []
    for first_row in range(0, seq_len, block_rows):
        last_row = first_row + block_rows
        scores = block_scores(queries, key_rows, first_row, last_row, length)
        row_max = jnp.max(scores, axis=-1, keepdims=True)
        exp_scores = jnp.exp(scores - row_max)
        row_total = jnp.sum(exp_scores, axis=-1, keepdims=True)
        probs_low = (exp_scores / row_total).astype(jnp.bfloat16)
        outputs.append(
            jnp.einsum(
                "hqk,khd->qhd", probs_low, values[:last_row], preferred_element_type=jnp.float32
            )
        )
        lse_parts.append((row_max + jnp.log(row_total))[..., 0])
    return (
        jnp.concatenate(outputs, axis=0).reshape(seq_len, -1),
        jnp.concatenate(lse_parts, axis=1),
    )


def attend_backward(queries, key_rows, values, grad_att, lse_rows, length, block_rows):
    seq_len = queries.shape[0]
    score_scale = HEAD_DIM ** (-0.5)
    queries = queries.reshape(seq_len, -1, HEAD_DIM)
    key_rows = key_rows.reshape(seq_len, -1, HEAD_DIM)
    values = values.reshape(seq_len, -1, HEAD_DIM)
    grad_att = grad_att.reshape(seq_len, -1, HEAD_DIM)
    key_grads = jnp.zeros(key_rows.shape, jnp.float32)
    value_grads = jnp.zeros(values.shape, jnp.float32)
    query_grads = []
    for first_row in range(0, seq_len, block_rows):
        last_row = first_row + block_rows
        scores = block_scores(queries, key_rows, first_row, last_row, length)
        probs = jnp.exp(scores - lse_rows[:, first_row:last_row, None])
        probs_low = probs.astype(jnp.bfloat16)
        grad_block = grad_att[first_row:last_row]
        grad_probs = jnp.einsum(
            "qhd,khd->hqk", grad_block, values[:last_row], preferred_element_type=jnp.float32
        )
        row_inner = jnp.sum(probs * grad_probs, axis=-1, keepdims=True)
        grad_scores = (probs * (grad_probs - row_inner)).astype(jnp.bfloat16)
        query_grads.append(
            jnp.einsum(
                "hqk,khd->qhd", grad_scores, key_rows[:last_row], preferred_element_type=jnp.float32
            )
            * score_scale
        )
        key_grads = key_grads.at[:last_row].add(
            jnp.einsum(
                "hqk,qhd->khd",
                grad_scores,
                queries[first_row:last_row],
                preferred_element_type=jnp.float32,
            )
            * score_scale
        )
        value_grads = value_grads.at[:last_row].add(
            jnp.einsum("hqk,qhd->khd", probs_low, grad_block, preferred_element_type=jnp.float32)
        )
    return (jnp.concatenate(query_grads, axis=0), key_grads, value_grads)


def on_device(
    inputs, cotangent, lengths, ln_gain, ln_bias, w_qkv, w_out, w_in, b_in, w_down, b_down
):
    groups = lax.axis_size("wide")
    narrow_size = lax.axis_size("narrow")
    column = lax.axis_index("narrow")
    seq_count = 2 * lengths.shape[0]
    rows_all = inputs.shape[0]
    pad_len = rows_all // seq_count
    model_width = w_qkv.shape[0]
    share_cols = model_width // narrow_size
    block_rows = min(512, pad_len)
    col_start = column * share_cols
    token_count = 2.0 * jnp.sum(lengths.astype(jnp.float32))
    token_sum = lax.psum(token_count, "wide")
    group_scale = groups * token_count / token_sum
    full_x, full_cot = (
        lax.all_gather(inputs, "narrow", axis=1, tiled=True),
        lax.all_gather(cotangent, "narrow", axis=1, tiled=True),
    )
    seq_lengths = jnp.repeat(lengths, 2)
    valid_rows = (
        (jnp.arange(pad_len)[None, :] < seq_lengths[:, None])
        .astype(jnp.float32)
        .reshape(rows_all, 1)
    )
    x_full = full_x.astype(jnp.float32)
    row_mean = jnp.mean(x_full, axis=-1, keepdims=True)
    centered = x_full - row_mean
    inv_std = lax.rsqrt(jnp.mean(centered * centered, axis=-1, keepdims=True) + norm_eps)
    x_hat = centered * inv_std
    hidden = (x_hat * ln_gain + ln_bias).astype(jnp.bfloat16)
    qkv_proj = jnp.dot(hidden, w_qkv, preferred_element_type=jnp.float32)
    qkv_proj = qkv_proj.reshape(seq_count, pad_len, 3, -1, HEAD_DIM)
    cosine, sine_table = rotary_tables(pad_len, ROT)
    q_seq = (
        rotate(qkv_proj[:, :, 0], cosine, sine_table, ROT)
        .astype(jnp.bfloat16)
        .reshape(seq_count, pad_len, -1)
    )
    k_seq = (
        rotate(qkv_proj[:, :, 1], cosine, sine_table, ROT)
        .astype(jnp.bfloat16)
        .reshape(seq_count, pad_len, -1)
    )
    v_seq = qkv_proj[:, :, 2].astype(jnp.bfloat16).reshape(seq_count, pad_len, -1)
    att_width = q_seq.shape[2]
    up_proj = jnp.dot(hidden, w_in, preferred_element_type=jnp.float32) + b_in
    activation = gelu_tanh(up_proj).astype(jnp.bfloat16)
    mlp_part = jnp.dot(activation, w_down, preferred_element_type=jnp.float32)

    def forward_one(packed):
        return attend_forward(packed[0], packed[1], packed[2], packed[3], block_rows)

    att_rows, lse_all = lax.map(forward_one, (q_seq, k_seq, v_seq, seq_lengths))
    attended = att_rows.astype(jnp.bfloat16).reshape(rows_all, att_width)
    branch_share = lax.psum_scatter(
        mlp_part.astype(jnp.bfloat16), "narrow", scatter_dimension=1, tiled=True
    ).astype(jnp.float32)
    w_out_cols = lax.dynamic_slice_in_dim(w_out, col_start, share_cols, 1)
    attn_share = jnp.dot(attended, w_out_cols, preferred_element_type=jnp.float32)
    mixed = (inputs.astype(jnp.float32) + (attn_share + (branch_share + b_down))).astype(
        jnp.bfloat16
    )
    grad_share = group_scale * valid_rows * cotangent.astype(jnp.float32)
    grad_share_low = grad_share.astype(jnp.bfloat16)
    grad_low = (group_scale * valid_rows * full_cot.astype(jnp.float32)).astype(jnp.bfloat16)
    g_b_down = jnp.sum(grad_share_low.astype(jnp.float32), axis=0)
    g_w_down = jnp.einsum("rf,rd->fd", activation, grad_low, preferred_element_type=jnp.float32)
    g_act = jnp.dot(grad_low, w_down.T, preferred_element_type=jnp.float32)
    gelu_value, gelu_pull = jax.vjp(gelu_tanh, up_proj)
    g_up = gelu_pull(g_act)[0].astype(jnp.bfloat16)
    g_b_in = jnp.sum(g_up.astype(jnp.float32), axis=0)
    g_w_in = jnp.einsum("rd,rf->df", hidden, g_up, preferred_element_type=jnp.float32)
    g_hidden_mlp = jnp.dot(g_up, w_in.T, preferred_element_type=jnp.float32)
    g_w_out_rows = jnp.einsum("rd,re->de", attended, grad_low, preferred_element_type=jnp.float32)
    g_att = jnp.dot(grad_low, w_out.T, preferred_element_type=jnp.float32).astype(jnp.bfloat16)

    def backward_one(packed):
        return attend_backward(
            packed[0], packed[1], packed[2], packed[3], packed[4], packed[5], block_rows
        )

    g_qrot, g_krot, g_val = lax.map(
        backward_one,
        (q_seq, k_seq, v_seq, g_att.reshape(seq_count, pad_len, att_width), lse_all, seq_lengths),
    )
    g_query = rotate(g_qrot, cosine, -sine_table, ROT)
    g_key = rotate(g_krot, cosine, -sine_table, ROT)
    g_qkv = (
        jnp.stack([g_query, g_key, g_val], axis=2)
        .reshape(rows_all, 3 * att_width)
        .astype(jnp.bfloat16)
    )
    g_w_qkv = jnp.einsum("rd,rc->dc", hidden, g_qkv, preferred_element_type=jnp.float32)
    g_hidden_attn = jnp.dot(g_qkv, w_qkv.T, preferred_element_type=jnp.float32)
    g_hidden = g_hidden_attn + lax.psum(g_hidden_mlp.astype(jnp.bfloat16), "narrow").astype(
        jnp.float32
    )
    d_hat = g_hidden * ln_gain
    g_x_full = inv_std * (
        d_hat
        - jnp.mean(d_hat, axis=-1, keepdims=True)
        - x_hat * jnp.mean(d_hat * x_hat, axis=-1, keepdims=True)
    )
    g_x_share = lax.dynamic_slice_in_dim(g_x_full, col_start, share_cols, 1)
    g_gain = lax.dynamic_slice_in_dim(jnp.sum(g_hidden * x_hat, axis=0), col_start, share_cols, 0)
    g_bias = lax.dynamic_slice_in_dim(jnp.sum(g_hidden, axis=0), col_start, share_cols, 0)
    g_inputs = grad_share + g_x_share
    qkv_three = g_w_qkv.reshape(model_width, 3, att_width)
    summed = (
        lax.psum_scatter(qkv_three, "wide", scatter_dimension=0, tiled=True),
        lax.psum_scatter(g_w_out_rows, "wide", scatter_dimension=1, tiled=True),
        lax.psum_scatter(g_w_in, "wide", scatter_dimension=0, tiled=True),
        lax.psum_scatter(g_w_down, "wide", scatter_dimension=1, tiled=True),
    )
    g_qkv_part = lax.dynamic_slice_in_dim(summed[0], col_start, share_cols, 2)
    g_out_part = lax.dynamic_slice_in_dim(summed[1], col_start, share_cols, 0)
    small = lax.psum((g_gain, g_bias, g_b_in, g_b_down), "wide")
    return (
        mixed,
        g_inputs,
        small[0],
        small[1],
        g_qkv_part,
        g_out_part,
        summed[2],
        small[2],
        summed[3],
        small[3],
    )


LOG2E = 1.4426950408889634


def inside(value):
    return pltpu.with_memory_space_constraint(value, pltpu.VMEM)


def outside(value):
    return pltpu.with_memory_space_constraint(value, pltpu.HBM)


def mm(left, right, dims=NN):
    return lax.dot_general(left, right, dims, preferred_element_type=F32)


COST_SCALE = 0.1


def cost(micros):
    return pl.CostEstimate(flops=int(COST_SCALE * micros * 1e9), bytes_accessed=1000000, transcendentals=0)


def load_kernel(place, w_qkv, w_out, w_in, w_down, cosine, sine, *refs):
    outs, sems = refs[:-1], refs[-1]
    share = outs[0].shape[1]
    own = place[0]
    sources = [w_qkv.at[:, pl.ds(pl.multiple_of((4 * j + own) * share, 128), share)] for j in range(3)]
    sources += [w_out.at[pl.ds(pl.multiple_of(own * share, 128), share), :], w_in, w_down, cosine, sine]
    copies = [pltpu.make_async_copy(src, dst, sems.at[k]) for k, (src, dst) in enumerate(zip(sources, outs))]
    for copy in copies:
        copy.start()
    for copy in copies:
        copy.wait()


def load_weights(place, w_qkv, w_out, w_in, w_down, cosine, sine):
    width = w_qkv.shape[0]
    share = width // 4
    shapes = [(width, share)] * 3 + [(share, width), w_in.shape, w_down.shape]
    any_place = pl.BlockSpec(memory_space=pl.ANY)
    return pl.pallas_call(
        load_kernel,
        in_specs=[pl.BlockSpec(memory_space=pltpu.SMEM)] + [any_place] * 6,
        out_specs=[any_place] * 8,
        out_shape=[pltpu.VMEM(shape, BF) for shape in shapes] + [pltpu.VMEM(cosine.shape, F32)] * 2,
        scratch_shapes=[pltpu.SemaphoreType.DMA((8,))],
        compiler_params=pltpu.CompilerParams(vmem_limit_bytes=VMEM_BYTES),
        cost_estimate=cost(3),
        name="load_weights",
    )(place, *[outside(value) for value in (w_qkv, w_out, w_in, w_down, cosine, sine)])


def norm_mlp_kernel(place, x0, x1, x2, x3, c0, c1, c2, c3, gain, bias, w_in, b_in, w_down, *refs, first_row):
    left, right, stats, sum_up, sum_grad = refs[-5:]
    step = pl.program_id(0)
    rows, cols = x0.shape
    width, units = w_in.shape
    own = place[0]
    xs = [ref[...].astype(F32) for ref in (x0, x1, x2, x3)]
    mean = jnp.sum(xs[0] + xs[1] + xs[2] + xs[3], axis=1, keepdims=True) * (1.0 / width)
    cs = [x - mean for x in xs]
    squares = cs[0] * cs[0] + cs[1] * cs[1] + cs[2] * cs[2] + cs[3] * cs[3]
    inv_std = lax.rsqrt(jnp.sum(squares, axis=1, keepdims=True) * (1.0 / width) + norm_eps)
    row = first_row + step * rows + lax.broadcasted_iota(jnp.int32, (rows, 1), 0)
    for j, (centered, cot) in enumerate(zip(cs, (c0, c1, c2, c3))):
        here = pl.ds(pl.multiple_of((own ^ j) * cols, cols), cols)
        left[0, :, here] = (centered * inv_std * gain[:, here] + bias[:, here]).astype(BF)
        low = jnp.where(row < place[1], cot[...], jnp.zeros_like(cot))
        left[1, :, here] = low
        if j == 0:
            sum_grad[...] = jnp.sum(low.astype(F32).reshape(rows // 8, 8, cols), axis=0)
    lane = lax.broadcasted_iota(jnp.int32, (rows, 128), 1)
    stats[...] = jnp.where(lane == 0, mean, inv_std)
    h = left[0]
    g = left[1]
    part = min(512, units)
    for first in range(0, units, part):
        here = pl.ds(first, part)
        up = mm(h, w_in[:, here]) + b_in[:, here]
        g_act = mm(g, w_down[here, :], NT)
        square = up * up
        tanh = jnp.tanh(up * (GELU_A + GELU_A * GELU_B * square))
        half = 0.5 * up
        plus = 1.0 + tanh
        slope = 0.5 * plus + (half * (1.0 - tanh * tanh)) * (GELU_A + 3.0 * GELU_A * GELU_B * square)
        g_up = slope * g_act
        right[0, :, here] = g_up.astype(BF)
        right[1, :, here] = (half * plus).astype(BF)
        sum_up[:, here] = jnp.sum(g_up.reshape(rows // 8, 8, part), axis=0)


def norm_mlp(place, near, far, gain, bias, w_in, b_in, w_down, start_row, first_row, total, before=None):
    rows, cols = far[0].shape
    rows //= 2
    width, units = w_in.shape
    tile = min(256, rows)
    tiles = rows // tile
    offset = first_row // tile
    begin = start_row // tile

    def part(j):
        return [pl.BlockSpec((tile, cols), lambda i: (i + begin, 0))] * 2 + [pl.BlockSpec((tile, cols), lambda i: (i + j * tiles, 0))] * 2

    def rowed(size):
        return pl.BlockSpec((tile, size), lambda i: (i + offset, 0))

    def paired(size):
        return pl.BlockSpec((2, tile, size), lambda i: (0, i + offset, 0))

    def eight(size):
        return pl.BlockSpec((8, size), lambda i: (i + offset, 0))

    def whole(shape):
        return pl.BlockSpec(memory_space=pltpu.VMEM)

    shape = jax.ShapeDtypeStruct
    outs = [pltpu.VMEM((2, total, width), BF), pltpu.VMEM((2, total, units), BF), shape((total, 128), F32),
            shape((total // tile * 8, units), F32), shape((total // tile * 8, cols), F32)]
    before = [] if before is None else [inside(before[0]), inside(before[1]), *before[2:]]
    return pl.pallas_call(
        functools.partial(norm_mlp_kernel, first_row=first_row),
        grid=(tiles,),
        in_specs=[pl.BlockSpec(memory_space=pltpu.SMEM)]
        + part(0) + part(1)
        + [whole((1, width)), whole((1, width)), whole((width, units)), whole((1, units)), whole((units, width))]
        + [pl.BlockSpec(memory_space=pl.ANY)] * len(before),
        out_specs=[paired(width), paired(units), rowed(128), eight(units), eight(cols)],
        out_shape=outs,
        input_output_aliases={14 + k: k for k in range(len(before))},
        compiler_params=pltpu.CompilerParams(vmem_limit_bytes=VMEM_BYTES),
        cost_estimate=cost(0.010 * rows),
        name="norm_mlp",
    )(place, near[0], near[1], *far, near[2], near[3], *far, gain, bias, inside(w_in), b_in, inside(w_down), *before)


def turn(field, cosine, sine):
    lane = lax.broadcasted_iota(jnp.int32, field.shape, 1)
    size = field.shape[1]
    other = jnp.where(lane % 2 == 0, pltpu.roll(field, size - 1, 1), pltpu.roll(field, 1, 1))
    return field * cosine + other * sine


def attend_kernel(
    place, left, w_q, w_k, w_v, w_o, cosine, sine, cos_all, sin_all, attended, g_qkv,
    k_aug, k_t, v_nat, v_t, q_nat, q_aug, d_out, gk_acc, gv_acc, *, tiles, tile, pairs,
):
    step = pl.program_id(0)
    length = place[1]
    share = 128 * pairs

    @pl.when(step < tiles)
    def project():
        h = left[0]
        cos = cosine[...]
        sin = sine[...]
        q_all = mm(h, w_q[...])
        k_all = mm(h, w_k[...])
        v_all = mm(h, w_v[...])
        g_all = mm(left[1], w_o[...], NT)
        start = pl.multiple_of(step * tile, tile)
        here = pl.ds(start, tile)
        lane = lax.broadcasted_iota(jnp.int32, (tile, 128), 1)
        key_row = start + lax.broadcasted_iota(jnp.int32, (tile, 128), 0)
        closed = jnp.where(key_row < length, 0.0, -1e30)
        first = lane < HEAD_DIM
        sub = lax.broadcasted_iota(jnp.int32, (128, tile), 0)
        for p in range(pairs):
            cut = slice(128 * p, 128 * (p + 1))
            q = turn(q_all[:, cut], cos, sin) * HEAD_DIM ** (-0.5)
            k = turn(k_all[:, cut], cos, sin)
            v = v_all[:, cut]
            q_nat[p, here, :] = q.astype(BF)
            v_nat[p, here, :] = v.astype(BF)
            k_aug[2 * p, here, :] = jnp.where(first, k, jnp.where(lane == HEAD_DIM, closed, 0.0)).astype(BF)
            k_aug[2 * p + 1, here, :] = jnp.where(first, jnp.where(lane == 0, closed, 0.0), k).astype(BF)
            q_t = q.T
            q_aug[2 * p, :, here] = jnp.where(sub < HEAD_DIM, q_t, jnp.where(sub == HEAD_DIM, 1.0, 0.0)).astype(BF)
            q_aug[2 * p + 1, :, here] = jnp.where(sub < HEAD_DIM, jnp.where(sub == 0, 1.0, 0.0), q_t).astype(BF)
            k_t[p, :, here] = k.T.astype(BF)
            v_t[p, :, here] = v.T.astype(BF)
            d_out[p, :, here] = g_all[:, cut].T

    @pl.when(step >= tiles)
    def attend():
        p = step - tiles
        lane = lax.broadcasted_iota(jnp.int32, (tile, 128), 1)
        later = lax.broadcasted_iota(jnp.int32, (tile, tile), 0) > lax.broadcasted_iota(jnp.int32, (tile, tile), 1)
        heads = range(2)
        mine = [lane < HEAD_DIM, lane >= HEAD_DIM]
        cuts = [slice(0, HEAD_DIM), slice(HEAD_DIM, 2 * HEAD_DIM)]

        def cut_of(j):
            return pl.ds(pl.multiple_of(j * share + p * 128, 128), 128)

        def score(i):
            n = (i + 1) * tile
            return [mm(k_aug[2 * p + h, :n, :], q_aug[2 * p + h, :, i * tile : n]) for h in heads]

        for i in range(tiles):
            n = (i + 1) * tile
            here = slice(i * tile, n)
            old = slice(0, i * tile)
            scores = ahead if i else score(0)
            weights, inverses = [], []
            for h in heads:
                s = scores[h]
                tail = jnp.where(later, -1e30, s[n - tile :])
                s = tail if i == 0 else jnp.concatenate([s[: n - tile], tail], axis=0)
                e = jnp.exp(s - jnp.max(s, axis=0, keepdims=True))
                inverses.append(1.0 / jnp.sum(e, axis=0, keepdims=True))
                weights.append(e)
            lows = [e.astype(BF) for e in weights]
            outs = [mm(v_t[p, cuts[h], :n], lows[h]) * inverses[h] for h in heads]
            scaled, inner = [], []
            for h in heads:
                d = d_out[p, cuts[h], here]
                inner.append(jnp.sum(d * outs[h], axis=0, keepdims=True) * inverses[h])
                scaled.append(d * inverses[h])
            g_scores = []
            for h in heads:
                zero = jnp.zeros((HEAD_DIM, tile), BF)
                d_t = scaled[h].astype(BF)
                d_t = jnp.concatenate([d_t, zero] if h == 0 else [zero, d_t], axis=0)
                g_scores.append((weights[h] * (mm(v_nat[p, :n, :], d_t) - inner[h])).astype(BF))
            if i + 1 < tiles:
                ahead = score(i + 1)
            attended[here, cut_of(0)] = jnp.concatenate(outs, axis=0).T.astype(BF)
            d_nat = jnp.concatenate(scaled, axis=0).T
            q_here = q_nat[p, here, :]
            g_q = jnp.concatenate([mm(k_t[p, cuts[h], :n], g_scores[h]) for h in heads], axis=0).T * HEAD_DIM ** (-0.5)
            g_qkv[here, cut_of(0)] = turn(g_q, cos_all[here, :], -sin_all[here, :]).astype(BF)
            add_v = sum(mm(lows[h], jnp.where(mine[h], d_nat, 0.0).astype(BF)) for h in heads)
            add_k = sum(mm(g_scores[h], jnp.where(mine[h], q_here, jnp.zeros_like(q_here))) for h in heads)
            if i > 0:
                gv_acc[old] += add_v[: n - tile]
                gk_acc[old] += add_k[: n - tile]
            gv_acc[here] = add_v[n - tile :]
            gk_acc[here] = add_k[n - tile :]
        g_qkv[:, cut_of(1)] = turn(gk_acc[...], cos_all[...], -sin_all[...]).astype(BF)
        g_qkv[:, cut_of(2)] = gv_acc[...].astype(BF)


def attend(place, left, weights):
    _, rows, width = left.shape
    share = width // 4
    pairs = share // 128
    tile = min(256, rows)
    tiles = rows // tile

    def early(i, _):
        return (jnp.minimum(i, tiles - 1), 0)

    def whole(shape):
        return pl.BlockSpec(shape, lambda i, _: (0, 0), pipeline_mode=pl.Buffered(1))

    w_q, w_k, w_v, w_o, _, _, cosine, sine = [inside(value) for value in weights]
    return pl.pallas_call(
        functools.partial(attend_kernel, tiles=tiles, tile=tile, pairs=pairs),
        grid_spec=pltpu.PrefetchScalarGridSpec(
            num_scalar_prefetch=1,
            grid=(tiles + pairs,),
            in_specs=[
                pl.BlockSpec((2, tile, width), lambda i, _: (0, jnp.minimum(i, tiles - 1), 0)),
                whole(w_q.shape), whole(w_k.shape), whole(w_v.shape), whole(w_o.shape),
                pl.BlockSpec((tile, 128), early),
                pl.BlockSpec((tile, 128), early),
                whole((rows, 128)), whole((rows, 128)),
            ],
            out_specs=[whole((rows, share)), whole((rows, 3 * share))],
            scratch_shapes=[
                pltpu.VMEM((2 * pairs, rows, 128), BF),
                pltpu.VMEM((pairs, 128, rows), BF),
                pltpu.VMEM((pairs, rows, 128), BF),
                pltpu.VMEM((pairs, 128, rows), BF),
                pltpu.VMEM((pairs, rows, 128), BF),
                pltpu.VMEM((2 * pairs, 128, rows), BF),
                pltpu.VMEM((pairs, 128, rows), F32),
                pltpu.VMEM((rows, 128), F32),
                pltpu.VMEM((rows, 128), F32),
            ],
        ),
        out_shape=[pltpu.VMEM((rows, share), BF), pltpu.VMEM((rows, 3 * share), BF)],
        compiler_params=pltpu.CompilerParams(vmem_limit_bytes=VMEM_BYTES),
        cost_estimate=cost(0.014 * rows),
        name="attend",
    )(place, inside(left), w_q, w_k, w_v, w_o, cosine, sine, cosine, sine)


def weight_mlp_kernel(place, scale, left_0, left_1, right_0, right_1, keep, send):
    total = (scale[0] * (mm(left_0[0], right_0[0], TN) + mm(left_1[0], right_1[0], TN))).astype(BF)
    half = total.shape[0] // 2
    odd = place[2] == 1
    keep[0] = jnp.where(odd, total[half:], total[:half])
    send[0] = jnp.where(odd, total[:half], total[half:])


def weight_att_kernel(place, scale, left_0, left_1, qkv_0, qkv_1, att_0, att_1, keep, send):
    odd = place[2] == 1
    size = qkv_0.shape[1]
    first = (scale[0] * (mm(left_0[0], qkv_0[...], TN) + mm(left_1[0], qkv_1[...], TN))).astype(BF)
    second = (scale[0] * (mm(left_0[1], att_0[...], TN) + mm(left_1[1], att_1[...], TN))).astype(BF)
    half = first.shape[0] // 2
    keep[0, :, :size] = jnp.where(odd, first[half:], first[:half])
    send[0, :, :size] = jnp.where(odd, first[:half], first[half:])
    keep[0, :, size:] = jnp.where(odd, second[half:], second[:half])
    send[0, :, size:] = jnp.where(odd, second[:half], second[half:])


def weight_hold_kernel(place, scale, left_0, left_1, right_0, right_1, hold, ship):
    total = (scale[0] * (mm(left_0[0], right_0[0], TN) + mm(left_1[0], right_1[0], TN))).astype(BF)
    half = total.shape[0] // 2
    odd = place[2] == 1
    mine = jnp.where(odd, total[half:], total[:half])
    other = jnp.where(odd, total[:half], total[half:])

    @pl.when(pl.program_id(0) < 2)
    def near():
        hold[0, 0] = mine
        hold[0, 1] = other

    @pl.when(pl.program_id(0) >= 2)
    def far():
        ship[0, 0] = mine
        ship[0, 1] = other


def chip_of(slot, place):
    return (2 * (slot & 1) + (slot >> 1)) ^ place[3]


def weight_mlp(place, scale, lefts, rights, kind):
    _, rows, width = lefts[0].shape
    units = rights[0].shape[2]
    size = width // 8
    column = pl.BlockSpec((1, rows, 2 * size), lambda i, where: (kind, 0, chip_of(i, where)))
    whole = pl.BlockSpec((1, rows, units), lambda i, where: (kind, 0, 0), pipeline_mode=pl.Buffered(1))
    if kind == 0:
        kernel = weight_mlp_kernel
        slot = pl.BlockSpec((1, size, units), lambda i, where: (i, 0, 0))
        outs = [slot, slot]
        out = [pltpu.HBM((4, size, units), BF)] * 2
    else:
        kernel = weight_hold_kernel
        outs = [pl.BlockSpec((1, 2, size, units), lambda i, where: (jnp.minimum(i, 1), 0, 0, 0)),
                pl.BlockSpec((1, 2, size, units), lambda i, where: (jnp.maximum(i - 2, 0), 0, 0, 0))]
        out = [pltpu.HBM((2, 2, size, units), BF)] * 2
    return pl.pallas_call(
        kernel,
        grid_spec=pltpu.PrefetchScalarGridSpec(
            num_scalar_prefetch=1, grid=(4,),
            in_specs=[pl.BlockSpec(memory_space=pltpu.SMEM), column, column, whole, whole], out_specs=outs,
        ),
        out_shape=out,
        compiler_params=pltpu.CompilerParams(vmem_limit_bytes=VMEM_BYTES),
        cost_estimate=cost(0.0065 * rows),
        name="weight_mlp",
    )(place, scale, *[inside(value) for value in (*lefts, *rights)])


def weight_att(place, scale, lefts, qkvs, atts):
    _, rows, width = lefts[0].shape
    units = qkvs[0].shape[1] + atts[0].shape[1]
    size = width // 8
    column = pl.BlockSpec((2, rows, 2 * size), lambda i, where: (0, 0, chip_of(i, where)))

    def whole(ref):
        return pl.BlockSpec(ref.shape, lambda i, where: (0, 0), pipeline_mode=pl.Buffered(1))

    slot = pl.BlockSpec((1, size, units), lambda i, where: (i, 0, 0))
    out = pltpu.HBM((4, size, units), BF)
    return pl.pallas_call(
        weight_att_kernel,
        grid_spec=pltpu.PrefetchScalarGridSpec(
            num_scalar_prefetch=1, grid=(4,),
            in_specs=[pl.BlockSpec(memory_space=pltpu.SMEM), column, column] + [whole(r) for r in (*qkvs, *atts)],
            out_specs=[slot, slot],
        ),
        out_shape=[out, out],
        compiler_params=pltpu.CompilerParams(vmem_limit_bytes=VMEM_BYTES),
        cost_estimate=cost(0.007 * rows),
        name="weight_att",
    )(place, scale, *[inside(value) for value in (*lefts, *qkvs, *atts)])


def branch_kernel(place, left, right, att, g_qkv, w_q, w_k, w_v, w_o, w_in, w_down, gain, bias,
                  keep, near, far_b, far_g, sums, column_sums):
    own = place[0]
    rows, share = att.shape
    total = mm(right[1], w_down[...]) + mm(att[...], w_o[...])
    g_total = mm(right[0], w_in[...], NT)
    for j, w in enumerate((w_q, w_k, w_v)):
        g_total += mm(g_qkv[:, j * share : (j + 1) * share], w[...], NT)
    odd = (own & 1) == 1
    up = (own >> 1) == 1
    for kind, (whole, far) in enumerate(((total, far_b), (g_total, far_g))):
        cuts = [whole[:, j * share : (j + 1) * share].astype(BF) for j in range(4)]
        low = [jnp.where(odd, cuts[2 * y + 1], cuts[2 * y]) for y in range(2)]
        high = [jnp.where(odd, cuts[2 * y], cuts[2 * y + 1]) for y in range(2)]
        keep[0, kind] = jnp.where(up, low[1], low[0])
        keep[1, kind] = jnp.where(up, low[0], low[1])
        near[kind] = jnp.where(up, high[1], high[0])
        far[...] = jnp.where(up, high[0], high[1])
    turned = g_total * (left[0].astype(F32) - bias[...])
    mean_part = jnp.sum(g_total * gain[...], axis=1, keepdims=True)
    inner_part = jnp.sum(turned, axis=1, keepdims=True)
    lane = lax.broadcasted_iota(jnp.int32, (rows, 128), 1)
    sums[...] = jnp.where(lane == 0, mean_part, inner_part).T[:8, :]

    @pl.when(pl.program_id(0) == 0)
    def clear():
        column_sums[...] = jnp.zeros_like(column_sums)

    column_sums[0:1, :] += jnp.sum(g_total, axis=0, keepdims=True)
    column_sums[1:2, :] += jnp.sum(turned, axis=0, keepdims=True)


def branch_parts(place, left, right, att, g_qkv, weights, gain, bias, first_row, rows):
    _, _, width = left.shape
    units = right.shape[2]
    share = att.shape[1]
    tile = min(256, rows)
    tiles = rows // tile
    offset = first_row // tile

    def paired(k, size):
        return pl.BlockSpec((k, tile, size), lambda i, _: (0, i + offset, 0))

    def rowed(size):
        return pl.BlockSpec((tile, size), lambda i, _: (i + offset, 0))

    def whole(shape):
        return pl.BlockSpec(shape, lambda i, _: (0, 0), pipeline_mode=pl.Buffered(1))

    weights = [inside(value) for value in weights[:6]]
    shape = jax.ShapeDtypeStruct
    slots = pl.BlockSpec((2, 2, tile, share), lambda i, _: (0, 0, i, 0))
    sent = pl.BlockSpec((2, tile, share), lambda i, _: (0, i, 0))
    rowed_out = pl.BlockSpec((tile, share), lambda i, _: (i, 0))
    return pl.pallas_call(
        branch_kernel,
        grid_spec=pltpu.PrefetchScalarGridSpec(
            num_scalar_prefetch=1,
            grid=(tiles,),
            in_specs=[
                paired(1, width), paired(2, units), rowed(share), rowed(3 * share),
                *[whole(value.shape) for value in weights],
                whole((1, width)), whole((1, width)),
            ],
            out_specs=[slots, sent, rowed_out, rowed_out, pl.BlockSpec((8, tile), lambda i, _: (0, i)), pl.BlockSpec((8, width), lambda i, _: (0, 0))],
        ),
        out_shape=[pltpu.HBM((2, 2, rows, share), BF)] + [pltpu.HBM((2, rows, share), BF)] + [pltpu.HBM((rows, share), BF)] * 2 + [shape((8, rows), F32),
                   shape((8, width), F32)],
        compiler_params=pltpu.CompilerParams(vmem_limit_bytes=VMEM_BYTES),
        cost_estimate=cost(0.010 * rows),
        name="branch_parts",
    )(place, inside(left), inside(right), inside(att), inside(g_qkv), *weights, gain, bias)


def combine_kernel(count, keep_in, x_in, hold, z_down, kept, core_b, core_g, z_in, low_in, zz_down, low_down, chip):
    size, units = keep_in.shape[1:]
    for k in range(2):
        z_in[k * size : (k + 1) * size] = keep_in[2 + k] + x_in[2 + k]
        low_in[k] = keep_in[k] + x_in[k]
        zz_down[k] = hold[1, k] + z_down[1, k]
        low_down[k] = hold[0, k] + z_down[0, k]
    rows = z_in.shape[0] - 2 * size
    row = lax.broadcasted_iota(jnp.int32, (rows, units), 0)
    value = jnp.full((rows, units), count[0], F32)
    high = value.astype(BF).astype(F32)
    z_in[2 * size :] = jnp.where(row == 0, high, jnp.where(row == 1, value - high, 0.0)).astype(BF)
    chip[0] = kept[1, 0] + core_b[...]
    chip[1] = kept[1, 1] + core_g[...]


def combine(count, keep_in, x_in, hold, z_down, kept, core):
    _, size, units = keep_in.shape
    _, _, rows, cols = kept.shape
    inner = pl.BlockSpec(memory_space=pltpu.VMEM)
    shapes = [(2 * size + 16, units), (2, size, units), (2, size, units), (2, size, units), (2, rows, cols)]
    return pl.pallas_call(
        combine_kernel,
        in_specs=[pl.BlockSpec(memory_space=pltpu.SMEM)] + [inner] * 7,
        out_specs=[inner] * 5,
        out_shape=[pltpu.HBM(shape, BF) for shape in shapes],
        compiler_params=pltpu.CompilerParams(vmem_limit_bytes=VMEM_BYTES),
        cost_estimate=cost(3),
        name="combine",
    )(count, *[outside(value) for value in (keep_in, x_in, hold, z_down, kept, *core)])


def relay_kernel(count, low, z_in, zz_in, kept, total):
    size, units = kept.shape
    kept[...] = low[0] + z_in[:size]
    zz_in[:size] = low[1] + z_in[size : 2 * size]
    tail = z_in[2 * size :].astype(F32)
    value = count[0] + tail[0:1] + tail[1:2]
    high = value.astype(BF).astype(F32)
    row = lax.broadcasted_iota(jnp.int32, tail.shape, 0)
    zz_in[size:] = jnp.where(row == 0, high, jnp.where(row == 1, value - high, 0.0)).astype(BF)
    total[...] = jnp.broadcast_to(value[:, :128], total.shape)


def relay(count, low, z_in):
    _, size, units = low.shape
    inner = pl.BlockSpec(memory_space=pltpu.VMEM)
    shape = jax.ShapeDtypeStruct
    return pl.pallas_call(
        relay_kernel,
        in_specs=[pl.BlockSpec(memory_space=pltpu.SMEM), inner, inner],
        out_specs=[inner] * 3,
        out_shape=[shape((size + 16, units), BF), shape((size, units), BF), shape((8, 128), F32)],
        compiler_params=pltpu.CompilerParams(vmem_limit_bytes=VMEM_BYTES),
        cost_estimate=cost(1),
        name="relay",
    )(count, low, z_in)


def final_kernel(place, scale, keep, near, far, x_ref, cot, stats, sums, gain, bias_down, *refs, first_row):
    mixed, g_x = refs[-2:]
    step = pl.program_id(0)
    rows, cols = x_ref.shape
    width = 4 * cols
    x = x_ref[...].astype(F32)
    branch = keep[0, 0].astype(F32) + near[0].astype(F32) + far[0].astype(F32)
    mixed[...] = (x + (branch + bias_down[...])).astype(BF)
    g = scale[0] * (keep[0, 1].astype(F32) + near[1].astype(F32) + far[1].astype(F32))
    inv_std = stats[:, 1:2]
    x_hat = (x - stats[:, 0:1]) * inv_std
    totals = (scale[0] / width) * jnp.concatenate([sums[...], jnp.zeros((126, rows), F32)], axis=0).T
    row = first_row + step * rows + lax.broadcasted_iota(jnp.int32, (rows, 1), 0)
    weight = jnp.where(row < place[1], scale[0], 0.0)
    g_out = weight * cot[...].astype(F32)
    g_x[...] = g_out + inv_std * (g * gain[...] - totals[:, 0:1] - x_hat * totals[:, 1:2])


def finish_rows(place, scale, keep, near, far, x, cot, stats, sums, gain, bias_down, sequence, first_row, before=None):
    _, rows, cols = far.shape
    tile = min(512, rows)
    tiles = rows // tile
    pad_len = stats.shape[0]
    begin = (sequence * pad_len + first_row) // tile
    inner = first_row // tile
    part = pl.BlockSpec((tile, cols), lambda i: (i + begin, 0))
    cored = pl.BlockSpec((1, tile, cols), lambda i: (0, i, 0))
    kept = pl.BlockSpec((1, 2, tile, cols), lambda i: (0, 0, i, 0))
    both = pl.BlockSpec((2, tile, cols), lambda i: (0, i, 0))
    flat = pl.BlockSpec((1, cols), lambda i: (0, 0))
    scalar = pl.BlockSpec(memory_space=pltpu.SMEM)
    shape = jax.ShapeDtypeStruct
    before = [] if before is None else list(before)
    return pl.pallas_call(
        functools.partial(final_kernel, first_row=first_row),
        grid=(tiles,),
        in_specs=[scalar, scalar, kept, both, both, part, part,
                  pl.BlockSpec((tile, 128), lambda i: (i + inner, 0)), pl.BlockSpec((2, tile), lambda i: (0, i + begin)), flat, flat]
        + [pl.BlockSpec(memory_space=pl.ANY)] * len(before),
        out_specs=[part, part],
        out_shape=[shape(x.shape, BF), shape(x.shape, F32)],
        input_output_aliases={11 + k: k for k in range(len(before))},
        compiler_params=pltpu.CompilerParams(vmem_limit_bytes=VMEM_BYTES),
        cost_estimate=cost(0.003 * rows),
        name="finish_rows",
    )(place, scale, *[outside(value) for value in (keep, near, far, x, cot, stats)], sums, gain, bias_down, *before)


def final_weight_kernel(factor, low_in, far_in, low_down, far_down, low_a, far_a, g_in, g_down, g_qkv, g_out):
    scale = factor[0]
    _, size, cols = g_qkv.shape
    g_in[...] = scale * (low_in[...].astype(F32) + far_in[:size].astype(F32))
    g_down[...] = (scale * (low_down[...].astype(F32) + far_down[...].astype(F32))).T
    for j in range(3):
        cut = slice(j * cols, (j + 1) * cols)
        g_qkv[j] = scale * (low_a[:, cut].astype(F32) + far_a[:size, cut].astype(F32))
    cut = slice(3 * cols, 4 * cols)
    g_out[...] = (scale * (low_a[:, cut].astype(F32) + far_a[:size, cut].astype(F32))).T


def finish_weights(factor, low_in, far_in, low_down, far_down, low_a, far_a):
    size, units = low_in.shape
    cols = low_a.shape[1] // 4
    shape = jax.ShapeDtypeStruct
    return pl.pallas_call(
        final_weight_kernel,
        in_specs=[pl.BlockSpec(memory_space=pltpu.SMEM)] + [pl.BlockSpec(memory_space=pltpu.VMEM)] * 6,
        out_specs=[pl.BlockSpec(memory_space=pltpu.VMEM)] * 4,
        out_shape=[shape((size, units), F32), shape((units, size), F32), shape((3, size, cols), F32), shape((cols, size), F32)],
        compiler_params=pltpu.CompilerParams(vmem_limit_bytes=VMEM_BYTES),
        cost_estimate=cost(3),
        name="finish_weights",
    )(factor, low_in, far_in, low_down, far_down, low_a, far_a)


def swap(value, axis, bit):
    size = lax.axis_size(axis)
    return lax.ppermute(value, axis, [(i, i ^ bit) for i in range(size)])


def sum_small(value, axis):
    bit = 1
    while bit < lax.axis_size(axis):
        value = value + swap(value, axis, bit)
        bit *= 2
    return value


def add_core(kept, core):
    return kept[1] + jnp.stack(core)


def unpack(rows, count):
    part = -(-count // rows.shape[1])
    high, low = rows[:part].astype(F32), rows[part : 2 * part].astype(F32)
    return (high + low).reshape(-1)[:count]


def after(value, *others):
    return lax.optimization_barrier((value, *others))[0]


def on_device_fast(inputs, cotangent, lengths, ln_gain, ln_bias, w_qkv, w_out, w_in, b_in, w_down, b_down):
    groups = lax.axis_size("wide")
    column = lax.axis_index("narrow")
    place_wide = lax.axis_index("wide")
    rows_all, cols = inputs.shape
    pad_len = rows_all // 2
    width = w_qkv.shape[0]
    units = w_in.shape[1]
    place = jnp.stack([column, lengths[0], place_wide & 1, place_wide >> 1]).astype(jnp.int32)
    gain = ln_gain.reshape(1, width)
    bias = ln_bias.reshape(1, width)
    b_up = b_in.reshape(1, units)
    half = pad_len // 2
    cuts = ((0, half), (half, pad_len), (pad_len, rows_all))
    own_gain = lax.dynamic_slice_in_dim(ln_gain, column * cols, cols, 0).reshape(1, cols)
    b_row = b_down.reshape(1, cols)

    across = [swap(jnp.concatenate([inputs[low:high], cotangent[low:high]], axis=0), "narrow", 2) for low, high in cuts]
    near = (inputs, swap(inputs, "narrow", 1), cotangent, swap(cotangent, "narrow", 1))
    count = (2.0 * jnp.sum(lengths.astype(F32))).reshape(1)
    count_x = count + swap(count, "wide", 1)
    weights = load_weights(place, w_qkv, w_out, w_in, w_down, *turn_tables(pad_len))
    up_in, up_down = weights[4:6]

    def far(k, *earlier):
        rows = after(across[k], *earlier)
        return rows, swap(rows, "narrow", 1)

    def branch(place, mlp, att, first_row, rows):
        kept, near, far_b, far_g, sums, columns = branch_parts(
            place, mlp[0], mlp[1], *att, weights, gain, bias, first_row, rows)
        return kept, near, (far_b, far_g), sums, columns

    first = norm_mlp(place, near, far(0, weights[0], count_x), gain, bias, up_in, b_up, up_down, 0, 0, pad_len)
    place = after(place, first[3])
    mlp_0 = norm_mlp(place, near, far(1, first[3]), gain, bias, up_in, b_up, up_down, half, half, pad_len, first)
    place = after(place, mlp_0[3])
    att_0 = attend(place, mlp_0[0], weights)
    place = after(place, att_0[0])
    mlp_1 = norm_mlp(place, near, far(2, att_0[0]), gain, bias, up_in, b_up, up_down, pad_len, 0, pad_len)
    place = after(place, mlp_1[3])
    lefts = (mlp_0[0], mlp_1[0])
    rights = (mlp_0[1], mlp_1[1])
    keep_in, send_in = weight_mlp(place, count, lefts, rights, 0)
    place = after(place, keep_in)
    x_in = swap(send_in, "wide", 1)
    hold_down, ship_down = weight_mlp(place, count, lefts, rights, 1)
    place = after(place, hold_down)
    z_down = swap(ship_down, "wide", 2)
    kept_0, near_0, sent_0, sums_0, columns_0 = branch(place, mlp_0, att_0, 0, pad_len)
    core_0 = [swap(part, "narrow", 1) for part in sent_0]
    place = after(place, sums_0)
    att_1 = attend(place, mlp_1[0], weights)
    size = keep_in.shape[1]
    x_in, z_down, count_x, *core_0 = lax.optimization_barrier((x_in, z_down, count_x, *core_0, att_1[0]))[:5]
    z_in, low_in, zz_down, low_down, chip_0 = combine(count_x, keep_in, x_in, hold_down, z_down, kept_0, core_0)
    z_in = swap(z_in, "wide", 2)
    zz_down = swap(zz_down, "wide", 4)
    y_0 = swap(chip_0, "narrow", 2)
    near_0 = swap(after(near_0, chip_0), "narrow", 1)
    place = after(place, low_in, low_down, chip_0, att_1[0])
    keep_a, send_a = weight_att(place, count, lefts, (att_0[1], att_1[1]), (att_0[0], att_1[0]))
    x_a = swap(send_a, "wide", 1)
    place = after(place, keep_a, near_0)
    kept_1, near_1, sent_1, sums_1, columns_1 = branch(place, mlp_1, att_1, 0, pad_len)
    core_1 = [swap(part, "narrow", 1) for part in sent_1]
    z_in, zz_down, y_0, sums_0, columns_0 = lax.optimization_barrier((z_in, zz_down, y_0, sums_0, columns_0, sums_1))[:5]
    zz_in, low_in, count_row = relay(count_x, low_in, z_in)
    zz_in = swap(zz_in, "wide", 4)
    x_d = swap(low_down[1] + zz_down[1], "wide", 1)
    low_down = low_down[0] + zz_down[0]
    sums = jnp.concatenate([sums_0[:2], sums_1[:2], columns_0[:2] + columns_1[:2]], axis=1)
    sums = after(sums, y_0)
    sums = sums + swap(sums, "narrow", 1)
    core_1 = [after(part, sums, low_down, low_in) for part in core_1]
    chip_1 = add_core(kept_1, core_1)
    y_1 = swap(chip_1, "narrow", 2)
    far_sums = swap(after(sums[:, :rows_all], chip_1), "narrow", 2)
    x_a = after(x_a, chip_1)
    z_a = swap(keep_a[2:] + x_a[2:], "wide", 2)
    low_a = keep_a[:2] + x_a[:2]
    sum_up, sum_down, columns = lax.optimization_barrier((mlp_0[3], mlp_0[4], sums[:, rows_all:], low_a))[:3]
    small = jnp.concatenate([columns.reshape(-1), jnp.sum(sum_up + mlp_1[3], axis=0), jnp.sum(sum_down + mlp_1[4], axis=0)])
    small = count * small
    small = small + swap(small, "wide", 1)
    z_small = swap(small, "wide", 2)
    zz_in = after(zz_in, small)
    count_row = count_row[0] + unpack(zz_in[size:], units)[:128]
    per_count = groups / count_row[:1]
    scale = count * per_count
    y_1, far_sums = lax.optimization_barrier((y_1, far_sums, scale))[:2]
    sums = sums[:, :rows_all] + far_sums
    small = small + after(z_small, sums)
    z_a = after(z_a, small)
    zz_a = swap(low_a[1] + z_a[1], "wide", 4)
    low_a = low_a[0] + z_a[0]
    zz_small = swap(small, "wide", 4)
    near_1 = swap(after(near_1, low_a), "narrow", 1)
    ends = finish_rows(after(place, small), scale, kept_0, near_0, y_0, inputs, cotangent, mlp_0[2], sums, own_gain, b_row, 0, 0)
    ends = finish_rows(place, scale, kept_1, near_1, y_1, inputs, cotangent, mlp_1[2], sums, own_gain, b_row, 1, 0, ends)
    small = per_count * (small + after(zz_small, ends[0]))
    columns = small[: 2 * width].reshape(2, width)
    far_columns = swap(columns, "narrow", 2)
    zz_a, x_d, far_columns = lax.optimization_barrier((zz_a, x_d, far_columns, ends[0]))[:3]
    columns = lax.dynamic_slice_in_dim(columns + far_columns, column * cols, cols, 1)
    g_in, g_down, g_qkv, g_out = finish_weights(per_count, low_in, zz_in, low_down, x_d, low_a, zz_a)
    return (
        ends[0],
        ends[1],
        columns[1] / own_gain[0],
        columns[0],
        jnp.transpose(g_qkv, (1, 0, 2)),
        g_out,
        g_in,
        small[2 * width : 2 * width + units],
        g_down,
        small[2 * width + units :],
    )


def turn_tables(length):
    position = np.arange(length, dtype=np.float32)[:, None]
    frequency = (10000.0 ** (-2.0 * np.arange(ROT // 2, dtype=np.float32) / ROT)).astype(np.float32)
    angles = (position * frequency[None, :]).astype(np.float32)
    cosine = np.ones((length, HEAD_DIM), np.float32)
    sine = np.zeros((length, HEAD_DIM), np.float32)
    cosine[:, :ROT] = np.repeat(np.cos(angles), 2, axis=1)
    sine[:, 0:ROT:2] = -np.sin(angles)
    sine[:, 1:ROT:2] = np.sin(angles)
    return jnp.asarray(np.tile(cosine, (1, 2))), jnp.asarray(np.tile(sine, (1, 2)))


def solution(mesh):
    placed = (
        P("wide", "narrow"),
        P("wide", "narrow"),
        P("wide"),
        P(),
        P(),
        P(),
        P(),
        P(None, "narrow"),
        P("narrow"),
        P("narrow", None),
        P("narrow"),
    )
    paired = mesh.shape["narrow"] == 4 and mesh.shape["wide"] == 8
    return jax.shard_map(
        on_device_fast if paired else on_device,
        mesh=mesh,
        in_specs=placed,
        out_specs=(
            P("wide", "narrow"),
            P("wide", "narrow"),
            P("narrow"),
            P("narrow"),
            P("wide", None, "narrow"),
            P("narrow", "wide"),
            P("wide", "narrow"),
            P("narrow"),
            P("narrow", "wide"),
            P("narrow"),
        ),
        check_vma=False,
    )
```

```python
import functools

import jax
import jax.numpy as jnp
import numpy as np
from jax import lax
from jax.experimental import pallas as pl
from jax.experimental.pallas import tpu as pltpu
from jax.sharding import PartitionSpec as P

HEAD_DIM = 64
ROT = 32
GELU_A = 0.7978845608028654
GELU_B = 0.044715
VMEM_BYTES = 24 * 1024 * 1024
F32 = jnp.float32
BF = jnp.bfloat16
NN = (((1,), (0,)), ((), ()))
NT = (((1,), (1,)), ((), ()))
TN = (((0,), (0,)), ((), ()))


norm_eps = 1e-05


def gelu_tanh(value_in):
    return (
        0.5
        * value_in
        * (
            1.0
            + jnp.tanh(0.7978845608028654 * (value_in + 0.044715 * value_in * value_in * value_in))
        )
    )


def rotary_tables(seq_len, rot_dims):
    position = jnp.arange(seq_len).astype(jnp.float32)[:, None]
    freq_index = jnp.arange(rot_dims // 2).astype(jnp.float32)[None, :]
    angles = position * 10000.0 ** (-2.0 * freq_index / rot_dims)
    return (jnp.cos(angles), jnp.sin(angles))


def rotate(field_in, cosine, sine_table, rot_dims):
    rotated = field_in[..., :rot_dims]
    others = field_in[..., rot_dims:]
    pair_view = rotated.reshape(rotated.shape[:-1] + (rot_dims // 2, 2))
    first_half = pair_view[..., 0]
    second_half = pair_view[..., 1]
    cos_table = cosine[:, None, :]
    sin_table = sine_table[:, None, :]
    new_first = first_half * cos_table - second_half * sin_table
    new_second = second_half * cos_table + first_half * sin_table
    joined = jnp.stack([new_first, new_second], axis=-1).reshape(rotated.shape)
    return jnp.concatenate([joined, others], axis=-1)


def causal_mask(first_row, block_rows, last_row, length):
    query_pos = first_row + jnp.arange(block_rows)[:, None]
    key_pos = jnp.arange(last_row)[None, :]
    return (key_pos <= query_pos) & (key_pos < length)


def block_scores(queries, key_rows, first_row, last_row, length):
    score_scale = HEAD_DIM ** (-0.5)
    scores = (
        jnp.einsum(
            "qhd,khd->hqk",
            queries[first_row:last_row],
            key_rows[:last_row],
            preferred_element_type=jnp.float32,
        )
        * score_scale
    )
    allowed = causal_mask(first_row, last_row - first_row, last_row, length)
    return jnp.where(allowed[None], scores, -1e30)


def attend_forward(queries, key_rows, values, length, block_rows):
    seq_len = queries.shape[0]
    queries = queries.reshape(seq_len, -1, HEAD_DIM)
    key_rows = key_rows.reshape(seq_len, -1, HEAD_DIM)
    values = values.reshape(seq_len, -1, HEAD_DIM)
    outputs = []
    lse_parts = []
    for first_row in range(0, seq_len, block_rows):
        last_row = first_row + block_rows
        scores = block_scores(queries, key_rows, first_row, last_row, length)
        row_max = jnp.max(scores, axis=-1, keepdims=True)
        exp_scores = jnp.exp(scores - row_max)
        row_total = jnp.sum(exp_scores, axis=-1, keepdims=True)
        probs_low = (exp_scores / row_total).astype(jnp.bfloat16)
        outputs.append(
            jnp.einsum(
                "hqk,khd->qhd", probs_low, values[:last_row], preferred_element_type=jnp.float32
            )
        )
        lse_parts.append((row_max + jnp.log(row_total))[..., 0])
    return (
        jnp.concatenate(outputs, axis=0).reshape(seq_len, -1),
        jnp.concatenate(lse_parts, axis=1),
    )


def attend_backward(queries, key_rows, values, grad_att, lse_rows, length, block_rows):
    seq_len = queries.shape[0]
    score_scale = HEAD_DIM ** (-0.5)
    queries = queries.reshape(seq_len, -1, HEAD_DIM)
    key_rows = key_rows.reshape(seq_len, -1, HEAD_DIM)
    values = values.reshape(seq_len, -1, HEAD_DIM)
    grad_att = grad_att.reshape(seq_len, -1, HEAD_DIM)
    key_grads = jnp.zeros(key_rows.shape, jnp.float32)
    value_grads = jnp.zeros(values.shape, jnp.float32)
    query_grads = []
    for first_row in range(0, seq_len, block_rows):
        last_row = first_row + block_rows
        scores = block_scores(queries, key_rows, first_row, last_row, length)
        probs = jnp.exp(scores - lse_rows[:, first_row:last_row, None])
        probs_low = probs.astype(jnp.bfloat16)
        grad_block = grad_att[first_row:last_row]
        grad_probs = jnp.einsum(
            "qhd,khd->hqk", grad_block, values[:last_row], preferred_element_type=jnp.float32
        )
        row_inner = jnp.sum(probs * grad_probs, axis=-1, keepdims=True)
        grad_scores = (probs * (grad_probs - row_inner)).astype(jnp.bfloat16)
        query_grads.append(
            jnp.einsum(
                "hqk,khd->qhd", grad_scores, key_rows[:last_row], preferred_element_type=jnp.float32
            )
            * score_scale
        )
        key_grads = key_grads.at[:last_row].add(
            jnp.einsum(
                "hqk,qhd->khd",
                grad_scores,
                queries[first_row:last_row],
                preferred_element_type=jnp.float32,
            )
            * score_scale
        )
        value_grads = value_grads.at[:last_row].add(
            jnp.einsum("hqk,qhd->khd", probs_low, grad_block, preferred_element_type=jnp.float32)
        )
    return (jnp.concatenate(query_grads, axis=0), key_grads, value_grads)


def on_device(
    inputs, cotangent, lengths, ln_gain, ln_bias, w_qkv, w_out, w_in, b_in, w_down, b_down
):
    groups = lax.axis_size("wide")
    narrow_size = lax.axis_size("narrow")
    column = lax.axis_index("narrow")
    seq_count = 2 * lengths.shape[0]
    rows_all = inputs.shape[0]
    pad_len = rows_all // seq_count
    model_width = w_qkv.shape[0]
    share_cols = model_width // narrow_size
    block_rows = min(512, pad_len)
    col_start = column * share_cols
    token_count = 2.0 * jnp.sum(lengths.astype(jnp.float32))
    token_sum = lax.psum(token_count, "wide")
    group_scale = groups * token_count / token_sum
    full_x, full_cot = (
        lax.all_gather(inputs, "narrow", axis=1, tiled=True),
        lax.all_gather(cotangent, "narrow", axis=1, tiled=True),
    )
    seq_lengths = jnp.repeat(lengths, 2)
    valid_rows = (
        (jnp.arange(pad_len)[None, :] < seq_lengths[:, None])
        .astype(jnp.float32)
        .reshape(rows_all, 1)
    )
    x_full = full_x.astype(jnp.float32)
    row_mean = jnp.mean(x_full, axis=-1, keepdims=True)
    centered = x_full - row_mean
    inv_std = lax.rsqrt(jnp.mean(centered * centered, axis=-1, keepdims=True) + norm_eps)
    x_hat = centered * inv_std
    hidden = (x_hat * ln_gain + ln_bias).astype(jnp.bfloat16)
    qkv_proj = jnp.dot(hidden, w_qkv, preferred_element_type=jnp.float32)
    qkv_proj = qkv_proj.reshape(seq_count, pad_len, 3, -1, HEAD_DIM)
    cosine, sine_table = rotary_tables(pad_len, ROT)
    q_seq = (
        rotate(qkv_proj[:, :, 0], cosine, sine_table, ROT)
        .astype(jnp.bfloat16)
        .reshape(seq_count, pad_len, -1)
    )
    k_seq = (
        rotate(qkv_proj[:, :, 1], cosine, sine_table, ROT)
        .astype(jnp.bfloat16)
        .reshape(seq_count, pad_len, -1)
    )
    v_seq = qkv_proj[:, :, 2].astype(jnp.bfloat16).reshape(seq_count, pad_len, -1)
    att_width = q_seq.shape[2]
    up_proj = jnp.dot(hidden, w_in, preferred_element_type=jnp.float32) + b_in
    activation = gelu_tanh(up_proj).astype(jnp.bfloat16)
    mlp_part = jnp.dot(activation, w_down, preferred_element_type=jnp.float32)

    def forward_one(packed):
        return attend_forward(packed[0], packed[1], packed[2], packed[3], block_rows)

    att_rows, lse_all = lax.map(forward_one, (q_seq, k_seq, v_seq, seq_lengths))
    attended = att_rows.astype(jnp.bfloat16).reshape(rows_all, att_width)
    branch_share = lax.psum_scatter(
        mlp_part.astype(jnp.bfloat16), "narrow", scatter_dimension=1, tiled=True
    ).astype(jnp.float32)
    w_out_cols = lax.dynamic_slice_in_dim(w_out, col_start, share_cols, 1)
    attn_share = jnp.dot(attended, w_out_cols, preferred_element_type=jnp.float32)
    mixed = (inputs.astype(jnp.float32) + (attn_share + (branch_share + b_down))).astype(
        jnp.bfloat16
    )
    grad_share = group_scale * valid_rows * cotangent.astype(jnp.float32)
    grad_share_low = grad_share.astype(jnp.bfloat16)
    grad_low = (group_scale * valid_rows * full_cot.astype(jnp.float32)).astype(jnp.bfloat16)
    g_b_down = jnp.sum(grad_share_low.astype(jnp.float32), axis=0)
    g_w_down = jnp.einsum("rf,rd->fd", activation, grad_low, preferred_element_type=jnp.float32)
    g_act = jnp.dot(grad_low, w_down.T, preferred_element_type=jnp.float32)
    gelu_value, gelu_pull = jax.vjp(gelu_tanh, up_proj)
    g_up = gelu_pull(g_act)[0].astype(jnp.bfloat16)
    g_b_in = jnp.sum(g_up.astype(jnp.float32), axis=0)
    g_w_in = jnp.einsum("rd,rf->df", hidden, g_up, preferred_element_type=jnp.float32)
    g_hidden_mlp = jnp.dot(g_up, w_in.T, preferred_element_type=jnp.float32)
    g_w_out_rows = jnp.einsum("rd,re->de", attended, grad_low, preferred_element_type=jnp.float32)
    g_att = jnp.dot(grad_low, w_out.T, preferred_element_type=jnp.float32).astype(jnp.bfloat16)

    def backward_one(packed):
        return attend_backward(
            packed[0], packed[1], packed[2], packed[3], packed[4], packed[5], block_rows
        )

    g_qrot, g_krot, g_val = lax.map(
        backward_one,
        (q_seq, k_seq, v_seq, g_att.reshape(seq_count, pad_len, att_width), lse_all, seq_lengths),
    )
    g_query = rotate(g_qrot, cosine, -sine_table, ROT)
    g_key = rotate(g_krot, cosine, -sine_table, ROT)
    g_qkv = (
        jnp.stack([g_query, g_key, g_val], axis=2)
        .reshape(rows_all, 3 * att_width)
        .astype(jnp.bfloat16)
    )
    g_w_qkv = jnp.einsum("rd,rc->dc", hidden, g_qkv, preferred_element_type=jnp.float32)
    g_hidden_attn = jnp.dot(g_qkv, w_qkv.T, preferred_element_type=jnp.float32)
    g_hidden = g_hidden_attn + lax.psum(g_hidden_mlp.astype(jnp.bfloat16), "narrow").astype(
        jnp.float32
    )
    d_hat = g_hidden * ln_gain
    g_x_full = inv_std * (
        d_hat
        - jnp.mean(d_hat, axis=-1, keepdims=True)
        - x_hat * jnp.mean(d_hat * x_hat, axis=-1, keepdims=True)
    )
    g_x_share = lax.dynamic_slice_in_dim(g_x_full, col_start, share_cols, 1)
    g_gain = lax.dynamic_slice_in_dim(jnp.sum(g_hidden * x_hat, axis=0), col_start, share_cols, 0)
    g_bias = lax.dynamic_slice_in_dim(jnp.sum(g_hidden, axis=0), col_start, share_cols, 0)
    g_inputs = grad_share + g_x_share
    qkv_three = g_w_qkv.reshape(model_width, 3, att_width)
    summed = (
        lax.psum_scatter(qkv_three, "wide", scatter_dimension=0, tiled=True),
        lax.psum_scatter(g_w_out_rows, "wide", scatter_dimension=1, tiled=True),
        lax.psum_scatter(g_w_in, "wide", scatter_dimension=0, tiled=True),
        lax.psum_scatter(g_w_down, "wide", scatter_dimension=1, tiled=True),
    )
    g_qkv_part = lax.dynamic_slice_in_dim(summed[0], col_start, share_cols, 2)
    g_out_part = lax.dynamic_slice_in_dim(summed[1], col_start, share_cols, 0)
    small = lax.psum((g_gain, g_bias, g_b_in, g_b_down), "wide")
    return (
        mixed,
        g_inputs,
        small[0],
        small[1],
        g_qkv_part,
        g_out_part,
        summed[2],
        small[2],
        summed[3],
        small[3],
    )


LOG2E = 1.4426950408889634


def inside(value):
    return pltpu.with_memory_space_constraint(value, pltpu.VMEM)


def outside(value):
    return pltpu.with_memory_space_constraint(value, pltpu.HBM)


def mm(left, right, dims=NN):
    return lax.dot_general(left, right, dims, preferred_element_type=F32)


COST_SCALE = 0.1


def cost(micros):
    return pl.CostEstimate(flops=int(COST_SCALE * micros * 1e9), bytes_accessed=1000000, transcendentals=0)


def load_kernel(place, w_qkv, w_out, w_in, w_down, cosine, sine, *refs):
    outs, sems = refs[:-1], refs[-1]
    share = outs[0].shape[1]
    own = place[0]
    sources = [w_qkv.at[:, pl.ds(pl.multiple_of((4 * j + own) * share, 128), share)] for j in range(3)]
    sources += [w_out.at[pl.ds(pl.multiple_of(own * share, 128), share), :], w_in, w_down, cosine, sine]
    copies = [pltpu.make_async_copy(src, dst, sems.at[k]) for k, (src, dst) in enumerate(zip(sources, outs))]
    for copy in copies:
        copy.start()
    for copy in copies:
        copy.wait()


def load_weights(place, w_qkv, w_out, w_in, w_down, cosine, sine):
    width = w_qkv.shape[0]
    share = width // 4
    shapes = [(width, share)] * 3 + [(share, width), w_in.shape, w_down.shape]
    any_place = pl.BlockSpec(memory_space=pl.ANY)
    return pl.pallas_call(
        load_kernel,
        in_specs=[pl.BlockSpec(memory_space=pltpu.SMEM)] + [any_place] * 6,
        out_specs=[any_place] * 8,
        out_shape=[pltpu.VMEM(shape, BF) for shape in shapes] + [pltpu.VMEM(cosine.shape, F32)] * 2,
        scratch_shapes=[pltpu.SemaphoreType.DMA((8,))],
        compiler_params=pltpu.CompilerParams(vmem_limit_bytes=VMEM_BYTES),
        cost_estimate=cost(3),
        name="load_weights",
    )(place, *[outside(value) for value in (w_qkv, w_out, w_in, w_down, cosine, sine)])


def norm_mlp_kernel(place, x0, x1, x2, x3, c0, c1, c2, c3, gain, bias, w_in, b_in, w_down, *refs, first_row):
    left, right, stats, sum_up, sum_grad = refs[-5:]
    step = pl.program_id(0)
    rows, cols = x0.shape
    width, units = w_in.shape
    own = place[0]
    xs = [ref[...].astype(F32) for ref in (x0, x1, x2, x3)]
    mean = jnp.sum(xs[0] + xs[1] + xs[2] + xs[3], axis=1, keepdims=True) * (1.0 / width)
    cs = [x - mean for x in xs]
    squares = cs[0] * cs[0] + cs[1] * cs[1] + cs[2] * cs[2] + cs[3] * cs[3]
    inv_std = lax.rsqrt(jnp.sum(squares, axis=1, keepdims=True) * (1.0 / width) + norm_eps)
    row = first_row + step * rows + lax.broadcasted_iota(jnp.int32, (rows, 1), 0)
    for j, (centered, cot) in enumerate(zip(cs, (c0, c1, c2, c3))):
        here = pl.ds(pl.multiple_of((own ^ j) * cols, cols), cols)
        left[0, :, here] = (centered * inv_std * gain[:, here] + bias[:, here]).astype(BF)
        low = jnp.where(row < place[1], cot[...], jnp.zeros_like(cot))
        left[1, :, here] = low
        if j == 0:
            sum_grad[...] = jnp.sum(low.astype(F32).reshape(rows // 8, 8, cols), axis=0)
    lane = lax.broadcasted_iota(jnp.int32, (rows, 128), 1)
    stats[...] = jnp.where(lane == 0, mean, inv_std)
    h = left[0]
    g = left[1]
    part = min(512, units)
    for first in range(0, units, part):
        here = pl.ds(first, part)
        up = mm(h, w_in[:, here]) + b_in[:, here]
        g_act = mm(g, w_down[here, :], NT)
        square = up * up
        tanh = jnp.tanh(up * (GELU_A + GELU_A * GELU_B * square))
        half = 0.5 * up
        plus = 1.0 + tanh
        slope = 0.5 * plus + (half * (1.0 - tanh * tanh)) * (GELU_A + 3.0 * GELU_A * GELU_B * square)
        g_up = slope * g_act
        right[0, :, here] = g_up.astype(BF)
        right[1, :, here] = (half * plus).astype(BF)
        sum_up[:, here] = jnp.sum(g_up.reshape(rows // 8, 8, part), axis=0)


def norm_mlp(place, near, far, gain, bias, w_in, b_in, w_down, start_row, first_row, total, before=None):
    rows, cols = far[0].shape
    rows //= 2
    width, units = w_in.shape
    tile = min(256, rows)
    tiles = rows // tile
    offset = first_row // tile
    begin = start_row // tile

    def part(j):
        return [pl.BlockSpec((tile, cols), lambda i: (i + begin, 0))] * 2 + [pl.BlockSpec((tile, cols), lambda i: (i + j * tiles, 0))] * 2

    def rowed(size):
        return pl.BlockSpec((tile, size), lambda i: (i + offset, 0))

    def paired(size):
        return pl.BlockSpec((2, tile, size), lambda i: (0, i + offset, 0))

    def eight(size):
        return pl.BlockSpec((8, size), lambda i: (i + offset, 0))

    def whole(shape):
        return pl.BlockSpec(memory_space=pltpu.VMEM)

    shape = jax.ShapeDtypeStruct
    outs = [pltpu.VMEM((2, total, width), BF), pltpu.VMEM((2, total, units), BF), shape((total, 128), F32),
            shape((total // tile * 8, units), F32), shape((total // tile * 8, cols), F32)]
    before = [] if before is None else [inside(before[0]), inside(before[1]), *before[2:]]
    return pl.pallas_call(
        functools.partial(norm_mlp_kernel, first_row=first_row),
        grid=(tiles,),
        in_specs=[pl.BlockSpec(memory_space=pltpu.SMEM)]
        + part(0) + part(1)
        + [whole((1, width)), whole((1, width)), whole((width, units)), whole((1, units)), whole((units, width))]
        + [pl.BlockSpec(memory_space=pl.ANY)] * len(before),
        out_specs=[paired(width), paired(units), rowed(128), eight(units), eight(cols)],
        out_shape=outs,
        input_output_aliases={14 + k: k for k in range(len(before))},
        compiler_params=pltpu.CompilerParams(vmem_limit_bytes=VMEM_BYTES),
        cost_estimate=cost(0.010 * rows),
        name="norm_mlp",
    )(place, near[0], near[1], *far, near[2], near[3], *far, gain, bias, inside(w_in), b_in, inside(w_down), *before)


def turn(field, cosine, sine):
    lane = lax.broadcasted_iota(jnp.int32, field.shape, 1)
    size = field.shape[1]
    other = jnp.where(lane % 2 == 0, pltpu.roll(field, size - 1, 1), pltpu.roll(field, 1, 1))
    return field * cosine + other * sine


def attend_kernel(
    place, left, w_q, w_k, w_v, w_o, cosine, sine, cos_all, sin_all, attended, g_qkv,
    k_aug, k_t, v_nat, v_t, q_nat, q_aug, d_out, gk_acc, gv_acc, *, tiles, tile, pairs,
):
    step = pl.program_id(0)
    length = place[1]
    share = 128 * pairs

    @pl.when(step < tiles)
    def project():
        h = left[0]
        cos = cosine[...]
        sin = sine[...]
        q_all = mm(h, w_q[...])
        k_all = mm(h, w_k[...])
        v_all = mm(h, w_v[...])
        g_all = mm(left[1], w_o[...], NT)
        start = pl.multiple_of(step * tile, tile)
        here = pl.ds(start, tile)
        lane = lax.broadcasted_iota(jnp.int32, (tile, 128), 1)
        key_row = start + lax.broadcasted_iota(jnp.int32, (tile, 128), 0)
        closed = jnp.where(key_row < length, 0.0, -1e30)
        first = lane < HEAD_DIM
        sub = lax.broadcasted_iota(jnp.int32, (128, tile), 0)
        for p in range(pairs):
            cut = slice(128 * p, 128 * (p + 1))
            q = turn(q_all[:, cut], cos, sin) * HEAD_DIM ** (-0.5)
            k = turn(k_all[:, cut], cos, sin)
            v = v_all[:, cut]
            q_nat[p, here, :] = q.astype(BF)
            v_nat[p, here, :] = v.astype(BF)
            k_aug[2 * p, here, :] = jnp.where(first, k, jnp.where(lane == HEAD_DIM, closed, 0.0)).astype(BF)
            k_aug[2 * p + 1, here, :] = jnp.where(first, jnp.where(lane == 0, closed, 0.0), k).astype(BF)
            q_t = q.T
            q_aug[2 * p, :, here] = jnp.where(sub < HEAD_DIM, q_t, jnp.where(sub == HEAD_DIM, 1.0, 0.0)).astype(BF)
            q_aug[2 * p + 1, :, here] = jnp.where(sub < HEAD_DIM, jnp.where(sub == 0, 1.0, 0.0), q_t).astype(BF)
            k_t[p, :, here] = k.T.astype(BF)
            v_t[p, :, here] = v.T.astype(BF)
            d_out[p, :, here] = g_all[:, cut].T

    @pl.when(step >= tiles)
    def attend():
        p = step - tiles
        lane = lax.broadcasted_iota(jnp.int32, (tile, 128), 1)
        later = lax.broadcasted_iota(jnp.int32, (tile, tile), 0) > lax.broadcasted_iota(jnp.int32, (tile, tile), 1)
        heads = range(2)
        mine = [lane < HEAD_DIM, lane >= HEAD_DIM]
        cuts = [slice(0, HEAD_DIM), slice(HEAD_DIM, 2 * HEAD_DIM)]

        def cut_of(j):
            return pl.ds(pl.multiple_of(j * share + p * 128, 128), 128)

        def score(i):
            n = (i + 1) * tile
            return [mm(k_aug[2 * p + h, :n, :], q_aug[2 * p + h, :, i * tile : n]) for h in heads]

        for i in range(tiles):
            n = (i + 1) * tile
            here = slice(i * tile, n)
            old = slice(0, i * tile)
            scores = ahead if i else score(0)
            weights, inverses = [], []
            for h in heads:
                s = scores[h]
                tail = jnp.where(later, -1e30, s[n - tile :])
                s = tail if i == 0 else jnp.concatenate([s[: n - tile], tail], axis=0)
                e = jnp.exp(s - jnp.max(s, axis=0, keepdims=True))
                inverses.append(1.0 / jnp.sum(e, axis=0, keepdims=True))
                weights.append(e)
            lows = [e.astype(BF) for e in weights]
            outs = [mm(v_t[p, cuts[h], :n], lows[h]) * inverses[h] for h in heads]
            scaled, inner = [], []
            for h in heads:
                d = d_out[p, cuts[h], here]
                inner.append(jnp.sum(d * outs[h], axis=0, keepdims=True) * inverses[h])
                scaled.append(d * inverses[h])
            g_scores = []
            for h in heads:
                zero = jnp.zeros((HEAD_DIM, tile), BF)
                d_t = scaled[h].astype(BF)
                d_t = jnp.concatenate([d_t, zero] if h == 0 else [zero, d_t], axis=0)
                g_scores.append((weights[h] * (mm(v_nat[p, :n, :], d_t) - inner[h])).astype(BF))
            if i + 1 < tiles:
                ahead = score(i + 1)
            attended[here, cut_of(0)] = jnp.concatenate(outs, axis=0).T.astype(BF)
            d_nat = jnp.concatenate(scaled, axis=0).T
            q_here = q_nat[p, here, :]
            g_q = jnp.concatenate([mm(k_t[p, cuts[h], :n], g_scores[h]) for h in heads], axis=0).T * HEAD_DIM ** (-0.5)
            g_qkv[here, cut_of(0)] = turn(g_q, cos_all[here, :], -sin_all[here, :]).astype(BF)
            add_v = sum(mm(lows[h], jnp.where(mine[h], d_nat, 0.0).astype(BF)) for h in heads)
            add_k = sum(mm(g_scores[h], jnp.where(mine[h], q_here, jnp.zeros_like(q_here))) for h in heads)
            if i > 0:
                gv_acc[old] += add_v[: n - tile]
                gk_acc[old] += add_k[: n - tile]
            gv_acc[here] = add_v[n - tile :]
            gk_acc[here] = add_k[n - tile :]
        g_qkv[:, cut_of(1)] = turn(gk_acc[...], cos_all[...], -sin_all[...]).astype(BF)
        g_qkv[:, cut_of(2)] = gv_acc[...].astype(BF)


def attend(place, left, weights):
    _, rows, width = left.shape
    share = width // 4
    pairs = share // 128
    tile = min(256, rows)
    tiles = rows // tile

    def early(i, _):
        return (jnp.minimum(i, tiles - 1), 0)

    def whole(shape):
        return pl.BlockSpec(shape, lambda i, _: (0, 0), pipeline_mode=pl.Buffered(1))

    w_q, w_k, w_v, w_o, _, _, cosine, sine = [inside(value) for value in weights]
    return pl.pallas_call(
        functools.partial(attend_kernel, tiles=tiles, tile=tile, pairs=pairs),
        grid_spec=pltpu.PrefetchScalarGridSpec(
            num_scalar_prefetch=1,
            grid=(tiles + pairs,),
            in_specs=[
                pl.BlockSpec((2, tile, width), lambda i, _: (0, jnp.minimum(i, tiles - 1), 0)),
                whole(w_q.shape), whole(w_k.shape), whole(w_v.shape), whole(w_o.shape),
                pl.BlockSpec((tile, 128), early),
                pl.BlockSpec((tile, 128), early),
                whole((rows, 128)), whole((rows, 128)),
            ],
            out_specs=[whole((rows, share)), whole((rows, 3 * share))],
            scratch_shapes=[
                pltpu.VMEM((2 * pairs, rows, 128), BF),
                pltpu.VMEM((pairs, 128, rows), BF),
                pltpu.VMEM((pairs, rows, 128), BF),
                pltpu.VMEM((pairs, 128, rows), BF),
                pltpu.VMEM((pairs, rows, 128), BF),
                pltpu.VMEM((2 * pairs, 128, rows), BF),
                pltpu.VMEM((pairs, 128, rows), F32),
                pltpu.VMEM((rows, 128), F32),
                pltpu.VMEM((rows, 128), F32),
            ],
        ),
        out_shape=[pltpu.VMEM((rows, share), BF), pltpu.VMEM((rows, 3 * share), BF)],
        compiler_params=pltpu.CompilerParams(vmem_limit_bytes=VMEM_BYTES),
        cost_estimate=cost(0.014 * rows),
        name="attend",
    )(place, inside(left), w_q, w_k, w_v, w_o, cosine, sine, cosine, sine)


def weight_mlp_kernel(place, scale, left_0, left_1, right_0, right_1, keep, send):
    total = (scale[0] * (mm(left_0[0], right_0[0], TN) + mm(left_1[0], right_1[0], TN))).astype(BF)
    half = total.shape[0] // 2
    odd = place[2] == 1
    keep[0] = jnp.where(odd, total[half:], total[:half])
    send[0] = jnp.where(odd, total[:half], total[half:])


def weight_att_kernel(place, scale, left_0, left_1, qkv_0, qkv_1, att_0, att_1, keep, send):
    odd = place[2] == 1
    size = qkv_0.shape[1]
    first = (scale[0] * (mm(left_0[0], qkv_0[...], TN) + mm(left_1[0], qkv_1[...], TN))).astype(BF)
    second = (scale[0] * (mm(left_0[1], att_0[...], TN) + mm(left_1[1], att_1[...], TN))).astype(BF)
    half = first.shape[0] // 2
    keep[0, :, :size] = jnp.where(odd, first[half:], first[:half])
    send[0, :, :size] = jnp.where(odd, first[:half], first[half:])
    keep[0, :, size:] = jnp.where(odd, second[half:], second[:half])
    send[0, :, size:] = jnp.where(odd, second[:half], second[half:])


def weight_hold_kernel(place, scale, left_0, left_1, right_0, right_1, hold, ship):
    total = (scale[0] * (mm(left_0[0], right_0[0], TN) + mm(left_1[0], right_1[0], TN))).astype(BF)
    half = total.shape[0] // 2
    odd = place[2] == 1
    mine = jnp.where(odd, total[half:], total[:half])
    other = jnp.where(odd, total[:half], total[half:])

    @pl.when(pl.program_id(0) < 2)
    def near():
        hold[0, 0] = mine
        hold[0, 1] = other

    @pl.when(pl.program_id(0) >= 2)
    def far():
        ship[0, 0] = mine
        ship[0, 1] = other


def chip_of(slot, place):
    return (2 * (slot & 1) + (slot >> 1)) ^ place[3]


def weight_mlp(place, scale, lefts, rights, kind):
    _, rows, width = lefts[0].shape
    units = rights[0].shape[2]
    size = width // 8
    column = pl.BlockSpec((1, rows, 2 * size), lambda i, where: (kind, 0, chip_of(i, where)))
    whole = pl.BlockSpec((1, rows, units), lambda i, where: (kind, 0, 0), pipeline_mode=pl.Buffered(1))
    if kind == 0:
        kernel = weight_mlp_kernel
        slot = pl.BlockSpec((1, size, units), lambda i, where: (i, 0, 0))
        outs = [slot, slot]
        out = [pltpu.HBM((4, size, units), BF)] * 2
    else:
        kernel = weight_hold_kernel
        outs = [pl.BlockSpec((1, 2, size, units), lambda i, where: (jnp.minimum(i, 1), 0, 0, 0)),
                pl.BlockSpec((1, 2, size, units), lambda i, where: (jnp.maximum(i - 2, 0), 0, 0, 0))]
        out = [pltpu.HBM((2, 2, size, units), BF)] * 2
    return pl.pallas_call(
        kernel,
        grid_spec=pltpu.PrefetchScalarGridSpec(
            num_scalar_prefetch=1, grid=(4,),
            in_specs=[pl.BlockSpec(memory_space=pltpu.SMEM), column, column, whole, whole], out_specs=outs,
        ),
        out_shape=out,
        compiler_params=pltpu.CompilerParams(vmem_limit_bytes=VMEM_BYTES),
        cost_estimate=cost(0.0065 * rows),
        name="weight_mlp",
    )(place, scale, *[inside(value) for value in (*lefts, *rights)])


def weight_att(place, scale, lefts, qkvs, atts):
    _, rows, width = lefts[0].shape
    units = qkvs[0].shape[1] + atts[0].shape[1]
    size = width // 8
    column = pl.BlockSpec((2, rows, 2 * size), lambda i, where: (0, 0, chip_of(i, where)))

    def whole(ref):
        return pl.BlockSpec(ref.shape, lambda i, where: (0, 0), pipeline_mode=pl.Buffered(1))

    slot = pl.BlockSpec((1, size, units), lambda i, where: (i, 0, 0))
    out = pltpu.HBM((4, size, units), BF)
    return pl.pallas_call(
        weight_att_kernel,
        grid_spec=pltpu.PrefetchScalarGridSpec(
            num_scalar_prefetch=1, grid=(4,),
            in_specs=[pl.BlockSpec(memory_space=pltpu.SMEM), column, column] + [whole(r) for r in (*qkvs, *atts)],
            out_specs=[slot, slot],
        ),
        out_shape=[out, out],
        compiler_params=pltpu.CompilerParams(vmem_limit_bytes=VMEM_BYTES),
        cost_estimate=cost(0.007 * rows),
        name="weight_att",
    )(place, scale, *[inside(value) for value in (*lefts, *qkvs, *atts)])


def branch_kernel(place, left, right, att, g_qkv, w_q, w_k, w_v, w_o, w_in, w_down, gain, bias,
                  keep, near, far_b, far_g, sums, column_sums):
    own = place[0]
    rows, share = att.shape
    total = mm(right[1], w_down[...]) + mm(att[...], w_o[...])
    g_total = mm(right[0], w_in[...], NT)
    for j, w in enumerate((w_q, w_k, w_v)):
        g_total += mm(g_qkv[:, j * share : (j + 1) * share], w[...], NT)
    odd = (own & 1) == 1
    up = (own >> 1) == 1
    for kind, (whole, far) in enumerate(((total, far_b), (g_total, far_g))):
        cuts = [whole[:, j * share : (j + 1) * share].astype(BF) for j in range(4)]
        low = [jnp.where(odd, cuts[2 * y + 1], cuts[2 * y]) for y in range(2)]
        high = [jnp.where(odd, cuts[2 * y], cuts[2 * y + 1]) for y in range(2)]
        keep[0, kind] = jnp.where(up, low[1], low[0])
        keep[1, kind] = jnp.where(up, low[0], low[1])
        near[kind] = jnp.where(up, high[1], high[0])
        far[...] = jnp.where(up, high[0], high[1])
    turned = g_total * (left[0].astype(F32) - bias[...])
    mean_part = jnp.sum(g_total * gain[...], axis=1, keepdims=True)
    inner_part = jnp.sum(turned, axis=1, keepdims=True)
    lane = lax.broadcasted_iota(jnp.int32, (rows, 128), 1)
    sums[...] = jnp.where(lane == 0, mean_part, inner_part).T[:8, :]

    @pl.when(pl.program_id(0) == 0)
    def clear():
        column_sums[...] = jnp.zeros_like(column_sums)

    column_sums[0:1, :] += jnp.sum(g_total, axis=0, keepdims=True)
    column_sums[1:2, :] += jnp.sum(turned, axis=0, keepdims=True)


def branch_parts(place, left, right, att, g_qkv, weights, gain, bias, first_row, rows):
    _, _, width = left.shape
    units = right.shape[2]
    share = att.shape[1]
    tile = min(256, rows)
    tiles = rows // tile
    offset = first_row // tile

    def paired(k, size):
        return pl.BlockSpec((k, tile, size), lambda i, _: (0, i + offset, 0))

    def rowed(size):
        return pl.BlockSpec((tile, size), lambda i, _: (i + offset, 0))

    def whole(shape):
        return pl.BlockSpec(shape, lambda i, _: (0, 0), pipeline_mode=pl.Buffered(1))

    weights = [inside(value) for value in weights[:6]]
    shape = jax.ShapeDtypeStruct
    slots = pl.BlockSpec((2, 2, tile, share), lambda i, _: (0, 0, i, 0))
    sent = pl.BlockSpec((2, tile, share), lambda i, _: (0, i, 0))
    rowed_out = pl.BlockSpec((tile, share), lambda i, _: (i, 0))
    return pl.pallas_call(
        branch_kernel,
        grid_spec=pltpu.PrefetchScalarGridSpec(
            num_scalar_prefetch=1,
            grid=(tiles,),
            in_specs=[
                paired(1, width), paired(2, units), rowed(share), rowed(3 * share),
                *[whole(value.shape) for value in weights],
                whole((1, width)), whole((1, width)),
            ],
            out_specs=[slots, sent, rowed_out, rowed_out, pl.BlockSpec((8, tile), lambda i, _: (0, i)), pl.BlockSpec((8, width), lambda i, _: (0, 0))],
        ),
        out_shape=[pltpu.HBM((2, 2, rows, share), BF)] + [pltpu.HBM((2, rows, share), BF)] + [pltpu.HBM((rows, share), BF)] * 2 + [shape((8, rows), F32),
                   shape((8, width), F32)],
        compiler_params=pltpu.CompilerParams(vmem_limit_bytes=VMEM_BYTES),
        cost_estimate=cost(0.010 * rows),
        name="branch_parts",
    )(place, inside(left), inside(right), inside(att), inside(g_qkv), *weights, gain, bias)


def combine_kernel(count, keep_in, x_in, hold, z_down, kept, core_b, core_g, z_in, low_in, zz_down, low_down, chip):
    size, units = keep_in.shape[1:]
    for k in range(2):
        z_in[k * size : (k + 1) * size] = keep_in[2 + k] + x_in[2 + k]
        low_in[k] = keep_in[k] + x_in[k]
        zz_down[k] = hold[1, k] + z_down[1, k]
        low_down[k] = hold[0, k] + z_down[0, k]
    rows = z_in.shape[0] - 2 * size
    row = lax.broadcasted_iota(jnp.int32, (rows, units), 0)
    value = jnp.full((rows, units), count[0], F32)
    high = value.astype(BF).astype(F32)
    z_in[2 * size :] = jnp.where(row == 0, high, jnp.where(row == 1, value - high, 0.0)).astype(BF)
    chip[0] = kept[1, 0] + core_b[...]
    chip[1] = kept[1, 1] + core_g[...]


def combine(count, keep_in, x_in, hold, z_down, kept, core):
    _, size, units = keep_in.shape
    _, _, rows, cols = kept.shape
    inner = pl.BlockSpec(memory_space=pltpu.VMEM)
    shapes = [(2 * size + 16, units), (2, size, units), (2, size, units), (2, size, units), (2, rows, cols)]
    return pl.pallas_call(
        combine_kernel,
        in_specs=[pl.BlockSpec(memory_space=pltpu.SMEM)] + [inner] * 7,
        out_specs=[inner] * 5,
        out_shape=[pltpu.HBM(shape, BF) for shape in shapes],
        compiler_params=pltpu.CompilerParams(vmem_limit_bytes=VMEM_BYTES),
        cost_estimate=cost(3),
        name="combine",
    )(count, *[outside(value) for value in (keep_in, x_in, hold, z_down, kept, *core)])


def relay_kernel(count, low, z_in, zz_in, kept, total):
    size, units = kept.shape
    kept[...] = low[0] + z_in[:size]
    zz_in[:size] = low[1] + z_in[size : 2 * size]
    tail = z_in[2 * size :].astype(F32)
    value = count[0] + tail[0:1] + tail[1:2]
    high = value.astype(BF).astype(F32)
    row = lax.broadcasted_iota(jnp.int32, tail.shape, 0)
    zz_in[size:] = jnp.where(row == 0, high, jnp.where(row == 1, value - high, 0.0)).astype(BF)
    total[...] = jnp.broadcast_to(value[:, :128], total.shape)


def relay(count, low, z_in):
    _, size, units = low.shape
    inner = pl.BlockSpec(memory_space=pltpu.VMEM)
    shape = jax.ShapeDtypeStruct
    return pl.pallas_call(
        relay_kernel,
        in_specs=[pl.BlockSpec(memory_space=pltpu.SMEM), inner, inner],
        out_specs=[inner] * 3,
        out_shape=[shape((size + 16, units), BF), shape((size, units), BF), shape((8, 128), F32)],
        compiler_params=pltpu.CompilerParams(vmem_limit_bytes=VMEM_BYTES),
        cost_estimate=cost(1),
        name="relay",
    )(count, low, z_in)


def final_kernel(place, scale, keep, near, far, x_ref, cot, stats, sums, gain, bias_down, *refs, first_row):
    mixed, g_x = refs[-2:]
    step = pl.program_id(0)
    rows, cols = x_ref.shape
    width = 4 * cols
    x = x_ref[...].astype(F32)
    branch = keep[0, 0].astype(F32) + near[0].astype(F32) + far[0].astype(F32)
    mixed[...] = (x + (branch + bias_down[...])).astype(BF)
    g = scale[0] * (keep[0, 1].astype(F32) + near[1].astype(F32) + far[1].astype(F32))
    inv_std = stats[:, 1:2]
    x_hat = (x - stats[:, 0:1]) * inv_std
    totals = (scale[0] / width) * jnp.concatenate([sums[...], jnp.zeros((126, rows), F32)], axis=0).T
    row = first_row + step * rows + lax.broadcasted_iota(jnp.int32, (rows, 1), 0)
    weight = jnp.where(row < place[1], scale[0], 0.0)
    g_out = weight * cot[...].astype(F32)
    g_x[...] = g_out + inv_std * (g * gain[...] - totals[:, 0:1] - x_hat * totals[:, 1:2])


def finish_rows(place, scale, keep, near, far, x, cot, stats, sums, gain, bias_down, sequence, first_row, before=None):
    _, rows, cols = far.shape
    tile = min(512, rows)
    tiles = rows // tile
    pad_len = stats.shape[0]
    begin = (sequence * pad_len + first_row) // tile
    inner = first_row // tile
    part = pl.BlockSpec((tile, cols), lambda i: (i + begin, 0))
    cored = pl.BlockSpec((1, tile, cols), lambda i: (0, i, 0))
    kept = pl.BlockSpec((1, 2, tile, cols), lambda i: (0, 0, i, 0))
    both = pl.BlockSpec((2, tile, cols), lambda i: (0, i, 0))
    flat = pl.BlockSpec((1, cols), lambda i: (0, 0))
    scalar = pl.BlockSpec(memory_space=pltpu.SMEM)
    shape = jax.ShapeDtypeStruct
    before = [] if before is None else list(before)
    return pl.pallas_call(
        functools.partial(final_kernel, first_row=first_row),
        grid=(tiles,),
        in_specs=[scalar, scalar, kept, both, both, part, part,
                  pl.BlockSpec((tile, 128), lambda i: (i + inner, 0)), pl.BlockSpec((2, tile), lambda i: (0, i + begin)), flat, flat]
        + [pl.BlockSpec(memory_space=pl.ANY)] * len(before),
        out_specs=[part, part],
        out_shape=[shape(x.shape, BF), shape(x.shape, F32)],
        input_output_aliases={11 + k: k for k in range(len(before))},
        compiler_params=pltpu.CompilerParams(vmem_limit_bytes=VMEM_BYTES),
        cost_estimate=cost(0.003 * rows),
        name="finish_rows",
    )(place, scale, *[outside(value) for value in (keep, near, far, x, cot, stats)], sums, gain, bias_down, *before)


def final_weight_kernel(factor, low_in, far_in, low_down, far_down, low_a, far_a, g_in, g_down, g_qkv, g_out):
    scale = factor[0]
    _, size, cols = g_qkv.shape
    g_in[...] = scale * (low_in[...].astype(F32) + far_in[:size].astype(F32))
    g_down[...] = (scale * (low_down[...].astype(F32) + far_down[...].astype(F32))).T
    for j in range(3):
        cut = slice(j * cols, (j + 1) * cols)
        g_qkv[j] = scale * (low_a[:, cut].astype(F32) + far_a[:size, cut].astype(F32))
    cut = slice(3 * cols, 4 * cols)
    g_out[...] = (scale * (low_a[:, cut].astype(F32) + far_a[:size, cut].astype(F32))).T


def finish_weights(factor, low_in, far_in, low_down, far_down, low_a, far_a):
    size, units = low_in.shape
    cols = low_a.shape[1] // 4
    shape = jax.ShapeDtypeStruct
    return pl.pallas_call(
        final_weight_kernel,
        in_specs=[pl.BlockSpec(memory_space=pltpu.SMEM)] + [pl.BlockSpec(memory_space=pltpu.VMEM)] * 6,
        out_specs=[pl.BlockSpec(memory_space=pltpu.VMEM)] * 4,
        out_shape=[shape((size, units), F32), shape((units, size), F32), shape((3, size, cols), F32), shape((cols, size), F32)],
        compiler_params=pltpu.CompilerParams(vmem_limit_bytes=VMEM_BYTES),
        cost_estimate=cost(3),
        name="finish_weights",
    )(factor, low_in, far_in, low_down, far_down, low_a, far_a)


def swap(value, axis, bit):
    size = lax.axis_size(axis)
    return lax.ppermute(value, axis, [(i, i ^ bit) for i in range(size)])


def sum_small(value, axis):
    bit = 1
    while bit < lax.axis_size(axis):
        value = value + swap(value, axis, bit)
        bit *= 2
    return value


def add_core(kept, core):
    return kept[1] + jnp.stack(core)


def unpack(rows, count):
    part = -(-count // rows.shape[1])
    high, low = rows[:part].astype(F32), rows[part : 2 * part].astype(F32)
    return (high + low).reshape(-1)[:count]


def after(value, *others):
    return lax.optimization_barrier((value, *others))[0]


def on_device_fast(inputs, cotangent, lengths, ln_gain, ln_bias, w_qkv, w_out, w_in, b_in, w_down, b_down):
    groups = lax.axis_size("wide")
    column = lax.axis_index("narrow")
    place_wide = lax.axis_index("wide")
    rows_all, cols = inputs.shape
    pad_len = rows_all // 2
    width = w_qkv.shape[0]
    units = w_in.shape[1]
    place = jnp.stack([column, lengths[0], place_wide & 1, place_wide >> 1]).astype(jnp.int32)
    gain = ln_gain.reshape(1, width)
    bias = ln_bias.reshape(1, width)
    b_up = b_in.reshape(1, units)
    half = pad_len // 2
    cuts = ((0, half), (half, pad_len), (pad_len, rows_all))
    own_gain = lax.dynamic_slice_in_dim(ln_gain, column * cols, cols, 0).reshape(1, cols)
    b_row = b_down.reshape(1, cols)

    count = (2.0 * jnp.sum(lengths.astype(F32))).reshape(1)
    count_x = count + swap(count, "wide", 1)
    later = lax.optimization_barrier((inputs, cotangent, count_x))[:2]
    sources = [(inputs, cotangent)] + [later] * (len(cuts) - 1)
    across = [swap(jnp.concatenate([a[low:high], b[low:high]], axis=0), "narrow", 2) for (a, b), (low, high) in zip(sources, cuts)]
    near = (inputs, swap(inputs, "narrow", 1), cotangent, swap(cotangent, "narrow", 1))
    weights = load_weights(place, w_qkv, w_out, w_in, w_down, *turn_tables(pad_len))
    up_in, up_down = weights[4:6]

    def far(k, *earlier):
        rows = after(across[k], *earlier)
        return rows, swap(rows, "narrow", 1)

    def branch(place, mlp, att, first_row, rows):
        kept, near, far_b, far_g, sums, columns = branch_parts(
            place, mlp[0], mlp[1], *att, weights, gain, bias, first_row, rows)
        return kept, near, (far_b, far_g), sums, columns

    first = norm_mlp(place, near, far(0, weights[0], count_x), gain, bias, up_in, b_up, up_down, 0, 0, pad_len)
    place = after(place, first[3])
    mlp_0 = norm_mlp(place, near, far(1, first[3]), gain, bias, up_in, b_up, up_down, half, half, pad_len, first)
    place = after(place, mlp_0[3])
    att_0 = attend(place, mlp_0[0], weights)
    place = after(place, att_0[0])
    mlp_1 = norm_mlp(place, near, far(2, att_0[0]), gain, bias, up_in, b_up, up_down, pad_len, 0, pad_len)
    place = after(place, mlp_1[3])
    lefts = (mlp_0[0], mlp_1[0])
    rights = (mlp_0[1], mlp_1[1])
    keep_in, send_in = weight_mlp(place, count, lefts, rights, 0)
    place = after(place, keep_in)
    x_in = swap(send_in, "wide", 1)
    hold_down, ship_down = weight_mlp(place, count, lefts, rights, 1)
    place = after(place, hold_down)
    z_down = swap(ship_down, "wide", 2)
    kept_0, near_0, sent_0, sums_0, columns_0 = branch(place, mlp_0, att_0, 0, pad_len)
    core_0 = [swap(part, "narrow", 1) for part in sent_0]
    place = after(place, sums_0)
    att_1 = attend(place, mlp_1[0], weights)
    size = keep_in.shape[1]
    x_in, z_down, count_x, *core_0 = lax.optimization_barrier((x_in, z_down, count_x, *core_0, att_1[0]))[:5]
    z_in, low_in, zz_down, low_down, chip_0 = combine(count_x, keep_in, x_in, hold_down, z_down, kept_0, core_0)
    z_in = swap(z_in, "wide", 2)
    zz_down = swap(zz_down, "wide", 4)
    y_0 = swap(chip_0, "narrow", 2)
    near_0 = swap(after(near_0, chip_0), "narrow", 1)
    place = after(place, low_in, low_down, chip_0, att_1[0])
    keep_a, send_a = weight_att(place, count, lefts, (att_0[1], att_1[1]), (att_0[0], att_1[0]))
    x_a = swap(send_a, "wide", 1)
    place = after(place, keep_a, near_0)
    kept_1, near_1, sent_1, sums_1, columns_1 = branch(place, mlp_1, att_1, 0, pad_len)
    core_1 = [swap(part, "narrow", 1) for part in sent_1]
    z_in, zz_down, y_0, sums_0, columns_0 = lax.optimization_barrier((z_in, zz_down, y_0, sums_0, columns_0, sums_1))[:5]
    zz_in, low_in, count_row = relay(count_x, low_in, z_in)
    zz_in = swap(zz_in, "wide", 4)
    x_d = swap(low_down[1] + zz_down[1], "wide", 1)
    low_down = low_down[0] + zz_down[0]
    sums = jnp.concatenate([sums_0[:2], sums_1[:2], columns_0[:2] + columns_1[:2]], axis=1)
    sums = after(sums, y_0)
    sums = sums + swap(sums, "narrow", 1)
    core_1 = [after(part, sums, low_down, low_in) for part in core_1]
    chip_1 = add_core(kept_1, core_1)
    y_1 = swap(chip_1, "narrow", 2)
    far_sums = swap(after(sums[:, :rows_all], chip_1), "narrow", 2)
    x_a = after(x_a, chip_1)
    z_a = swap(keep_a[2:] + x_a[2:], "wide", 2)
    low_a = keep_a[:2] + x_a[:2]
    sum_up, sum_down, columns = lax.optimization_barrier((mlp_0[3], mlp_0[4], sums[:, rows_all:], low_a))[:3]
    small = jnp.concatenate([columns.reshape(-1), jnp.sum(sum_up + mlp_1[3], axis=0), jnp.sum(sum_down + mlp_1[4], axis=0)])
    small = count * small
    small = small + swap(small, "wide", 1)
    z_small = swap(small, "wide", 2)
    zz_in = after(zz_in, small)
    count_row = count_row[0] + unpack(zz_in[size:], units)[:128]
    per_count = groups / count_row[:1]
    scale = count * per_count
    y_1, far_sums, x_d = lax.optimization_barrier((y_1, far_sums, x_d, scale))[:3]
    sums = sums[:, :rows_all] + far_sums
    small = small + after(z_small, sums)
    z_a = after(z_a, small)
    zz_a = swap(low_a[1] + z_a[1], "wide", 4)
    low_a = low_a[0] + z_a[0]
    zz_small = swap(small, "wide", 4)
    near_1 = swap(after(near_1, low_a), "narrow", 1)
    ends = finish_rows(after(place, small), scale, kept_0, near_0, y_0, inputs, cotangent, mlp_0[2], sums, own_gain, b_row, 0, 0)
    ends = finish_rows(place, scale, kept_1, near_1, y_1, inputs, cotangent, mlp_1[2], sums, own_gain, b_row, 1, 0, ends)
    small = per_count * (small + after(zz_small, ends[0]))
    columns = small[: 2 * width].reshape(2, width)
    far_columns = swap(columns, "narrow", 2)
    zz_a, far_columns = lax.optimization_barrier((zz_a, far_columns, ends[0]))[:2]
    columns = lax.dynamic_slice_in_dim(columns + far_columns, column * cols, cols, 1)
    g_in, g_down, g_qkv, g_out = finish_weights(per_count, low_in, zz_in, low_down, x_d, low_a, zz_a)
    return (
        ends[0],
        ends[1],
        columns[1] / own_gain[0],
        columns[0],
        jnp.transpose(g_qkv, (1, 0, 2)),
        g_out,
        g_in,
        small[2 * width : 2 * width + units],
        g_down,
        small[2 * width + units :],
    )


def turn_tables(length):
    position = np.arange(length, dtype=np.float32)[:, None]
    frequency = (10000.0 ** (-2.0 * np.arange(ROT // 2, dtype=np.float32) / ROT)).astype(np.float32)
    angles = (position * frequency[None, :]).astype(np.float32)
    cosine = np.ones((length, HEAD_DIM), np.float32)
    sine = np.zeros((length, HEAD_DIM), np.float32)
    cosine[:, :ROT] = np.repeat(np.cos(angles), 2, axis=1)
    sine[:, 0:ROT:2] = -np.sin(angles)
    sine[:, 1:ROT:2] = np.sin(angles)
    return jnp.asarray(np.tile(cosine, (1, 2))), jnp.asarray(np.tile(sine, (1, 2)))


def solution(mesh):
    placed = (
        P("wide", "narrow"),
        P("wide", "narrow"),
        P("wide"),
        P(),
        P(),
        P(),
        P(),
        P(None, "narrow"),
        P("narrow"),
        P("narrow", None),
        P("narrow"),
    )
    paired = mesh.shape["narrow"] == 4 and mesh.shape["wide"] == 8
    return jax.shard_map(
        on_device_fast if paired else on_device,
        mesh=mesh,
        in_specs=placed,
        out_specs=(
            P("wide", "narrow"),
            P("wide", "narrow"),
            P("narrow"),
            P("narrow"),
            P("wide", None, "narrow"),
            P("narrow", "wide"),
            P("wide", "narrow"),
            P("narrow"),
            P("narrow", "wide"),
            P("narrow"),
        ),
        check_vma=False,
    )
```
